32 devices in a mesh: seq: 16 (over z, y, x), head: 2 (over core).
Axes of the slice: x: 2, y: 2, z: 4, core: 2. Of those that a mesh axis runs over, the one named last changes fastest.
Arguments:
- hidden: float32 [2, 4096, 768], P(None, 'seq'), may hold values from -6 to 6
- lengths: int32 [2, 8], replicated, may hold values from 1 to 3967, as said below
- prenorm: float32 [768], replicated, may hold values from 0.5 to 1.5
- gating: float32 [768, 1536], P(None, 'head'), may hold values from -0.21875 to 0.21875
- values: float32 [768, 1536], P(None, 'head'), may hold values from -0.21875 to 0.21875
- states: float32 [768, 4, 64], replicated, may hold values from -0.21875 to 0.21875
- stepper: float32 [768, 2, 24], P(None, None, 'head'), may hold values from -0.21875 to 0.21875
- offsets: float32 [2, 24], P(None, 'head'), may hold values from -2 to 1
- decays: float32 [2, 24], P(None, 'head'), may hold values from -9 to 0
- filters: float32 [7, 1536], P(None, 'head'), may hold values from -2 to 2
- shifts: float32 [1536], P('head'), may hold values from -0.5 to 0.5
- kernels: float32 [7, 4, 64], replicated, may hold values from -2 to 2
- biases: float32 [4, 64], replicated, may hold values from -0.5 to 0.5
- direct: float32 [24], P('head'), may hold values from 0.5 to 1.5
- postnorm: float32 [1536], P('head'), may hold values from 0.5 to 1.5
- output: float32 [1536, 768], P('head'), may hold values from -0.15625 to 0.15625
- cotangent: float32 [2, 4096, 768], P(None, 'seq'), may hold values from -6 to 6
Outputs:
- result: float32 [2, 4096, 768], P(None, 'seq')
- grad_hidden: float32 [2, 4096, 768], P(None, 'seq')
- grad_prenorm: float32 [768], replicated
- grad_gating: float32 [768, 1536], P(None, 'head')
- grad_values: float32 [768, 1536], P(None, 'head')
- grad_states: float32 [768, 4, 64], replicated
- grad_stepper: float32 [768, 2, 24], P(None, None, 'head')
- grad_offsets: float32 [2, 24], P(None, 'head')
- grad_decays: float32 [2, 24], P(None, 'head')
- grad_filters: float32 [7, 1536], P(None, 'head')
- grad_shifts: float32 [1536], P('head')
- grad_kernels: float32 [7, 4, 64], replicated
- grad_biases: float32 [4, 64], replicated
- grad_direct: float32 [24], P('head')
- grad_postnorm: float32 [1536], P('head')
- grad_output: float32 [1536, 768], P('head')
The draws below stay inside these ranges and needn't reach their ends.
Inputs may be any that keep to these rules, and one draw needn't show every extreme that they name: In each micro-batch the 8 lengths sum to 4096; exactly one of them, at a place drawn from the seed, is 3967; the others are at most 36 and sum to 129.
All inputs are finite; a program needn't handle non-finite values.
Results may differ from the reference program's by a relative error of at most 0.0003.
Values sent between devices are 32-bit elements; how exact they have to be, the bound alone decides.
No kernel may reach another device: no remote copies, remote signals or barrier semaphores. Data moves between devices by JAX's collectives and lax.ppermute only.
A program may use at most 640 MiB of HBM per device.

```python
import jax
import jax.numpy as jnp
from jax import lax

D = 768
HEADS = 24
HEAD_DIM = 64
STATE = 64
INNER = 1536
BLOCK = 128
CONV_REACH = 3
MICRO = 2
SEQS = 8
TOKENS_MB = 4096
SMALL = 36


def draw_lengths(key, part):
    key = jax.random.fold_in(key, 11)
    keys = jax.random.split(key, 3)
    pair_count = (SEQS - 1) // 2
    firsts = jax.random.randint(keys[0], (MICRO, pair_count), 1, SMALL + 1)
    firsts = jnp.where(jnp.arange(pair_count)[None, :] == 0, 1, firsts)
    middle = jnp.full((MICRO, (SEQS - 1) % 2), (SMALL + 1) // 2, dtype=jnp.int32)
    shorts = jnp.concatenate([firsts, SMALL + 1 - firsts, middle], axis=1).astype(jnp.int32)
    row_keys = jax.random.split(keys[1], MICRO)
    shorts = jax.vmap(lambda row_key, row: jax.random.permutation(row_key, row))(row_keys, shorts)
    chosen = jax.random.randint(keys[2], (MICRO, 1), 0, SEQS)
    column = jnp.arange(SEQS)[None, :]
    source = jnp.clip(jnp.where(column < chosen, column, column - 1), 0, SEQS - 2)
    picked = jnp.take_along_axis(shorts, jnp.broadcast_to(source, (MICRO, SEQS)), axis=1)
    longest = TOKENS_MB - jnp.sum(shorts, axis=1, keepdims=True)
    return jnp.where(column == chosen, longest, picked).astype(jnp.int32)


def shard_levels(stream_key, extent, cuts, low, largest):
    def one(axis_at, parts):
        draws = jax.random.uniform(jax.random.fold_in(jax.random.fold_in(stream_key, 6), axis_at), (parts,), jnp.float32, low / len(cuts), largest / len(cuts))
        return jnp.repeat(jnp.exp(draws), extent[axis_at] // parts).reshape((-1,) + (1,) * (len(extent) - axis_at - 1))

    factor_of = one(*cuts[0])
    for cut in cuts[1:]:
        factor_of = factor_of * one(*cut)
    return factor_of


def normal_values(rng, dims, spread, limit, cuts=(), kind=jnp.bfloat16):
    values = jax.random.normal(rng, dims, jnp.float32) * spread
    if len(cuts) > 0:
        values = shard_levels(rng, dims, cuts, -0.22, 0.18) * values
    return jnp.clip(values, min=-limit, max=limit).astype(kind)


def setup_inputs(seed: int = 0) -> dict:
    streams_of = jax.random.split(jax.random.key(seed), 18)
    hidden = normal_values(streams_of[0], (MICRO, TOKENS_MB, D), 1.0, 6.0, ((1, 16),), jnp.float32)
    lengths = draw_lengths(jax.random.fold_in(streams_of[17], 71), 0)
    prenorm = jnp.clip(1.0 + 0.1 * jax.random.normal(streams_of[2], (D,), jnp.float32), 0.5, 1.5)
    gating = normal_values(streams_of[3], (D, INNER), D ** -0.5, 0.21875, ((1, 2),), jnp.float32)
    values = normal_values(streams_of[4], (D, INNER), D ** -0.5, 0.21875, ((1, 2),), jnp.float32)
    states = normal_values(streams_of[5], (D, 4, STATE), D ** -0.5, 0.21875, (), jnp.float32)
    stepper = normal_values(streams_of[6], (D, 2, HEADS), D ** -0.5, 0.21875, ((2, 2),), jnp.float32)
    offsets = jnp.clip(-2.0 + 3.0 * jax.random.uniform(streams_of[7], (2, HEADS), jnp.float32) ** shard_levels(streams_of[7], (2, HEADS), ((1, 2),), -0.2, 0.2), -2.0, 1.0)
    decays = jnp.clip(-9.0 + 9.0 * jax.random.uniform(streams_of[8], (2, HEADS), jnp.float32) ** shard_levels(streams_of[8], (2, HEADS), ((1, 2),), -0.2, 0.2), -9.0, 0.0)
    filters = normal_values(streams_of[9], (2 * CONV_REACH + 1, INNER), (2 * CONV_REACH + 1) ** -0.5, 2.0, ((1, 2),), jnp.float32)
    shifts = jnp.clip(jax.random.uniform(streams_of[10], (INNER,), jnp.float32, -0.5, 0.5) * shard_levels(streams_of[10], (INNER,), ((0, 2),), -0.4, 0.0), -0.5, 0.5)
    kernels = normal_values(streams_of[11], (2 * CONV_REACH + 1, 4, STATE), (2 * CONV_REACH + 1) ** -0.5, 2.0, (), jnp.float32)
    biases = jnp.clip(jax.random.uniform(streams_of[12], (4, STATE), jnp.float32, -0.5, 0.5), -0.5, 0.5)
    direct = jnp.clip(0.5 + 1.0 * jax.random.uniform(streams_of[13], (HEADS,), jnp.float32) ** shard_levels(streams_of[13], (HEADS,), ((0, 2),), -0.2, 0.2), 0.5, 1.5)
    postnorm = jnp.clip(1.0 + 0.1 * jax.random.normal(streams_of[14], (INNER,), jnp.float32), 0.5, 1.5)
    output = normal_values(streams_of[15], (INNER, D), INNER ** -0.5, 0.15625, ((0, 2),), jnp.float32)
    cotangent = normal_values(streams_of[16], (MICRO, TOKENS_MB, D), 1.0, 6.0, ((1, 16),), jnp.float32)
    return {"hidden": hidden, "lengths": lengths, "prenorm": prenorm, "gating": gating, "values": values, "states": states, "stepper": stepper, "offsets": offsets, "decays": decays, "filters": filters, "shifts": shifts, "kernels": kernels, "biases": biases, "direct": direct, "postnorm": postnorm, "output": output, "cotangent": cotangent}


@jax.custom_vjp
def low(v):
    return lax.optimization_barrier(v.astype(jnp.bfloat16)).astype(jnp.float32)

@jax.custom_vjp
def low_back(v):
    return v

def low_keep(v):
    return (low(v), None)

def low_pass(kept, grad):
    return (grad,)

def back_keep(v):
    return (v, None)

def back_low(kept, grad):
    return (low(grad),)
low.defvjp(low_keep, low_pass)
low_back.defvjp(back_keep, back_low)
EPSILON = 1e-05
HIGHEST = lax.Precision.HIGHEST

def matmul(left, right):
    return jnp.dot(left, right, precision=HIGHEST, preferred_element_type=jnp.float32)

def segment_of(lengths_row, stream_total):
    bounds = jnp.cumsum(lengths_row).astype(jnp.int32)
    places = jnp.arange(stream_total, dtype=jnp.int32)
    return lax.optimization_barrier(jnp.sum((places[:, None] >= bounds[None, :]).astype(jnp.int32), axis=1)).astype(jnp.int32)

def conv_mixed(signal_in, taps, bias_row, segment):
    length = signal_in.shape[0]
    padded = jnp.pad(signal_in, ((CONV_REACH, CONV_REACH), (0, 0)))
    seg_pad = jnp.pad(segment, (CONV_REACH, CONV_REACH), constant_values=-1)
    result = jnp.zeros_like(signal_in) + bias_row[None, :]
    for offset in range(2 * CONV_REACH + 1):
        same_doc = (seg_pad[offset:offset + length] == segment).astype(jnp.float32)
        result = result + taps[offset][None, :] * padded[offset:offset + length] * same_doc[:, None]
    return result

def block_math(carry_state, before, signal, step_sizes, inputs, readers, segment, decay_rates):
    log_decay = -step_sizes * decay_rates[None, :]
    running = jnp.cumsum(log_decay, axis=0)
    places = jnp.arange(signal.shape[0])
    within = (places[:, None] > places[None, :]) & (segment[:, None] == segment[None, :])
    gap_sizes = jnp.where(within[:, :, None], running[:, None, :] - running[None, :, :], 0.0)
    weights = jnp.where(within[:, :, None], jnp.exp(gap_sizes), 0.0)
    scores = jnp.einsum('tn,sn->ts', readers, inputs, precision=HIGHEST)
    scaled = signal * step_sizes[:, :, None]
    inside = jnp.einsum('ts,tsh,shp->thp', scores, weights, scaled, precision=HIGHEST)
    reach_factor = (segment == before).astype(jnp.float32)[:, None] * jnp.exp(running)
    carried = jnp.einsum('tn,hnp->thp', readers, carry_state, precision=HIGHEST) * reach_factor[:, :, None]
    tail_factor = (segment == segment[-1]).astype(jnp.float32)[:, None] * jnp.exp(running[-1][None, :] - running)
    keep_factor = (segment[-1] == before).astype(jnp.float32) * jnp.exp(running[-1])
    fresh_state = jnp.einsum('sn,sh,shp->hnp', inputs, tail_factor, scaled, precision=HIGHEST)
    return (inside + carried, reach_factor, keep_factor[:, None, None] * carry_state + fresh_state, keep_factor)

def scan_direction(signal, step_sizes, inputs, readers, decay_rates, segment):
    block_count = signal.shape[0] // BLOCK
    pieces = (signal.reshape(block_count, BLOCK, HEADS, HEAD_DIM), step_sizes.reshape(block_count, BLOCK, HEADS), inputs.reshape(block_count, BLOCK, STATE), readers.reshape(block_count, BLOCK, STATE), segment.reshape(block_count, BLOCK))

    def advance(carry_all, block_piece):
        carry_state, before = carry_all
        outputs, reach_factor, state_new, keep_factor = block_math(carry_state, before, *block_piece, decay_rates)
        return ((state_new, block_piece[4][-1]), outputs)
    initial = (jnp.zeros((HEADS, STATE, HEAD_DIM), jnp.float32), jnp.array(-1, dtype=jnp.int32))
    final_carry, outputs = lax.scan(jax.checkpoint(advance), initial, pieces)
    return outputs.reshape(-1, HEADS, HEAD_DIM)

def hydra_block(stream, params, segment):
    prenorm, gating, values, states, stepper, offsets, decays, filters, shifts, kernels, biases, direct, postnorm, output = params
    length = stream.shape[0]
    normed = stream * lax.rsqrt(lax.optimization_barrier(jnp.mean(stream * stream, axis=1, keepdims=True)) + EPSILON) * prenorm
    gate_raw = matmul(normed, gating)
    value_in = matmul(normed, values)
    state_in = matmul(normed, states.reshape(D, 4 * STATE))
    step_raw = matmul(normed, stepper.reshape(D, 2 * HEADS)).reshape(length, 2, HEADS)
    signal = jax.nn.silu(conv_mixed(value_in, filters, shifts, segment)).reshape(length, HEADS, HEAD_DIM)
    maps = jax.nn.silu(conv_mixed(state_in, kernels.reshape(2 * CONV_REACH + 1, 4 * STATE), biases.reshape(4 * STATE), segment)).reshape(length, 4, STATE)
    step_sizes = jax.nn.softplus(step_raw + offsets[None])
    rate_pair = jnp.exp(decays)
    ahead = scan_direction(signal, step_sizes[:, 0], maps[:, 0], maps[:, 1], rate_pair[0], segment)
    behind = scan_direction(signal[::-1], step_sizes[::-1, 1], maps[::-1, 2], maps[::-1, 3], rate_pair[1], segment[::-1])[::-1]
    combined = ahead + behind + direct[None, :, None] * signal
    gated = combined.reshape(length, INNER) * jax.nn.silu(gate_raw)
    normal_gated = gated * lax.rsqrt(lax.optimization_barrier(jnp.mean(gated * gated, axis=1, keepdims=True)) + EPSILON) * postnorm
    return stream + matmul(normal_gated, output)

def reference(hidden, lengths, prenorm, gating, values, states, stepper, offsets, decays, filters, shifts, kernels, biases, direct, postnorm, output, cotangent):
    params = (prenorm, gating, values, states, stepper, offsets, decays, filters, shifts, kernels, biases, direct, postnorm, output)

    def one_batch(totals, micro_slice):
        stream, upstream, sizes = micro_slice
        segment = segment_of(sizes, stream.shape[0])

        def forward(stream_now, *param_now):
            return hydra_block(stream_now, param_now, segment)
        result, pull_back = jax.vjp(forward, stream, *params)
        grads = pull_back(upstream)
        return (jax.tree.map(jnp.add, totals, tuple(grads[1:])), (result, grads[0]))
    zeros_all = tuple((jnp.zeros_like(param) for param in params))
    sums, (results, input_grads) = lax.scan(one_batch, zeros_all, (hidden, cotangent, lengths))
    return (results, input_grads, sums[0], sums[1], sums[2], sums[3], sums[4], sums[5], sums[6], sums[7], sums[8], sums[9], sums[10], sums[11], sums[12], sums[13])
```

```python
from functools import partial

import jax
import jax.numpy as jnp
from jax import lax
from jax.experimental import pallas as pl
from jax.experimental.pallas import tpu as pltpu
from jax.sharding import PartitionSpec as P

EPSILON = 1e-05
HIGH = lax.Precision.HIGH
F32 = jnp.float32
BF16 = jnp.bfloat16
LANES = 128
EDGE = 8
PARAMS = pltpu.CompilerParams(vmem_limit_bytes=56 * 1024 * 1024)


def dot(left, right, over_left=1, over_right=0, precision=HIGH):
    return lax.dot_general(
        left,
        right,
        (((over_left,), (over_right,)), ((), ())),
        precision=precision,
        preferred_element_type=F32,
    )


def split(x):
    top = x.astype(BF16)
    return top, (x - top.astype(F32)).astype(BF16)


def dot_bf16(left, right, over_left=1, over_right=0):
    return lax.dot_general(
        left,
        right,
        (((over_left,), (over_right,)), ((), ())),
        preferred_element_type=F32,
    )


def spread(heads, first, head_size, both):
    rows = lax.broadcasted_iota(jnp.int32, (2 * both, LANES), 0)
    columns = lax.broadcasted_iota(jnp.int32, (2 * both, LANES), 1)
    return (lax.rem(rows, both) == first + columns // head_size).astype(BF16)


def gather_heads(first, head_size, both):
    rows = lax.broadcasted_iota(jnp.int32, (2 * LANES, both), 0)
    columns = lax.broadcasted_iota(jnp.int32, (2 * LANES, both), 1)
    return (columns == first + lax.rem(rows, LANES) // head_size).astype(BF16)


def halves(x):
    return jnp.concatenate(split(x), axis=1)


def triangle(size, keep):
    rows = lax.broadcasted_iota(jnp.int32, (size, size), 0)
    columns = lax.broadcasted_iota(jnp.int32, (size, size), 1)
    return keep(rows, columns)


def exact_sum(zero_one, x):
    a = x.astype(BF16)
    rest = x - a.astype(F32)
    b = rest.astype(BF16)
    c = (rest - b.astype(F32)).astype(BF16)
    return dot_bf16(zero_one, a) + dot_bf16(zero_one, b) + dot_bf16(zero_one, c)


def flip(x):
    size = x.shape[1]
    one = triangle(size, lambda r, c: r == c).astype(BF16)
    a = x.astype(BF16)
    rest = x - a.astype(F32)
    b = rest.astype(BF16)
    c = (rest - b.astype(F32)).astype(BF16)
    return dot_bf16(one, a, 1, 1) + dot_bf16(one, b, 1, 1) + dot_bf16(one, c, 1, 1)


def sigmoid(x):
    return 1.0 / (1.0 + jnp.exp(-x))


def softplus(x):
    return jnp.maximum(x, 0.0) + jnp.log1p(jnp.exp(-jnp.abs(x)))


def front_kernel(
    dims,
    mixed,
    raw,
    taps,
    bias,
    offsets,
    rates,
    emask,
    cols,
    keep_mask,
    conv,
    act,
    steps,
    run,
    reach,
    tail,
    run_rows,
    late_rows,
    keep,
    pay,
    masks,
):
    length, inner, heads, state, reach_cells, rows = dims
    head_size = inner // heads
    both = 2 * heads
    width = conv.shape[2]
    offsets_count = 2 * reach_cells + 1
    for o in range(offsets_count):
        masks[o] = jnp.broadcast_to(
            emask[0, EDGE : EDGE + length, o : o + 1], (length, LANES)
        )

    def column(j, _):
        at = pl.ds(pl.multiple_of(j * LANES, LANES), LANES)
        total = jnp.broadcast_to(bias[:, at], (length, LANES))
        for o in range(offsets_count):
            total = total + (
                mixed[0, EDGE - reach_cells + o : EDGE - reach_cells + o + length, at]
                * taps[o : o + 1, at]
            ) * masks[o]
        conv[0, :, at] = total
        act[0, :, at] = total * sigmoid(total)
        return 0

    lax.fori_loop(0, width // LANES, column, 0)

    ahead = lax.broadcasted_iota(jnp.int32, (length, both), 1) < heads
    ahead_row = ahead[:1]
    z = raw[0] + offsets[...]
    step = softplus(z)
    decay = -step * rates[...]
    lower = triangle(length, lambda r, c: r >= c).astype(BF16)
    upper = triangle(length, lambda r, c: r <= c).astype(BF16)
    running = jnp.where(ahead, exact_sum(lower, decay), exact_sum(upper, decay))
    edge = jnp.where(ahead_row, running[length - 1 :], running[:1])
    enter = jnp.where(ahead, cols[0, :, 0:1], cols[0, :, 1:2])
    leave = jnp.where(ahead, cols[0, :, 2:3], cols[0, :, 3:4])
    reach_now = enter * jnp.exp(running)
    tail_now = leave * jnp.exp(edge - running) * step
    keep_now = keep_mask[0] * jnp.exp(edge)
    steps[0] = z
    run[0] = running
    reach[0] = reach_now
    tail[0] = tail_now
    run_rows[0] = flip(running)
    late_rows[0] = flip(running - jnp.log(jnp.maximum(step, 1e-37)))
    keep[0] = keep_now

    tail_halves = halves(tail_now)
    keep_halves = halves(jnp.broadcast_to(keep_now, (EDGE, both)))
    pieces = state // rows
    tiles = inner // LANES
    per_tile = LANES // head_size
    for d in range(2):
        inputs = act[0, :, inner + 2 * d * state : inner + (2 * d + 1) * state]
        keeps = []
        for t in range(tiles):
            grow = spread(heads, d * heads + t * per_tile, head_size, both)
            weighted = act[0, :, t * LANES : (t + 1) * LANES] * dot_bf16(tail_halves, grow)
            own = dot(inputs, weighted, 0, 0)
            for j in range(pieces):
                pay[d * pieces + j, t * rows : (t + 1) * rows, :] = own[j * rows : (j + 1) * rows]
            keeps.append(dot_bf16(keep_halves, grow)[:1])
        keeps.append(jnp.zeros((EDGE - tiles, LANES), F32))
        keep_block = jnp.concatenate(keeps, axis=0)
        for j in range(pieces):
            pay[d * pieces + j, tiles * rows :, :] = keep_block


def prefix_kernel(tiles, rows, flipped, terms, keeps, into):
    peers = terms.shape[0]
    back = flipped[0] != 0

    def turn(i, carry):
        at = jnp.where(back, peers - 1 - i, i)
        factor = keeps[at, tiles * rows :, :]
        new = []
        for t in range(tiles):
            into[at, t * rows : (t + 1) * rows, :] = carry[t]
            new.append(
                carry[t] * factor[t : t + 1] + terms[at, t * rows : (t + 1) * rows, :]
            )
        return tuple(new)

    lax.fori_loop(0, peers, turn, tuple(jnp.zeros((rows, LANES), F32) for _ in range(tiles)))


def scores_of(act, seg_col, seg_row, inner, state, length):
    def part(i):
        return act[0, :, inner + i * state : inner + (i + 1) * state]

    same = seg_col[0] == seg_row[0]
    below = triangle(length, lambda r, c: r > c)
    above = triangle(length, lambda r, c: r < c)
    scores = jnp.where(below & same, dot(part(1), part(0), 1, 1), 0.0) + jnp.where(
        above & same, dot(part(3), part(2), 1, 1), 0.0
    )
    return scores, below, above, same


def weights_of(below, run, run_at, late_rows, heads, h):
    return jnp.exp(
        jnp.where(
            below,
            run_at[:, h : h + 1] - late_rows[0, h : h + 1, :],
            run_at[:, heads + h : heads + h + 1] - late_rows[0, heads + h : heads + h + 1, :],
        )
    )


def inside_kernel(dims, act, run, late_rows, seg_col, seg_row, inside):
    length, inner, heads, state, _, _ = dims
    head_size = inner // heads
    per_tile = LANES // head_size
    scores, below, _, _ = scores_of(act, seg_col, seg_row, inner, state, length)
    run_at = run[0]
    lane = lax.broadcasted_iota(jnp.int32, (length, LANES), 1) // head_size
    for t in range(inner // LANES):
        top, low = split(act[0, :, t * LANES : (t + 1) * LANES])
        pair = jnp.concatenate([top, low], axis=1)
        total = jnp.zeros((length, LANES), F32)
        for i in range(per_tile):
            weights = weights_of(below, run, run_at, late_rows, heads, t * per_tile + i)
            m_top, m_low = split(scores * weights)
            wide = dot_bf16(m_top, pair)
            now = wide[:, :LANES] + wide[:, LANES:] + dot_bf16(m_low, top)
            total = jnp.where(lane == i, now, total)
        inside[0, :, t * LANES : (t + 1) * LANES] = total


def unpack(pay, into, tiles, rows, state):
    pieces = state // rows
    for d in range(2):
        for j in range(pieces):
            for t in range(tiles):
                into[d, j * rows : (j + 1) * rows, t * LANES : (t + 1) * LANES] = pay[
                    d * pieces + j, t * rows : (t + 1) * rows, :
                ]


def join_kernel(
    dims, inside, pay, act, reach, gate, back, direct, postnorm, mixed_y, sums, states
):
    length, inner, heads, state, _, rows = dims
    head_size = inner // heads
    both = 2 * heads
    per_tile = LANES // head_size
    tiles = inner // LANES
    into = states.at[0]
    unpack(pay, into, tiles, rows, state)
    reach_halves = halves(reach[0])
    readers = [act[0, :, inner + i * state : inner + (i + 1) * state] for i in (1, 3)]
    squares = jnp.zeros((length, LANES), F32)
    crossed = jnp.zeros((length, LANES), F32)
    for t in range(tiles):
        at = slice(t * LANES, (t + 1) * LANES)
        total = inside[0, :, at] + direct[:, at] * act[0, :, at]
        for d in range(2):
            grow = spread(heads, d * heads + t * per_tile, head_size, both)
            total = total + dot(readers[d], states[0, d, :, at]) * dot_bf16(reach_halves, grow)
        mixed_y[0, :, at] = total
        gate_now = gate[0, :, at]
        gated = total * (gate_now * sigmoid(gate_now))
        squares = squares + gated * gated
        crossed = crossed + gated * postnorm[:, at] * back[0, :, at]
    lane = lax.broadcasted_iota(jnp.int32, (length, LANES), 1)
    sums[0] = jnp.where(
        lane == 0,
        jnp.sum(squares, axis=1, keepdims=True),
        jnp.sum(crossed, axis=1, keepdims=True),
    )


def turn_kernel(
    dims,
    inner_all,
    sums,
    peer_sums,
    mixed_y,
    gate,
    back,
    act,
    reach,
    direct,
    postnorm,
    grad_y,
    grad_gate,
    normal,
    pay,
    grad_post,
    grad_direct,
):
    length, inner, heads, state, _, rows = dims
    head_size = inner // heads
    both = 2 * heads
    per_tile = LANES // head_size
    tiles = inner // LANES
    pieces = state // rows
    both_sums = sums[0] + peer_sums[0]
    q = lax.rsqrt(both_sums[:, 0:1] / inner_all + EPSILON)
    pull = both_sums[:, 1:2] * (q * q * q) / inner_all
    q_wide = jnp.broadcast_to(q, (length, LANES))
    pull_wide = jnp.broadcast_to(pull, (length, LANES))
    reach_halves = halves(reach[0])
    readers = [act[0, :, inner + i * state : inner + (i + 1) * state] for i in (1, 3)]
    for t in range(tiles):
        at = slice(t * LANES, (t + 1) * LANES)
        y = mixed_y[0, :, at]
        gate_now = gate[0, :, at]
        chance = sigmoid(gate_now)
        opened = gate_now * chance
        gated = y * opened
        post = postnorm[:, at]
        scaled = q_wide * back[0, :, at]
        grad_gated = scaled * post - pull_wide * gated
        upstream = grad_gated * opened
        grad_y[0, :, at] = upstream
        grad_gate[0, :, at] = grad_gated * y * (chance * (1.0 + gate_now * (1.0 - chance)))
        normal[0, :, at] = gated * post * q_wide
        grad_post[0, :, at] = jnp.sum(scaled * gated, axis=0, keepdims=True)
        grad_direct[0, :, at] = jnp.sum(upstream * act[0, :, at], axis=0, keepdims=True)
        for d in range(2):
            grow = spread(heads, d * heads + t * per_tile, head_size, both)
            seed = dot(readers[d], upstream * dot_bf16(reach_halves, grow), 0, 0)
            for j in range(pieces):
                pay[d * pieces + j, t * rows : (t + 1) * rows, :] = seed[j * rows : (j + 1) * rows]


def inside_back_kernel(
    dims,
    act,
    grad_y,
    run,
    late_rows,
    seg_col,
    seg_row,
    grad_signal,
    grad_maps,
    differ,
    column_sums,
    row_parts,
    column_parts,
):
    length, inner, heads, state, _, _ = dims
    head_size = inner // heads
    per_tile = LANES // head_size
    scores, below, above, same = scores_of(act, seg_col, seg_row, inner, state, length)
    run_at = run[0]
    both = 2 * heads
    lane = lax.broadcasted_iota(jnp.int32, (length, LANES), 1)
    row_sums = jnp.zeros((length, LANES), F32)
    grad_scores = jnp.zeros((length, length), F32)
    for t in range(inner // LANES):
        at = slice(t * LANES, (t + 1) * LANES)
        s_top, s_low = split(act[0, :, at])
        g_now = grad_y[0, :, at]
        g_top, g_low = split(g_now)
        pair = jnp.concatenate([g_top, g_low], axis=1)
        total = jnp.zeros((length, LANES), F32)
        for i in range(per_tile):
            h = t * per_tile + i
            weights = weights_of(below, run, run_at, late_rows, heads, h)
            mine = lane // head_size == i
            zero = jnp.zeros((length, LANES), BF16)
            gi_top = jnp.where(mine, g_top, zero)
            gi_low = jnp.where(mine, g_low, zero)
            overlap = (
                dot_bf16(
                    jnp.concatenate([gi_top, gi_low], axis=1),
                    jnp.concatenate([s_top, s_top], axis=1),
                    1,
                    1,
                )
                + dot_bf16(gi_top, s_low, 1, 1)
            )
            product = weights * overlap
            grad_scores = grad_scores + product
            whole = product * scores
            ahead = jnp.where(below, whole, 0.0)
            ahead_rows = jnp.sum(ahead, axis=1, keepdims=True)
            all_rows = jnp.sum(whole, axis=1, keepdims=True)
            row_sums = jnp.where(lane == h, ahead_rows, row_sums)
            row_sums = jnp.where(lane == heads + h, all_rows - ahead_rows, row_sums)
            ahead_columns = jnp.sum(ahead, axis=0, keepdims=True)
            column_parts[h : h + 1, :] = ahead_columns
            column_parts[heads + h : heads + h + 1, :] = (
                jnp.sum(whole, axis=0, keepdims=True) - ahead_columns
            )
            m_top, m_low = split(scores * weights)
            wide = dot_bf16(m_top, pair, 0, 0)
            now = wide[:, :LANES] + wide[:, LANES:] + dot_bf16(m_low, g_top, 0, 0)
            total = jnp.where(lane // head_size == i, now, total)
        grad_signal[0, :, at] = total

    columns = flip_back(column_parts[...])
    column_sums[0] = columns
    differ[0] = row_sums[:, :both] - columns
    for d, side in enumerate((below, above)):
        grads = jnp.where(side & same, grad_scores, 0.0)
        start = inner + 2 * d * state
        grad_maps[0, :, 2 * d * state : (2 * d + 1) * state] = dot(
            grads, act[0, :, start + state : start + 2 * state], 0, 0
        )
        grad_maps[0, :, (2 * d + 1) * state : (2 * d + 2) * state] = dot(
            grads, act[0, :, start : start + state]
        )


def flip_back(x):
    size = x.shape[0]
    one = triangle(size, lambda r, c: r == c).astype(BF16)
    a = x.astype(BF16)
    rest = x - a.astype(F32)
    b = rest.astype(BF16)
    c = (rest - b.astype(F32)).astype(BF16)
    return dot_bf16(a, one, 0, 0) + dot_bf16(b, one, 0, 0) + dot_bf16(c, one, 0, 0)


def end_kernel(
    dims,
    pay,
    act,
    grad_y,
    reach,
    tail,
    z_in,
    conv,
    states,
    keep,
    grad_inside,
    grad_maps_inside,
    differ,
    column_sums,
    mixed,
    taps,
    emask,
    rates,
    direct,
    grad_mixed,
    grad_raw,
    grad_taps,
    grad_bias,
    grad_offsets,
    grad_decays,
    later,
    grad_maps,
    padded,
    masks,
):
    length, inner, heads, state, reach_cells, rows = dims
    head_size = inner // heads
    both = 2 * heads
    per_tile = LANES // head_size
    tiles = inner // LANES
    width = conv.shape[2]
    offsets_count = 2 * reach_cells + 1
    unpack(pay, later, tiles, rows, state)
    for o in range(offsets_count):
        masks[o] = jnp.broadcast_to(emask[0, :, o : o + 1], (length + 2 * EDGE, LANES))
    padded[:EDGE] = jnp.zeros((EDGE, LANES), F32)
    padded[EDGE + length :] = jnp.zeros((EDGE, LANES), F32)

    def turn_back(j, total):
        at = pl.ds(j * LANES, LANES)
        value = conv[0, :, at]
        chance = sigmoid(value)
        grad = total * (chance * (1.0 + value * (1.0 - chance)))
        padded[EDGE : EDGE + length] = grad
        grad_bias[0, :, at] = jnp.sum(grad, axis=0, keepdims=True)
        back = jnp.zeros((length + 2 * EDGE - 8, LANES), F32)
        first = EDGE - reach_cells
        wide = length + 2 * reach_cells
        back = jnp.zeros((wide, LANES), F32)
        for o in range(offsets_count):
            mirror = offsets_count - 1 - o
            begin = first - (o - reach_cells)
            lo = max(begin, 0)
            piece = padded[lo : lo + wide]
            back = back + (piece * taps[o : o + 1, at]) * masks[mirror, first : first + wide]
            grad_taps[0, o : o + 1, at] = jnp.sum(
                (grad * mixed[0, EDGE - reach_cells + o : EDGE - reach_cells + o + length, at])
                * masks[o, EDGE : EDGE + length],
                axis=0,
                keepdims=True,
            )
        grad_mixed[0, :first, at] = jnp.zeros((first, LANES), F32)
        grad_mixed[0, first + wide :, at] = jnp.zeros((first, LANES), F32)
        grad_mixed[0, first : first + wide, at] = back

    reach_halves = halves(reach[0])
    tail_halves = halves(tail[0])
    enter = jnp.zeros((length, both), F32)
    leave = jnp.zeros((length, both), F32)
    through = jnp.zeros((1, both), F32)
    readers = [act[0, :, inner + (2 * d + 1) * state : inner + (2 * d + 2) * state] for d in (0, 1)]
    inputs = [act[0, :, inner + 2 * d * state : inner + (2 * d + 1) * state] for d in (0, 1)]
    grad_readers = [
        grad_maps_inside[0, :, (2 * d + 1) * state : (2 * d + 2) * state] for d in (0, 1)
    ]
    grad_inputs = [grad_maps_inside[0, :, 2 * d * state : (2 * d + 1) * state] for d in (0, 1)]
    for t in range(tiles):
        at = slice(t * LANES, (t + 1) * LANES)
        signal = act[0, :, at]
        upstream = grad_y[0, :, at]
        total = grad_inside[0, :, at] + direct[:, at] * upstream
        for d in range(2):
            first = d * heads + t * per_tile
            grow = spread(heads, first, head_size, both)
            fold = gather_heads(first, head_size, both)
            before = states[0, d, :, at]
            after = later[d, :, at]
            reached = upstream * dot_bf16(reach_halves, grow)
            tails = dot_bf16(tail_halves, grow)
            weighted = signal * tails
            enter = enter + dot_bf16(halves(reached * dot(readers[d], before)), fold)
            pulled = dot(inputs[d], after)
            total = total + tails * pulled
            leave = leave + dot_bf16(halves(weighted * pulled), fold)
            grad_readers[d] = grad_readers[d] + dot(reached, before, 1, 1)
            grad_inputs[d] = grad_inputs[d] + dot(weighted, after, 1, 1)
            crossed = jnp.sum(before * after, axis=0, keepdims=True)
            through = through + dot_bf16(
                halves(jnp.broadcast_to(crossed, (EDGE, LANES))), fold
            )[:1]
        turn_back(t, total)
    for d in range(2):
        grad_maps[:, 2 * d * state : (2 * d + 1) * state] = grad_inputs[d]
        grad_maps[:, (2 * d + 1) * state : (2 * d + 2) * state] = grad_readers[d]
    for j in range(4 * state // LANES):
        turn_back(tiles + j, grad_maps[:, j * LANES : (j + 1) * LANES])

    ahead = lax.broadcasted_iota(jnp.int32, (length, both), 1) < heads
    from_here = triangle(length, lambda r, c: c >= r).astype(BF16)
    to_here = triangle(length, lambda r, c: c <= r).astype(BF16)
    before_here = triangle(length, lambda r, c: c < r).astype(BF16)
    after_here = triangle(length, lambda r, c: c > r).astype(BF16)
    own = enter + differ[0]
    grad_decay = (
        jnp.where(
            ahead,
            exact_sum(from_here, own) + exact_sum(before_here, leave),
            exact_sum(to_here, own) + exact_sum(after_here, leave),
        )
        + through * keep[0]
    )
    z = z_in[0]
    step = softplus(z)
    chance = sigmoid(z)
    ratio = jnp.where(step > 1e-30, chance / jnp.maximum(step, 1e-30), 1.0)
    rate = rates[...]
    grad_z = (leave + column_sums[0]) * ratio - rate * grad_decay * chance
    grad_raw[0] = grad_z
    grad_offsets[0] = jnp.sum(grad_z, axis=0, keepdims=True)
    grad_decays[0] = -rate * jnp.sum(step * grad_decay, axis=0, keepdims=True)


def exchange(x, axis, bit):
    peers = lax.axis_size(axis)
    return lax.ppermute(x, axis, [(i, i ^ (1 << bit)) for i in range(peers)])


def sum_rows(parts, axis, orders):
    place = lax.axis_index(axis)
    now = list(parts)
    for stage in range(len(orders[0])):
        for i, order in enumerate(orders):
            bit = order[stage]
            mine = (place >> bit) & 1
            half = now[i].shape[0] // 2
            sent = lax.dynamic_slice_in_dim(now[i], (1 - mine) * half, half)
            kept = lax.dynamic_slice_in_dim(now[i], mine * half, half)
            now[i] = kept + exchange(sent, axis, bit)
    for stage in reversed(range(len(orders[0]))):
        for i, order in enumerate(orders):
            bit = order[stage]
            mine = (place >> bit) & 1
            other = exchange(now[i], axis, bit)
            now[i] = jnp.where(
                mine == 0,
                jnp.concatenate([now[i], other]),
                jnp.concatenate([other, now[i]]),
            )
    return now


def orders_of(peers, count):
    bits = peers.bit_length() - 1
    plain = list(range(bits))
    if count == 1:
        return [plain]
    return [plain, [1, 0] + plain[2:]]


def local(
    hidden,
    lengths,
    prenorm,
    gating,
    values,
    states,
    stepper,
    offsets,
    decays,
    filters,
    shifts,
    kernels,
    biases,
    direct,
    postnorm,
    output,
    cotangent,
):
    micro, length, model = hidden.shape
    inner = gating.shape[1]
    heads = direct.shape[0]
    both = 2 * heads
    head_size = inner // heads
    state = states.shape[2]
    reach_cells = (filters.shape[0] - 1) // 2
    peers = lax.axis_size("seq")
    place = lax.axis_index("seq")
    head_place = lax.axis_index("head")
    inner_all = inner * lax.axis_size("head")
    rows = micro * 2 * state // peers
    tiles = inner // LANES
    dims = (length, inner, heads, state, reach_cells, rows)
    maps_width = 4 * state
    width = inner + maps_width
    long = length + 2 * EDGE
    half_peers = peers // micro

    up = [(i, i + 1) for i in range(peers - 1)]
    down = [(i + 1, i) for i in range(peers - 1)]
    swap = [(0, 1), (1, 0)]
    before = lax.ppermute(hidden[:, length - EDGE :], "seq", up)
    after = lax.ppermute(hidden[:, :EDGE], "seq", down)

    total = length * peers
    places = place * length - EDGE - reach_cells + jnp.arange(long + 2 * reach_cells, dtype=jnp.int32)
    bounds = jnp.cumsum(lengths, axis=1)
    seg = jnp.sum((places[None, :, None] >= bounds[:, None, :]).astype(jnp.int32), axis=2)
    seg = jnp.where(places < 0, -1, jnp.where(places >= total, -2, seg))
    center = seg[:, reach_cells : reach_cells + long]
    emask = jnp.stack(
        [(seg[:, o : o + long] == center).astype(F32) for o in range(2 * reach_cells + 1)], axis=2
    )
    here = center[:, EDGE : EDGE + length]
    seg_before = center[:, EDGE - 1]
    seg_after = center[:, EDGE + length]
    first, last = here[:, 0], here[:, -1]
    cols = jnp.stack(
        [(here == s[:, None]).astype(F32) for s in (seg_before, seg_after, last, first)], axis=2
    )
    keep_mask = jnp.concatenate(
        [
            jnp.broadcast_to((last == seg_before)[:, None], (micro, heads)),
            jnp.broadcast_to((first == seg_after)[:, None], (micro, heads)),
        ],
        axis=1,
    ).astype(F32)[:, None, :]
    seg_col = here[:, :, None]
    seg_row = here[:, None, :]

    taps = jnp.concatenate([filters, kernels.reshape(kernels.shape[0], -1)], axis=1)
    bias = jnp.concatenate([shifts, biases.reshape(-1)])[None]
    offsets_row = offsets.reshape(1, both)
    rates = jnp.exp(decays).reshape(1, both)
    direct_row = jnp.repeat(direct, head_size)[None]
    post_row = postnorm[None]
    states_flat = states.reshape(model, maps_width)
    stepper_flat = stepper.reshape(model, both)

    stream = jnp.concatenate([before, hidden, after], axis=1)
    scale = lax.rsqrt(jnp.mean(stream * stream, axis=2, keepdims=True) + EPSILON)
    normed = stream * scale * prenorm
    flat = normed.reshape(micro * long, model)
    weights_in = jnp.concatenate([values, states_flat], axis=1)
    mixed = dot(flat, weights_in).reshape(micro, long, width)
    normed_here = normed[:, EDGE : EDGE + length].reshape(micro * length, model)
    raw = dot(normed_here, stepper_flat).reshape(micro, length, both)
    gate = dot(normed_here, gating).reshape(micro, length, inner)
    back = dot(cotangent.reshape(micro * length, model), output, 1, 1).reshape(micro, length, inner)

    def spec(*block):
        return pl.BlockSpec((1,) + block, lambda i: (i,) + (0,) * len(block))

    def fixed(*block):
        return pl.BlockSpec(block, lambda i: (0,) * len(block))

    def shape(*dims):
        return jax.ShapeDtypeStruct(dims, F32)

    packed = tiles * rows + EDGE
    pay_spec = pl.BlockSpec((half_peers, packed, LANES), lambda i: (i, 0, 0))
    plain_spec = pl.BlockSpec((half_peers, tiles * rows, LANES), lambda i: (i, 0, 0))
    small = spec(length, both)
    (
        conv,
        act,
        z,
        run,
        reach,
        tail,
        run_rows,
        late_rows,
        keep,
        pay,
    ) = pl.pallas_call(
        partial(front_kernel, dims),
        grid=(micro,),
        in_specs=[
            spec(long, width),
            small,
            fixed(2 * reach_cells + 1, width),
            fixed(1, width),
            fixed(1, both),
            fixed(1, both),
            spec(long, 2 * reach_cells + 1),
            spec(length, 4),
            spec(1, both),
        ],
        out_specs=[
            spec(length, width),
            spec(length, width),
            small,
            small,
            small,
            small,
            spec(both, length),
            spec(both, length),
            spec(1, both),
            pay_spec,
        ],
        out_shape=[
            shape(micro, length, width),
            shape(micro, length, width),
            shape(micro, length, both),
            shape(micro, length, both),
            shape(micro, length, both),
            shape(micro, length, both),
            shape(micro, both, length),
            shape(micro, both, length),
            shape(micro, 1, both),
            shape(peers, packed, LANES),
        ],
        scratch_shapes=[pltpu.VMEM((2 * reach_cells + 1, length, LANES), F32)],
        compiler_params=PARAMS,
        name="front",
    )(mixed, raw, taps, bias, offsets_row, rates, emask, cols, keep_mask)

    direction = lax.rem(place // (peers // (2 * micro)), 2)

    def prefix(terms, keeps, flipped):
        return pl.pallas_call(
            partial(prefix_kernel, tiles, rows),
            in_specs=[
                pl.BlockSpec(memory_space=pltpu.SMEM),
                pl.BlockSpec(memory_space=pltpu.VMEM),
                pl.BlockSpec(memory_space=pltpu.VMEM),
            ],
            out_specs=pl.BlockSpec(memory_space=pltpu.VMEM),
            out_shape=shape(peers, tiles * rows, LANES),
            compiler_params=PARAMS,
            name="prefix",
        )(flipped.reshape(1).astype(jnp.int32), terms, keeps)

    def swap_all(x):
        return lax.all_to_all(x, "seq", 0, 0, tiled=True)

    terms = swap_all(pay)
    arrived = swap_all(prefix(terms, terms, direction))

    inside = pl.pallas_call(
        partial(inside_kernel, dims),
        grid=(micro,),
        in_specs=[spec(length, width), small, spec(both, length), spec(length, 1), spec(1, length)],
        out_specs=spec(length, inner),
        out_shape=shape(micro, length, inner),
        compiler_params=PARAMS,
        name="inside",
    )(act, run, late_rows, seg_col, seg_row)

    wide = spec(length, inner)
    row = fixed(1, inner)
    mixed_y, sums, before_states = pl.pallas_call(
        partial(join_kernel, dims),
        grid=(micro,),
        in_specs=[wide, plain_spec, spec(length, width), small, wide, wide, row, row],
        out_specs=[wide, spec(length, LANES), spec(2, state, inner)],
        out_shape=[
            shape(micro, length, inner),
            shape(micro, length, LANES),
            shape(micro, 2, state, inner),
        ],
        compiler_params=PARAMS,
        name="join",
    )(inside, arrived, act, reach, gate, back, direct_row, post_row)
    peer_sums = lax.ppermute(sums, "head", swap)

    row_out = spec(1, inner)
    grad_y, grad_gate, normal, pay_back, grad_post, grad_direct = pl.pallas_call(
        partial(turn_kernel, dims, inner_all),
        grid=(micro,),
        in_specs=[
            spec(length, LANES),
            spec(length, LANES),
            wide,
            wide,
            wide,
            spec(length, width),
            small,
            row,
            row,
        ],
        out_specs=[wide, wide, wide, plain_spec, row_out, row_out],
        out_shape=[
            shape(micro, length, inner),
            shape(micro, length, inner),
            shape(micro, length, inner),
            shape(peers, tiles * rows, LANES),
            shape(micro, 1, inner),
            shape(micro, 1, inner),
        ],
        compiler_params=PARAMS,
        name="turn",
    )(sums, peer_sums, mixed_y, gate, back, act, reach, direct_row, post_row)

    back_terms = swap_all(pay_back)
    back_arrived = swap_all(prefix(back_terms, terms, 1 - direction))

    normal_flat = normal.reshape(micro * length, inner)
    grad_gate_flat = grad_gate.reshape(micro * length, inner)
    grad_output = dot(normal_flat, cotangent.reshape(micro * length, model), 0, 0)
    grad_gating = dot(normed_here, grad_gate_flat, 0, 0)
    early = jnp.concatenate([grad_output, grad_gating], axis=0)
    half = early.shape[0] // 2
    early_sum = sum_rows([early[:half], early[half:]], "seq", orders_of(peers, 2))

    projected = dot(normal_flat, output)
    result = hidden + (projected + lax.ppermute(projected, "head", swap)).reshape(hidden.shape)
    grad_normed_gate = dot(grad_gate_flat, gating, 1, 1).reshape(micro, length, model)

    grad_inside, grad_maps_inside, differ, column_sums = pl.pallas_call(
        partial(inside_back_kernel, dims),
        grid=(micro,),
        in_specs=[
            spec(length, width),
            wide,
            small,
            spec(both, length),
            spec(length, 1),
            spec(1, length),
        ],
        out_specs=[wide, spec(length, maps_width), small, small],
        out_shape=[
            shape(micro, length, inner),
            shape(micro, length, maps_width),
            shape(micro, length, both),
            shape(micro, length, both),
        ],
        scratch_shapes=[pltpu.VMEM((length, LANES), F32), pltpu.VMEM((both, length), F32)],
        compiler_params=PARAMS,
        name="inside_back",
    )(act, grad_y, run, late_rows, seg_col, seg_row)

    taps_spec = spec(2 * reach_cells + 1, width)
    (grad_mixed, grad_raw, grad_taps, grad_bias, grad_offsets, grad_decays) = pl.pallas_call(
        partial(end_kernel, dims),
        grid=(micro,),
        in_specs=[
            plain_spec,
            spec(length, width),
            wide,
            small,
            small,
            small,
            spec(length, width),
            spec(2, state, inner),
            spec(1, both),
            wide,
            spec(length, maps_width),
            small,
            small,
            spec(long, width),
            fixed(2 * reach_cells + 1, width),
            spec(long, 2 * reach_cells + 1),
            fixed(1, both),
            row,
        ],
        out_specs=[
            spec(long, width),
            small,
            taps_spec,
            spec(1, width),
            spec(1, both),
            spec(1, both),
        ],
        out_shape=[
            shape(micro, long, width),
            shape(micro, length, both),
            shape(micro, 2 * reach_cells + 1, width),
            shape(micro, 1, width),
            shape(micro, 1, both),
            shape(micro, 1, both),
        ],
        scratch_shapes=[
            pltpu.VMEM((2, state, inner), F32),
            pltpu.VMEM((length, maps_width), F32),
            pltpu.VMEM((length + 2 * EDGE, LANES), F32),
            pltpu.VMEM((2 * reach_cells + 1, long, LANES), F32),
        ],
        compiler_params=PARAMS,
        name="end",
    )(
        back_arrived,
        act,
        grad_y,
        reach,
        tail,
        z,
        conv,
        before_states,
        keep,
        grad_inside,
        grad_maps_inside,
        differ,
        column_sums,
        mixed,
        taps,
        emask,
        rates,
        direct_row,
    )

    grad_mixed_flat = grad_mixed.reshape(micro * long, width)
    grad_raw_flat = grad_raw.reshape(micro * length, both)
    grad_in = dot(flat, grad_mixed_flat, 0, 0)
    grad_values = grad_in[:, :inner]
    grad_states = grad_in[:, inner:]
    grad_stepper = dot(normed_here, grad_raw_flat, 0, 0)

    grad_normed = dot(grad_mixed_flat, weights_in, 1, 1).reshape(micro, long, model)
    grad_normed = grad_normed + jnp.pad(
        grad_normed_gate
        + dot(grad_raw_flat, stepper_flat, 1, 1).reshape(micro, length, model),
        ((0, 0), (EDGE, EDGE), (0, 0)),
    )
    grad_prenorm = jnp.sum(grad_normed * (stream * scale), axis=(0, 1))
    grad_normed = grad_normed + lax.ppermute(grad_normed, "head", swap)
    from_after = lax.ppermute(grad_normed[:, :EDGE], "seq", down)
    from_before = lax.ppermute(grad_normed[:, EDGE + length :], "seq", up)
    grad_here = grad_normed[:, EDGE : EDGE + length] + jnp.concatenate(
        [from_before, jnp.zeros((micro, length - 2 * EDGE, model), F32), from_after], axis=1
    )
    scale_here = scale[:, EDGE : EDGE + length]
    pulled = grad_here * prenorm
    grad_hidden = (
        cotangent
        + scale_here * pulled
        - hidden
        * (scale_here**3 * jnp.sum(pulled * hidden, axis=2, keepdims=True) / model)
    )

    cut = maps_width // 2
    own_states = lax.dynamic_slice_in_dim(grad_states, head_place * cut, cut, 1)
    sent_states = lax.dynamic_slice_in_dim(grad_states, (1 - head_place) * cut, cut, 1)
    own_states = own_states + lax.ppermute(sent_states, "head", swap)

    def lay(x):
        flat_x = x.reshape(-1)
        pad = -flat_x.shape[0] % model
        return jnp.pad(flat_x, (0, pad)).reshape(-1, model)

    grad_taps = jnp.sum(grad_taps, axis=0)
    grad_bias = jnp.sum(grad_bias, axis=0)
    grad_direct = jnp.sum(jnp.sum(grad_direct, axis=0).reshape(heads, head_size), axis=1)
    pieces = [
        grad_values,
        lay(own_states),
        lay(grad_stepper),
        lay(grad_taps[:, :inner]),
        lay(grad_bias[:, :inner]),
        lay(jnp.sum(grad_post, axis=0)),
        lay(
            jnp.concatenate(
                [
                    grad_direct,
                    jnp.sum(grad_offsets, axis=0).reshape(-1),
                    jnp.sum(grad_decays, axis=0).reshape(-1),
                ]
            )
        ),
        lay(grad_prenorm),
        lay(grad_taps[:, inner:]),
        lay(grad_bias[:, inner:]),
    ]
    late = jnp.concatenate(pieces, axis=0)
    unit = 2 * EDGE * peers
    late = jnp.pad(late, ((0, -late.shape[0] % unit), (0, 0)))
    half = late.shape[0] // 2
    late_sum = jnp.concatenate(sum_rows([late[:half], late[half:]], "seq", orders_of(peers, 2)))
    done = []
    at = 0
    for piece in pieces:
        done.append(late_sum[at : at + piece.shape[0]])
        at += piece.shape[0]
    shared = jnp.concatenate(done[7:])
    shared = shared + lax.ppermute(shared, "head", swap)
    misc = done[6].reshape(-1)
    own_states = done[1].reshape(model, cut)
    other_states = lax.ppermute(own_states, "head", swap)
    grad_states = jnp.where(
        head_place == 0,
        jnp.concatenate([own_states, other_states], axis=1),
        jnp.concatenate([other_states, own_states], axis=1),
    ).reshape(states.shape)
    kernel_size = kernels.size
    kernel_rows = done[8].shape[0]
    return (
        result,
        grad_hidden,
        shared[0],
        early_sum[1],
        done[0],
        grad_states,
        done[2].reshape(-1)[: stepper.size].reshape(stepper.shape),
        misc[heads : heads + both].reshape(offsets.shape),
        misc[heads + both : heads + 2 * both].reshape(decays.shape),
        done[3],
        done[4].reshape(-1),
        shared[1 : 1 + kernel_rows].reshape(-1)[:kernel_size].reshape(kernels.shape),
        shared[1 + kernel_rows :].reshape(-1)[: biases.size].reshape(biases.shape),
        misc[:heads],
        done[5].reshape(-1),
        early_sum[0],
    )


def solution(mesh):
    in_specs = (
        P(None, "seq", None),
        P(),
        P(),
        P(None, "head"),
        P(None, "head"),
        P(),
        P(None, None, "head"),
        P(None, "head"),
        P(None, "head"),
        P(None, "head"),
        P("head"),
        P(),
        P(),
        P("head"),
        P("head"),
        P("head", None),
        P(None, "seq", None),
    )
    out_specs = (
        P(None, "seq", None),
        P(None, "seq", None),
        P(),
        P(None, "head"),
        P(None, "head"),
        P(),
        P(None, None, "head"),
        P(None, "head"),
        P(None, "head"),
        P(None, "head"),
        P("head"),
        P(),
        P(),
        P("head"),
        P("head"),
        P("head", None),
    )
    return jax.shard_map(local, mesh=mesh, in_specs=in_specs, out_specs=out_specs, check_vma=False)
```

```python
from functools import partial

import jax
import jax.numpy as jnp
from jax import lax
from jax.experimental import pallas as pl
from jax.experimental.pallas import tpu as pltpu
from jax.sharding import PartitionSpec as P

EPSILON = 1e-05
HIGH = lax.Precision.HIGH
F32 = jnp.float32
BF16 = jnp.bfloat16
LANES = 128
WIDE = 256
EDGE = 8
PARAMS = pltpu.CompilerParams(vmem_limit_bytes=56 * 1024 * 1024)


def dot(left, right, over_left=1, over_right=0, precision=HIGH):
    return lax.dot_general(
        left,
        right,
        (((over_left,), (over_right,)), ((), ())),
        precision=precision,
        preferred_element_type=F32,
    )


def split(x):
    top = x.astype(BF16)
    return top, (x - top.astype(F32)).astype(BF16)


def dot_bf16(left, right, over_left=1, over_right=0):
    return lax.dot_general(
        left,
        right,
        (((over_left,), (over_right,)), ((), ())),
        preferred_element_type=F32,
    )


def spread(first, head_size, both):
    rows = lax.broadcasted_iota(jnp.int32, (2 * both, WIDE), 0)
    columns = lax.broadcasted_iota(jnp.int32, (2 * both, WIDE), 1)
    return (lax.rem(rows, both) == first + columns // head_size).astype(BF16)


def gather_heads(first, head_size, both, parts=2):
    rows = lax.broadcasted_iota(jnp.int32, (parts * WIDE, both), 0)
    columns = lax.broadcasted_iota(jnp.int32, (parts * WIDE, both), 1)
    return (columns == first + lax.rem(rows, WIDE) // head_size).astype(BF16)


def split3(x):
    top = x.astype(BF16)
    rest = x - top.astype(F32)
    middle = rest.astype(BF16)
    return top, middle, (rest - middle.astype(F32)).astype(BF16)


def halves(x):
    return jnp.concatenate(split(x), axis=1)


def triangle(size, keep):
    rows = lax.broadcasted_iota(jnp.int32, (size, size), 0)
    columns = lax.broadcasted_iota(jnp.int32, (size, size), 1)
    return keep(rows, columns)


def exact_sum(zero_one, x):
    a, b, c = split3(x)
    return dot_bf16(zero_one, a) + dot_bf16(zero_one, b) + dot_bf16(zero_one, c)


def flip(x):
    size = x.shape[1]
    one = triangle(size, lambda r, c: r == c).astype(BF16)
    a, b, c = split3(x)
    return dot_bf16(one, a, 1, 1) + dot_bf16(one, b, 1, 1) + dot_bf16(one, c, 1, 1)


def sigmoid(x):
    return 1.0 / (1.0 + jnp.exp(-x))


def softplus(x):
    return jnp.maximum(x, 0.0) + jnp.log1p(jnp.exp(-jnp.abs(x)))


def bounds_of(lengths, i):
    ends = []
    total = jnp.int32(0)
    for k in range(lengths.shape[1]):
        total = total + lengths[i, k]
        ends.append(total)
    return ends


def document(places, ends):
    found = sum(jnp.where(places >= end, 1, 0) for end in ends)
    return jnp.where(places < 0, -1, jnp.where(places >= ends[-1], -2, found))


def same_document(first, ends, length):
    rows = document(first + lax.broadcasted_iota(jnp.int32, (length, LANES), 0), ends)
    columns = document(first + lax.broadcasted_iota(jnp.int32, (1, length), 1), ends)
    return jnp.concatenate([rows] * (length // LANES), axis=1) == columns


def fill_masks(masks, documents, first, ends, start, rows, reach_cells):
    total = documents.shape[0]
    documents[...] = document(
        first - 2 * EDGE + lax.broadcasted_iota(jnp.int32, (total, LANES), 0), ends
    )
    center = documents[EDGE + start : EDGE + start + rows]
    for o in range(2 * reach_cells + 1):
        at = EDGE + start + o - reach_cells
        masks[o] = (documents[at : at + rows] == center).astype(F32)


def left3(x):
    top = x.astype(BF16).astype(F32)
    return jnp.concatenate([top, top, x - top], axis=1).astype(BF16)


def right3(x):
    top, low = split(x)
    return jnp.concatenate([top, low, top], axis=0)


def stacked(x):
    return jnp.concatenate(split(x), axis=0)


def front_kernel(
    dims,
    place,
    lengths,
    before,
    hidden,
    after,
    prenorm,
    values,
    states,
    stepper,
    filters,
    kernels,
    shifts,
    biases,
    offsets,
    decays,
    normed,
    mixed,
    conv,
    act,
    maps_t,
    z_out,
    run,
    late,
    run_rows,
    late_rows,
    reach,
    tail,
    keep,
    taps,
    pay,
    documents,
    masks,
):
    length, inner, heads, state, reach_cells, rows = dims
    head_size = inner // heads
    both = 2 * heads
    maps_width = 4 * state
    width = inner + maps_width
    offsets_count = 2 * reach_cells + 1
    i = pl.program_id(0)
    ends = bounds_of(lengths, i)
    first = place[0] * length
    fill_masks(masks, documents, first, ends, EDGE, length, reach_cells)

    gain = prenorm[...]

    def norm(x):
        mean = jnp.sum(x * x, axis=1, keepdims=True) / x.shape[1]
        return x * lax.rsqrt(mean + EPSILON) * gain

    normed[0, :EDGE] = norm(before[0])
    for r in range(0, length, 64):
        normed[0, EDGE + r : EDGE + r + 64] = norm(hidden[0, r : r + 64])
    normed[0, EDGE + length :] = norm(after[0])

    whole = normed[0]
    for t in range(inner // WIDE):
        at = slice(t * WIDE, (t + 1) * WIDE)
        mixed[0, :, at] = dot(whole, values[:, at])
    mixed[0, :, inner:] = dot(whole, states[...])
    raw = dot(normed[0, EDGE : EDGE + length], stepper[...])

    taps[:offsets_count, :inner] = filters[...]
    taps[offsets_count:, :inner] = shifts[...]
    for k in range(4):
        at = slice(inner + k * state, inner + (k + 1) * state)
        taps[:offsets_count, at] = kernels[:, k, :]
        taps[offsets_count:, at] = biases[k : k + 1, :]

    def column(j, _):
        at = pl.ds(pl.multiple_of(j * LANES, LANES), LANES)
        total = jnp.broadcast_to(taps[offsets_count:, at], (length, LANES))
        for o in range(offsets_count):
            begin = EDGE - reach_cells + o
            total = total + (mixed[0, begin : begin + length, at] * taps[o : o + 1, at]) * masks[o]
        conv[0, :, at] = total
        act[0, :, at] = total * sigmoid(total)
        return 0

    lax.fori_loop(0, width // LANES, column, 0)
    flipped = jnp.transpose(act[0, :, inner:])
    maps_t[0] = flipped

    ahead = lax.broadcasted_iota(jnp.int32, (length, both), 1) < heads
    ahead_row = ahead[:1]
    z = raw + jnp.concatenate([offsets[0:1, :], offsets[1:2, :]], axis=1)
    rates = jnp.exp(jnp.concatenate([decays[0:1, :], decays[1:2, :]], axis=1))
    step = softplus(z)
    decay = -step * rates
    lower = triangle(length, lambda r, c: r >= c).astype(BF16)
    upper = triangle(length, lambda r, c: r <= c).astype(BF16)
    running = jnp.where(ahead, exact_sum(lower, decay), exact_sum(upper, decay))
    edge = jnp.where(ahead_row, running[length - 1 :], running[:1])
    here = document(first + lax.broadcasted_iota(jnp.int32, (length, both), 0), ends)
    seg_before = document(first - 1, ends)
    seg_after = document(first + length, ends)
    seg_first = document(first, ends)
    seg_last = document(first + length - 1, ends)
    enter = (here == jnp.where(ahead, seg_before, seg_after)).astype(F32)
    leave = (here == jnp.where(ahead, seg_last, seg_first)).astype(F32)
    keep_mask = jnp.where(
        ahead_row,
        jnp.where(seg_last == seg_before, 1.0, 0.0),
        jnp.where(seg_first == seg_after, 1.0, 0.0),
    )
    reach_now = enter * jnp.exp(running)
    tail_now = leave * jnp.exp(edge - running) * step
    keep_now = keep_mask * jnp.exp(edge)
    late_now = running - jnp.log(jnp.maximum(step, 1e-37))
    z_out[0] = z
    run[0] = running
    late[0] = late_now
    reach[0] = reach_now
    tail[0] = tail_now
    run_rows[0] = flip(running)
    late_rows[0] = flip(late_now)
    keep[0] = keep_now

    tail_halves = halves(tail_now)
    keep_halves = halves(jnp.broadcast_to(keep_now, (EDGE, both)))
    pieces = state // rows
    per_tile = WIDE // head_size
    for d in range(2):
        maps_now = stacked(flipped[2 * d * state : (2 * d + 1) * state])
        keeps = []
        for t in range(inner // WIDE):
            grow = spread(d * heads + t * per_tile, head_size, both)
            weighted = act[0, :, t * WIDE : (t + 1) * WIDE] * dot_bf16(tail_halves, grow)
            put_states(pay, d, t, product_of_stack(maps_now, weighted, state), pieces, rows)
            keep_wide = dot_bf16(keep_halves, grow)[:1]
            keeps += [keep_wide[:, k * LANES : (k + 1) * LANES] for k in range(WIDE // LANES)]
        tiles = inner // LANES
        keeps.append(jnp.zeros((EDGE - tiles, LANES), F32))
        keep_block = jnp.concatenate(keeps, axis=0)
        for j in range(pieces):
            pay[d * pieces + j, tiles * rows :, :] = keep_block


def product_of_stack(stack, x, size):
    top, low = split(x)
    twice = dot_bf16(stack, top)
    return twice[:size] + twice[size:] + dot_bf16(stack[:size], low)


def put_states(pay, d, t, own, pieces, rows):
    for k in range(WIDE // LANES):
        at = (t * (WIDE // LANES) + k) * rows
        for j in range(pieces):
            pay[d * pieces + j, at : at + rows, :] = own[
                j * rows : (j + 1) * rows, k * LANES : (k + 1) * LANES
            ]


def prefix_kernel(tiles, rows, flipped, terms, keeps, into):
    peers = terms.shape[0]
    back = flipped[0] != 0

    def turn(i, carry):
        at = jnp.where(back, peers - 1 - i, i)
        factor = keeps[at, tiles * rows :, :]
        new = []
        for t in range(tiles):
            into[at, t * rows : (t + 1) * rows, :] = carry[t]
            new.append(
                carry[t] * factor[t : t + 1] + terms[at, t * rows : (t + 1) * rows, :]
            )
        return tuple(new)

    lax.fori_loop(0, peers, turn, tuple(jnp.zeros((rows, LANES), F32) for _ in range(tiles)))


def scores_of(act, ends, first, inner, state, length):
    def part(k):
        return act[0, :, inner + k * state : inner + (k + 1) * state]

    same = same_document(first, ends, length)
    below = triangle(length, lambda r, c: r > c)
    above = triangle(length, lambda r, c: r < c)
    return part, same, below, above


def inside_kernel(dims, place, lengths, act, run, late_rows, inside):
    length, inner, heads, state, _, _ = dims
    head_size = inner // heads
    per_tile = LANES // head_size
    ends = bounds_of(lengths, pl.program_id(0))
    part, same, below, above = scores_of(act, ends, place[0] * length, inner, state, length)
    scores = jnp.where(below & same, dot(part(1), part(0), 1, 1), 0.0) + jnp.where(
        above & same, dot(part(3), part(2), 1, 1), 0.0
    )
    run_at = run[0]
    lane = lax.broadcasted_iota(jnp.int32, (length, LANES), 1) // head_size
    for t in range(inner // LANES):
        top, low = split(act[0, :, t * LANES : (t + 1) * LANES])
        pair = jnp.concatenate([top, low], axis=1)
        total = jnp.zeros((length, LANES), F32)
        for k in range(per_tile):
            h = t * per_tile + k
            weights = jnp.exp(
                jnp.where(
                    below,
                    run_at[:, h : h + 1] - late_rows[0, h : h + 1, :],
                    run_at[:, heads + h : heads + h + 1]
                    - late_rows[0, heads + h : heads + h + 1, :],
                )
            )
            m_top, m_low = split(scores * weights)
            wide = dot_bf16(m_top, pair)
            now = wide[:, :LANES] + wide[:, LANES:] + dot_bf16(m_low, top)
            total = jnp.where(lane == k, now, total)
        inside[0, :, t * LANES : (t + 1) * LANES] = total


def unpack(pay, into, tiles, rows, state):
    pieces = state // rows
    for d in range(2):
        for j in range(pieces):
            for t in range(tiles):
                into[d, j * rows : (j + 1) * rows, t * LANES : (t + 1) * LANES] = pay[
                    d * pieces + j, t * rows : (t + 1) * rows, :
                ]


def join_kernel(
    dims, inside, pay, act, reach, gate, back, direct, postnorm, mixed_y, sums, states
):
    length, inner, heads, state, _, rows = dims
    head_size = inner // heads
    both = 2 * heads
    per_tile = WIDE // head_size
    unpack(pay, states.at[0], inner // LANES, rows, state)
    reach_halves = halves(reach[0])
    readers = [left3(act[0, :, inner + k * state : inner + (k + 1) * state]) for k in (1, 3)]
    squares = jnp.zeros((length, WIDE), F32)
    crossed = jnp.zeros((length, WIDE), F32)
    for t in range(inner // WIDE):
        at = slice(t * WIDE, (t + 1) * WIDE)
        total = inside[0, :, at] + direct[:, at] * act[0, :, at]
        for d in range(2):
            grow = spread(d * heads + t * per_tile, head_size, both)
            total = total + dot_bf16(readers[d], right3(states[0, d, :, at])) * dot_bf16(
                reach_halves, grow
            )
        mixed_y[0, :, at] = total
        gate_now = gate[0, EDGE : EDGE + length, at]
        gated = total * (gate_now * sigmoid(gate_now))
        squares = squares + gated * gated
        crossed = crossed + gated * postnorm[:, at] * back[0, :, at]
    lane = lax.broadcasted_iota(jnp.int32, (length, LANES), 1)
    sums[0] = jnp.where(
        lane == 0,
        jnp.sum(squares, axis=1, keepdims=True),
        jnp.sum(crossed, axis=1, keepdims=True),
    )


def norm_of(sums, peer_sums, inner_all, length):
    both_sums = sums[0] + peer_sums[0]
    q = lax.rsqrt(both_sums[:, 0:1] / inner_all + EPSILON)
    pull = both_sums[:, 1:2] * (q * q * q) / inner_all
    return (
        jnp.broadcast_to(q, (length, LANES)),
        jnp.broadcast_to(pull, (length, LANES)),
    )


def turn_kernel(
    dims,
    inner_all,
    sums,
    peer_sums,
    mixed_y,
    gate,
    back,
    maps_t,
    reach,
    postnorm,
    grad_y,
    normal,
    pay,
):
    length, inner, heads, state, _, rows = dims
    head_size = inner // heads
    both = 2 * heads
    per_tile = WIDE // head_size
    pieces = state // rows
    q, pull = norm_of(sums, peer_sums, inner_all, length)
    reach_halves = halves(reach[0])
    readers = [stacked(maps_t[0, k * state : (k + 1) * state]) for k in (1, 3)]
    for t in range(inner // WIDE):
        upstreams = []
        for k in range(WIDE // LANES):
            at = slice(t * WIDE + k * LANES, t * WIDE + (k + 1) * LANES)
            gate_now = gate[0, EDGE : EDGE + length, at]
            opened = gate_now * sigmoid(gate_now)
            gated = mixed_y[0, :, at] * opened
            post = postnorm[:, at]
            upstream = (q * back[0, :, at] * post - pull * gated) * opened
            grad_y[0, :, at] = upstream
            normal[0, :, at] = gated * post * q
            upstreams.append(upstream)
        upstream = jnp.concatenate(upstreams, axis=1)
        for d in range(2):
            grow = spread(d * heads + t * per_tile, head_size, both)
            seed = product_of_stack(readers[d], upstream * dot_bf16(reach_halves, grow), state)
            put_states(pay, d, t, seed, pieces, rows)


def side_kernel(
    dims,
    inner_all,
    sums,
    peer_sums,
    mixed_y,
    gate,
    back,
    act,
    grad_y,
    postnorm,
    grad_gate,
    smalls,
):
    length, inner, heads, _, _, _ = dims
    q, pull = norm_of(sums, peer_sums, inner_all, length)
    grad_gate[0, :EDGE] = jnp.zeros((EDGE, inner), F32)
    grad_gate[0, EDGE + length :] = jnp.zeros((EDGE, inner), F32)
    smalls[0] = jnp.zeros((EDGE, inner), F32)
    for t in range(inner // LANES):
        at = slice(t * LANES, (t + 1) * LANES)
        y = mixed_y[0, :, at]
        gate_now = gate[0, EDGE : EDGE + length, at]
        chance = sigmoid(gate_now)
        gated = y * (gate_now * chance)
        scaled = q * back[0, :, at]
        grad_gated = scaled * postnorm[:, at] - pull * gated
        grad_gate[0, EDGE : EDGE + length, at] = (
            grad_gated * y * (chance * (1.0 + gate_now * (1.0 - chance)))
        )
        smalls[0, 0:1, at] = jnp.sum(scaled * gated, axis=0, keepdims=True)
        smalls[0, 1:2, at] = jnp.sum(grad_y[0, :, at] * act[0, :, at], axis=0, keepdims=True)


def inside_back_kernel(
    dims,
    place,
    lengths,
    act,
    grad_y,
    late,
    run_rows,
    reach,
    states,
    direct,
    grad_signal,
    grad_maps,
    own,
    column_sums,
    read_parts,
):
    length, inner, heads, state, _, _ = dims
    head_size = inner // heads
    per_tile = LANES // head_size
    both = 2 * heads
    ends = bounds_of(lengths, pl.program_id(0))
    part, same, below, above = scores_of(act, ends, place[0] * length, inner, state, length)
    scores = jnp.where(above & same, dot(part(0), part(1), 1, 1), 0.0) + jnp.where(
        below & same, dot(part(2), part(3), 1, 1), 0.0
    )
    late_at = late[0]
    lane = lax.broadcasted_iota(jnp.int32, (length, LANES), 1)
    write_sums = jnp.zeros((length, LANES), F32)
    grad_scores = jnp.zeros((length, length), F32)
    zero = jnp.zeros((length, LANES), BF16)
    for t in range(inner // LANES):
        at = slice(t * LANES, (t + 1) * LANES)
        s_top, s_low = split(act[0, :, at])
        g_top, g_low = split(grad_y[0, :, at])
        pair = jnp.concatenate([g_top, g_low], axis=1)
        two = jnp.concatenate([g_top, g_top], axis=1)
        total = jnp.zeros((length, LANES), F32)
        for k in range(per_tile):
            h = t * per_tile + k
            weights = jnp.exp(
                jnp.where(
                    above,
                    run_rows[0, h : h + 1, :] - late_at[:, h : h + 1],
                    run_rows[0, heads + h : heads + h + 1, :]
                    - late_at[:, heads + h : heads + h + 1],
                )
            )
            mine = lane // head_size == k
            i_top = jnp.where(mine, s_top, zero)
            i_low = jnp.where(mine, s_low, zero)
            overlap = dot_bf16(jnp.concatenate([i_top, i_low], axis=1), two, 1, 1) + dot_bf16(
                i_top, g_low, 1, 1
            )
            product = weights * overlap
            grad_scores = grad_scores + product
            whole = product * scores
            ahead = jnp.where(above, whole, 0.0)
            ahead_writes = jnp.sum(ahead, axis=1, keepdims=True)
            all_writes = jnp.sum(whole, axis=1, keepdims=True)
            write_sums = jnp.where(lane == h, ahead_writes, write_sums)
            write_sums = jnp.where(lane == heads + h, all_writes - ahead_writes, write_sums)
            ahead_reads = jnp.sum(ahead, axis=0, keepdims=True)
            read_parts[h : h + 1, :] = ahead_reads
            read_parts[heads + h : heads + h + 1, :] = (
                jnp.sum(whole, axis=0, keepdims=True) - ahead_reads
            )
            m_top, m_low = split(scores * weights)
            wide = dot_bf16(m_top, pair)
            now = wide[:, :LANES] + wide[:, LANES:] + dot_bf16(m_low, g_top)
            total = jnp.where(mine, now, total)
        grad_signal[0, :, at] = total + direct[:, at] * grad_y[0, :, at]

    writes = write_sums[:, :both]
    column_sums[0] = writes
    total_own = flip_back(read_parts[...]) - writes
    reach_halves = halves(reach[0])
    per_wide = WIDE // head_size
    for d in range(2):
        side = (above, below)[d]
        grads = jnp.where(side & same, grad_scores, 0.0)
        reader = part(2 * d + 1)
        reader3 = left3(reader)
        grad_reader = dot(grads, part(2 * d), 0, 0)
        for t in range(inner // WIDE):
            at = slice(t * WIDE, (t + 1) * WIDE)
            first = d * heads + t * per_wide
            before = states[0, d, :, at]
            reached = grad_y[0, :, at] * dot_bf16(
                reach_halves, spread(first, head_size, both)
            )
            seen = dot_bf16(reader3, right3(before))
            total_own = total_own + dot_bf16(
                halves(reached * seen), gather_heads(first, head_size, both)
            )
            grad_reader = grad_reader + product_with(reached, stacked(before), state)
        grad_maps[0, :, 2 * d * state : (2 * d + 1) * state] = dot(grads, reader)
        grad_maps[0, :, (2 * d + 1) * state : (2 * d + 2) * state] = grad_reader
    own[0] = total_own


def product_with(x, stack, size):
    top, low = split(x)
    twice = dot_bf16(top, stack, 1, 1)
    return twice[:, :size] + twice[:, size:] + dot_bf16(low, stack[:size], 1, 1)


def flip_back(x):
    size = x.shape[0]
    one = triangle(size, lambda r, c: r == c).astype(BF16)
    a, b, c = split3(x)
    return dot_bf16(a, one, 0, 0) + dot_bf16(b, one, 0, 0) + dot_bf16(c, one, 0, 0)


def end_kernel(
    dims,
    place,
    lengths,
    pay,
    act,
    z_in,
    tail,
    conv,
    states,
    keep,
    grad_inside,
    grad_maps,
    own,
    column_sums,
    mixed,
    taps,
    decays,
    grad_values,
    grad_states,
    grad_raw,
    smalls,
    later,
    grad_act,
    padded,
    documents,
    masks,
):
    length, inner, heads, state, reach_cells, rows = dims
    head_size = inner // heads
    both = 2 * heads
    per_tile = WIDE // head_size
    width = inner + 4 * state
    offsets_count = 2 * reach_cells + 1
    long = length + 2 * EDGE
    first_row = EDGE - reach_cells
    span = length + 2 * reach_cells
    unpack(pay, later, inner // LANES, rows, state)
    ends = bounds_of(lengths, pl.program_id(0))
    fill_masks(masks, documents, place[0] * length, ends, first_row, span, reach_cells)

    tail_halves = halves(tail[0])
    leave = jnp.zeros((length, both), F32)
    through = jnp.zeros((1, both), F32)
    for d in range(2):
        writer3 = left3(act[0, :, inner + 2 * d * state : inner + (2 * d + 1) * state])
        grad_writer = grad_maps[0, :, 2 * d * state : (2 * d + 1) * state]
        for t in range(inner // WIDE):
            at = slice(t * WIDE, (t + 1) * WIDE)
            first = d * heads + t * per_tile
            fold = gather_heads(first, head_size, both)
            after = later[d, :, at]
            tails = dot_bf16(tail_halves, spread(first, head_size, both))
            weighted = act[0, :, at] * tails
            pulled = dot_bf16(writer3, right3(after))
            base = grad_inside[0, :, at] if d == 0 else grad_act[:, at]
            grad_act[:, at] = base + tails * pulled
            leave = leave + dot_bf16(halves(weighted * pulled), fold)
            grad_writer = grad_writer + product_with(weighted, stacked(after), state)
            crossed = jnp.sum(states[0, d, :, at] * after, axis=0, keepdims=True)
            through = (
                through + dot_bf16(halves(jnp.broadcast_to(crossed, (EDGE, WIDE))), fold)[:1]
            )
        at = inner + 2 * d * state
        grad_act[:, at : at + state] = grad_writer
        grad_act[:, at + state : at + 2 * state] = grad_maps[
            0, :, (2 * d + 1) * state : (2 * d + 2) * state
        ]

    for edge in (slice(0, EDGE), slice(EDGE + length, long)):
        padded[edge] = jnp.zeros((EDGE, LANES), F32)

    def column(j, _, into, shift):
        at = pl.ds(pl.multiple_of(j * LANES, LANES), LANES)
        put = pl.ds(pl.multiple_of((j - shift) * LANES, LANES), LANES)
        value = conv[0, :, at]
        chance = sigmoid(value)
        grad = grad_act[:, at] * (chance * (1.0 + value * (1.0 - chance)))
        padded[EDGE : EDGE + length] = grad
        smalls[0, offsets_count : offsets_count + 1, at] = jnp.sum(grad, axis=0, keepdims=True)
        back = jnp.zeros((span, LANES), F32)
        for o in range(offsets_count):
            mirror = offsets_count - 1 - o
            begin = first_row - (o - reach_cells)
            back = back + (padded[begin : begin + span] * taps[o : o + 1, at]) * masks[mirror]
            smalls[0, o : o + 1, at] = jnp.sum(
                (grad * mixed[0, first_row + o : first_row + o + length, at])
                * masks[o, reach_cells : reach_cells + length],
                axis=0,
                keepdims=True,
            )
        into[0, :EDGE, put] = jnp.zeros((EDGE, LANES), F32)
        into[0, EDGE + length :, put] = jnp.zeros((EDGE, LANES), F32)
        into[0, first_row : first_row + span, put] = back
        return 0

    split_at = inner // LANES
    lax.fori_loop(0, split_at, partial(column, into=grad_values, shift=0), 0)
    lax.fori_loop(
        split_at, width // LANES, partial(column, into=grad_states, shift=split_at), 0
    )

    ahead = lax.broadcasted_iota(jnp.int32, (length, both), 1) < heads
    from_here = triangle(length, lambda r, c: c >= r).astype(BF16)
    to_here = triangle(length, lambda r, c: c <= r).astype(BF16)
    before_here = triangle(length, lambda r, c: c < r).astype(BF16)
    after_here = triangle(length, lambda r, c: c > r).astype(BF16)
    entered = own[0]
    grad_decay = (
        jnp.where(
            ahead,
            exact_sum(from_here, entered) + exact_sum(before_here, leave),
            exact_sum(to_here, entered) + exact_sum(after_here, leave),
        )
        + through * keep[0]
    )
    z = z_in[0]
    step = softplus(z)
    chance = sigmoid(z)
    rates = jnp.exp(jnp.concatenate([decays[0:1, :], decays[1:2, :]], axis=1))
    ratio = jnp.where(step > 1e-30, chance / jnp.maximum(step, 1e-30), 1.0)
    grad_z = (leave + column_sums[0]) * ratio - rates * grad_decay * chance
    grad_raw[0, :EDGE] = jnp.zeros((EDGE, both), F32)
    grad_raw[0, EDGE + length :] = jnp.zeros((EDGE, both), F32)
    grad_raw[0, EDGE : EDGE + length] = grad_z
    smalls[0, EDGE:, :] = jnp.zeros((EDGE, width), F32)
    smalls[0, EDGE : EDGE + 1, :both] = jnp.sum(grad_z, axis=0, keepdims=True)
    smalls[0, EDGE + 1 : EDGE + 2, :both] = -rates * jnp.sum(
        step * grad_decay, axis=0, keepdims=True
    )


def pack_kernel(
    dims, rest, own_states, smalls, side_smalls, grad_stepper, grad_prenorm, packed
):
    _, inner, _, state, reach_cells, _ = dims
    both = grad_stepper.shape[0]
    small = smalls[0]
    side = side_smalls[0]
    for i in range(1, smalls.shape[0]):
        small = small + smalls[i]
        side = side + side_smalls[i]
    at = rest.shape[0]
    packed[:at] = rest[...]
    cut = own_states.shape[0]
    packed[at : at + cut] = own_states[...]
    at += cut
    packed[at:] = jnp.zeros((packed.shape[0] - at, inner), F32)
    packed[at : at + both] = grad_stepper[...]
    at += both
    packed[at : at + EDGE] = small[:EDGE, :inner]
    packed[at + EDGE : at + 2 * EDGE, : 4 * state] = small[:EDGE, inner:]
    packed[at + 2 * EDGE : at + 2 * EDGE + 2, :] = side[:2]
    packed[at + 2 * EDGE + 2 : at + 2 * EDGE + 4, :] = small[EDGE : EDGE + 2, :inner]
    packed[at + 2 * EDGE + 4 : at + 2 * EDGE + 5, :] = grad_prenorm[...]


def unpack_kernel(
    dims,
    mine,
    peer,
    filters,
    shifts,
    kernels,
    biases,
    postnorm,
    direct,
    offsets,
    decays,
    prenorm,
):
    _, inner, heads, state, reach_cells, _ = dims
    head_size = inner // heads
    count = 2 * reach_cells + 1
    at = 2 * state + 2 * heads
    filters[...] = mine[at : at + count]
    shifts[...] = mine[at + count]
    at += EDGE
    shared = mine[at : at + EDGE, : 4 * state] + peer[at : at + EDGE, : 4 * state]
    for k in range(4):
        kernels[:, k, :] = shared[:count, k * state : (k + 1) * state]
        biases[k : k + 1, :] = shared[count:, k * state : (k + 1) * state]
    at += EDGE
    postnorm[...] = mine[at]
    fold = jnp.zeros((EDGE, heads), F32)
    for t in range(inner // WIDE):
        row = jnp.broadcast_to(mine[at + 1 : at + 2, t * WIDE : (t + 1) * WIDE], (EDGE, WIDE))
        fold = fold + dot_bf16(
            jnp.concatenate(split3(row), axis=1),
            gather_heads(t * (WIDE // head_size), head_size, heads, 3),
        )
    direct[...] = fold[0]
    for d in range(2):
        offsets[d : d + 1, :] = mine[at + 2 : at + 3, d * heads : (d + 1) * heads]
        decays[d : d + 1, :] = mine[at + 3 : at + 4, d * heads : (d + 1) * heads]
    prenorm[...] = mine[at + 4] + peer[at + 4]


def exchange(x, axis, bit):
    peers = lax.axis_size(axis)
    return lax.ppermute(x, axis, [(i, i ^ (1 << bit)) for i in range(peers)])


def bit_of(place, bit):
    return (place >> bit) & 1


def join_halves(mine, own, other):
    return jnp.where(
        mine == 0, jnp.concatenate([own, other]), jnp.concatenate([other, own])
    )


def tie(*arrays):
    return lax.optimization_barrier(arrays)


class PairTotal:
    def __init__(self, axis):
        self.axis = axis
        self.place = lax.axis_index(axis)
        bits = lax.axis_size(axis).bit_length() - 1
        down = [(0, 1), (1, 0), (2,)] + [(bit,) for bit in range(3, bits)]
        self.steps = [("halve", order) for order in down]
        self.steps += [("join", order) for order in reversed(down)]
        self.at = 0
        self.now = [None, None]
        self.came = [None, None]

    def mine(self, bit):
        return bit_of(self.place, bit)

    def outgoing(self, k=None):
        kind, order = self.steps[self.at]
        which = range(len(order)) if k is None else (k,)
        out = []
        for i in which:
            x, mine = self.now[i], self.mine(order[i])
            if kind == "join":
                out.append(x)
            elif order == (2,):
                out.append(jnp.where(mine == 0, self.now[1], self.now[0]))
            else:
                half = x.shape[0] // 2
                out.append(lax.dynamic_slice_in_dim(x, (1 - mine) * half, half))
        return out

    def go(self, sent, k=None):
        _, order = self.steps[self.at]
        which = range(len(order)) if k is None else (k,)
        for i, x in zip(which, sent):
            self.came[i] = exchange(x, self.axis, order[i])

    def take(self, *others):
        kind, order = self.steps[self.at]
        came = [c for c in self.came[: len(order)]]
        if others:
            came = list(tie(*came, *others)[: len(order)])
        now = []
        for i, bit in enumerate(order):
            x, mine, c = self.now[i], self.mine(bit), came[i]
            if order == (2,):
                if kind == "halve":
                    now = [jnp.where(mine == 0, self.now[0], self.now[1]) + c]
                else:
                    now = [jnp.where(mine == 0, x, c), jnp.where(mine == 0, c, x)]
            elif kind == "halve":
                half = x.shape[0] // 2
                now.append(lax.dynamic_slice_in_dim(x, mine * half, half) + c)
            else:
                now.append(join_halves(mine, x, c))
        self.now = now
        self.at += 1

    def ahead_of(self, array, k=None):
        sent = self.outgoing(k)
        self.go(sent, k)
        return tie(array, *sent)[0]

    @property
    def done(self):
        return self.at == len(self.steps)

    def turn(self, *others):
        if self.done:
            return self.now[0]
        self.take(*others)
        if not self.done:
            sent = self.outgoing()
            self.go(sent)
            return sent[0]
        return self.now[0]


def local(
    hidden,
    lengths,
    prenorm,
    gating,
    values,
    states,
    stepper,
    offsets,
    decays,
    filters,
    shifts,
    kernels,
    biases,
    direct,
    postnorm,
    output,
    cotangent,
):
    micro, length, model = hidden.shape
    inner = gating.shape[1]
    heads = direct.shape[0]
    both = 2 * heads
    head_size = inner // heads
    state = states.shape[2]
    reach_cells = (filters.shape[0] - 1) // 2
    count = 2 * reach_cells + 1
    peers = lax.axis_size("seq")
    place = lax.axis_index("seq")
    head_place = lax.axis_index("head")
    inner_all = inner * lax.axis_size("head")
    rows = micro * 2 * state // peers
    tiles = inner // LANES
    dims = (length, inner, heads, state, reach_cells, rows)
    maps_width = 4 * state
    width = inner + maps_width
    long = length + 2 * EDGE
    half_peers = peers // micro
    where = place.reshape(1).astype(jnp.int32)

    up = [(i, i + 1) for i in range(peers - 1)]
    down = [(i + 1, i) for i in range(peers - 1)]
    swap = [(0, 1), (1, 0)]
    before = lax.ppermute(hidden[:, length - EDGE :], "seq", up)
    after = lax.ppermute(hidden[:, :EDGE], "seq", down)
    states_flat = states.reshape(model, maps_width)
    stepper_flat = stepper.reshape(model, both)
    direct_row = jnp.repeat(direct, head_size)[None]
    post_row = postnorm[None]

    def spec(*block):
        return pl.BlockSpec((1,) + block, lambda i: (i,) + (0,) * len(block))

    def fixed(*block):
        return pl.BlockSpec(block, lambda i: (0,) * len(block))

    def shape(*dims):
        return jax.ShapeDtypeStruct(dims, F32)

    smem = pl.BlockSpec(memory_space=pltpu.SMEM)
    vmem = pl.BlockSpec(memory_space=pltpu.VMEM)
    packed = tiles * rows + EDGE
    pay_spec = pl.BlockSpec((half_peers, packed, LANES), lambda i: (i, 0, 0))
    plain_spec = pl.BlockSpec((half_peers, tiles * rows, LANES), lambda i: (i, 0, 0))
    small = spec(length, both)
    wide = spec(length, inner)
    acts = spec(length, width)
    row = fixed(1, inner)
    flat = spec(both, length)

    (
        normed,
        mixed,
        conv,
        act,
        maps_t,
        z,
        run,
        late,
        run_rows,
        late_rows,
        reach,
        tail,
        keep,
        taps,
        pay,
    ) = pl.pallas_call(
        partial(front_kernel, dims),
        grid=(micro,),
        in_specs=[
            smem,
            smem,
            spec(EDGE, model),
            spec(length, model),
            spec(EDGE, model),
            fixed(1, model),
            fixed(model, inner),
            fixed(model, maps_width),
            fixed(model, both),
            fixed(count, inner),
            fixed(count, 4, state),
            fixed(1, inner),
            fixed(4, state),
            fixed(2, heads),
            fixed(2, heads),
        ],
        out_specs=[
            spec(long, model),
            spec(long, width),
            acts,
            acts,
            spec(maps_width, length),
            small,
            small,
            small,
            flat,
            flat,
            small,
            small,
            spec(1, both),
            fixed(EDGE, width),
            pay_spec,
        ],
        out_shape=[
            shape(micro, long, model),
            shape(micro, long, width),
            shape(micro, length, width),
            shape(micro, length, width),
            shape(micro, maps_width, length),
            shape(micro, length, both),
            shape(micro, length, both),
            shape(micro, length, both),
            shape(micro, both, length),
            shape(micro, both, length),
            shape(micro, length, both),
            shape(micro, length, both),
            shape(micro, 1, both),
            shape(EDGE, width),
            shape(peers, packed, LANES),
        ],
        scratch_shapes=[
            pltpu.VMEM((long + 2 * EDGE, LANES), jnp.int32),
            pltpu.VMEM((count, length, LANES), F32),
        ],
        compiler_params=PARAMS,
        name="front",
    )(
        where,
        lengths,
        before,
        hidden,
        after,
        prenorm[None],
        values,
        states_flat,
        stepper_flat,
        filters,
        kernels,
        shifts[None],
        biases,
        offsets,
        decays,
    )

    direction = lax.rem(place // (peers // (2 * micro)), 2)

    def prefix(terms, keeps, flipped):
        return pl.pallas_call(
            partial(prefix_kernel, tiles, rows),
            grid=(1,),
            in_specs=[smem, fixed(*terms.shape), fixed(*keeps.shape)],
            out_specs=fixed(peers, tiles * rows, LANES),
            out_shape=shape(peers, tiles * rows, LANES),
            compiler_params=PARAMS,
            name="prefix",
        )(flipped.reshape(1).astype(jnp.int32), terms, keeps)

    def swap_all(x):
        return lax.all_to_all(x, "seq", 0, 0, tiled=True)

    terms = swap_all(pay)
    arrived = swap_all(prefix(terms, terms, direction))

    normed_flat = normed.reshape(micro * long, model)
    cotangent_flat = cotangent.reshape(micro * length, model)
    back = dot(cotangent_flat, output, 1, 1).reshape(micro, length, inner)
    inside = pl.pallas_call(
        partial(inside_kernel, dims),
        grid=(micro,),
        in_specs=[smem, smem, acts, small, flat],
        out_specs=wide,
        out_shape=shape(micro, length, inner),
        compiler_params=PARAMS,
        name="inside",
    )(where, lengths, act, run, late_rows)
    gate = dot(normed_flat, gating).reshape(micro, long, inner)

    gates = spec(long, inner)
    sum_spec = spec(length, LANES)
    state_spec = spec(2, state, inner)
    mixed_y, sums, before_states = pl.pallas_call(
        partial(join_kernel, dims),
        grid=(micro,),
        in_specs=[wide, plain_spec, acts, small, gates, wide, row, row],
        out_specs=[wide, sum_spec, state_spec],
        out_shape=[
            shape(micro, length, inner),
            shape(micro, length, LANES),
            shape(micro, 2, state, inner),
        ],
        compiler_params=PARAMS,
        name="join",
    )(inside, arrived, act, reach, gate, back, direct_row, post_row)
    peer_sums = lax.ppermute(sums, "head", swap)

    grad_y, normal, pay_back = pl.pallas_call(
        partial(turn_kernel, dims, inner_all),
        grid=(micro,),
        in_specs=[
            sum_spec,
            sum_spec,
            wide,
            gates,
            wide,
            spec(maps_width, length),
            small,
            row,
        ],
        out_specs=[wide, wide, plain_spec],
        out_shape=[
            shape(micro, length, inner),
            shape(micro, length, inner),
            shape(peers, tiles * rows, LANES),
        ],
        compiler_params=PARAMS,
        name="turn",
    )(sums, peer_sums, mixed_y, gate, back, maps_t, reach, post_row)

    back_terms = swap_all(pay_back)

    normal_flat = normal.reshape(micro * length, inner)
    grad_output = dot(normal_flat, cotangent_flat, 0, 0)

    grad_gate, side_smalls = pl.pallas_call(
        partial(side_kernel, dims, inner_all),
        grid=(micro,),
        in_specs=[sum_spec, sum_spec, wide, gates, wide, acts, wide, row],
        out_specs=[gates, spec(EDGE, inner)],
        out_shape=[shape(micro, long, inner), shape(micro, EDGE, inner)],
        compiler_params=PARAMS,
        name="side",
    )(sums, peer_sums, mixed_y, gate, back, act, grad_y, post_row)
    grad_gate_flat = grad_gate.reshape(micro * long, inner)
    grad_gating = dot(normed_flat, grad_gate_flat, 0, 0)
    early = PairTotal("seq")
    early.now = [grad_output, grad_gating]
    back_terms = early.ahead_of(back_terms)
    prefixed = prefix(back_terms, terms, 1 - direction)
    back_arrived = swap_all(prefixed)
    grad_y = tie(grad_y, prefixed)[0]

    grad_inside, grad_maps, own, column_sums = pl.pallas_call(
        partial(inside_back_kernel, dims),
        grid=(micro,),
        in_specs=[smem, smem, acts, wide, small, flat, small, state_spec, row],
        out_specs=[wide, spec(length, maps_width), small, small],
        out_shape=[
            shape(micro, length, inner),
            shape(micro, length, maps_width),
            shape(micro, length, both),
            shape(micro, length, both),
        ],
        scratch_shapes=[pltpu.VMEM((both, length), F32)],
        compiler_params=PARAMS,
        name="inside_back",
    )(where, lengths, act, grad_y, late, run_rows, reach, before_states, direct_row)

    grad_normed_gate = dot(grad_gate_flat, gating, 1, 1)
    early.take(own, grad_normed_gate)
    normal_flat = early.ahead_of(normal_flat)
    projected = dot(normal_flat, output)
    result = hidden + (projected + lax.ppermute(projected, "head", swap)).reshape(hidden.shape)
    back_arrived = tie(back_arrived, projected)[0]

    grad_mixed, grad_mixed_maps, grad_raw, smalls = pl.pallas_call(
        partial(end_kernel, dims),
        grid=(micro,),
        in_specs=[
            smem,
            smem,
            plain_spec,
            acts,
            small,
            small,
            acts,
            state_spec,
            spec(1, both),
            wide,
            spec(length, maps_width),
            small,
            small,
            spec(long, width),
            fixed(EDGE, width),
            fixed(2, heads),
        ],
        out_specs=[gates, spec(long, maps_width), spec(long, both), spec(2 * EDGE, width)],
        out_shape=[
            shape(micro, long, inner),
            shape(micro, long, maps_width),
            shape(micro, long, both),
            shape(micro, 2 * EDGE, width),
        ],
        scratch_shapes=[
            pltpu.VMEM((2, state, inner), F32),
            pltpu.VMEM((length, width), F32),
            pltpu.VMEM((long, LANES), F32),
            pltpu.VMEM((long + 2 * EDGE, LANES), jnp.int32),
            pltpu.VMEM((count, length + 2 * reach_cells, LANES), F32),
        ],
        compiler_params=PARAMS,
        name="end",
    )(
        where,
        lengths,
        back_arrived,
        act,
        z,
        tail,
        conv,
        before_states,
        keep,
        grad_inside,
        grad_maps,
        own,
        column_sums,
        mixed,
        taps,
        decays,
    )
    all_maps = grad_mixed_maps.reshape(micro * long, maps_width)
    all_maps = all_maps + lax.ppermute(all_maps, "head", swap)

    early.take(grad_raw)
    grad_mixed = early.ahead_of(grad_mixed)
    grad_mixed = grad_mixed.reshape(micro * long, inner)
    grad_mixed_maps = grad_mixed_maps.reshape(micro * long, maps_width)
    grad_raw = grad_raw.reshape(micro * long, both)
    cut = maps_width // 2
    most = (model + cut + cut) // 2
    late_total = PairTotal("seq")
    late_total.now = [dot(normed_flat[:, :most], grad_mixed, 0, 0), None]
    normed_flat = late_total.ahead_of(normed_flat, 0)
    grad_normed = (
        dot(grad_mixed, values, 1, 1)
        + dot(grad_mixed_maps, states_flat, 1, 1)
        + grad_normed_gate
        + dot(grad_raw, stepper_flat, 1, 1)
    )
    grad_prenorm = jnp.sum(grad_normed * normed_flat, axis=0, keepdims=True) / prenorm[None]
    own_maps = lax.dynamic_slice_in_dim(all_maps, head_place * cut, cut, 1)
    second_late = pl.pallas_call(
        partial(pack_kernel, dims),
        in_specs=[vmem] * 6,
        out_specs=vmem,
        out_shape=shape(most, inner),
        compiler_params=PARAMS,
        name="pack",
    )(
        dot(normed_flat[:, most:], grad_mixed, 0, 0),
        dot(own_maps, normed_flat, 0, 0),
        smalls,
        side_smalls,
        dot(grad_raw, normed_flat, 0, 0),
        grad_prenorm,
    )
    late_total.now[1] = second_late
    grad_normed = late_total.ahead_of(grad_normed, 1)

    grad_normed = grad_normed.reshape(micro, long, model)
    grad_normed = grad_normed + lax.ppermute(grad_normed, "head", swap)
    from_after = lax.ppermute(grad_normed[:, :EDGE], "seq", down)
    from_before = lax.ppermute(grad_normed[:, EDGE + length :], "seq", up)
    grad_here = grad_normed[:, EDGE : EDGE + length] + jnp.concatenate(
        [from_before, jnp.zeros((micro, length - 2 * EDGE, model), F32), from_after], axis=1
    )
    scale = lax.rsqrt(jnp.mean(hidden * hidden, axis=2, keepdims=True) + EPSILON)
    pulled = grad_here * prenorm
    grad_hidden = (
        cotangent
        + scale * pulled
        - hidden * (scale**3 * jnp.sum(pulled * hidden, axis=2, keepdims=True) / model)
    )

    held = early.turn(second_late)
    held = late_total.turn(held)
    held = early.turn(held, grad_hidden)
    while not late_total.done:
        held = late_total.turn(held)
        held = early.turn(held)
    late_done = late_total.now
    grad_output, grad_gating = early.now
    last = late_done[1][model - most :]
    peer_last = lax.ppermute(last, "head", swap)
    own_states, other_states = last[:cut], peer_last[:cut]
    grad_states = jnp.where(
        head_place == 0,
        jnp.concatenate([own_states, other_states]),
        jnp.concatenate([other_states, own_states]),
    ).T.reshape(states.shape)
    grad_stepper = last[cut : cut + both].T.reshape(stepper.shape)
    (
        grad_filters,
        grad_shifts,
        grad_kernels,
        grad_biases,
        grad_postnorm,
        grad_direct,
        grad_offsets,
        grad_decays,
        grad_prenorm,
    ) = pl.pallas_call(
        partial(unpack_kernel, dims),
        in_specs=[vmem, vmem],
        out_specs=[vmem] * 9,
        out_shape=[
            shape(count, inner),
            shape(inner),
            shape(*kernels.shape),
            shape(*biases.shape),
            shape(inner),
            shape(heads),
            shape(*offsets.shape),
            shape(*decays.shape),
            shape(model),
        ],
        compiler_params=PARAMS,
        name="unpack",
    )(last, peer_last)
    late_done = jnp.concatenate([late_done[0], late_done[1][: model - most]], axis=0)
    return (
        result,
        grad_hidden,
        grad_prenorm,
        grad_gating,
        late_done,
        grad_states,
        grad_stepper,
        grad_offsets,
        grad_decays,
        grad_filters,
        grad_shifts,
        grad_kernels,
        grad_biases,
        grad_direct,
        grad_postnorm,
        grad_output,
    )


def solution(mesh):
    in_specs = (
        P(None, "seq", None),
        P(),
        P(),
        P(None, "head"),
        P(None, "head"),
        P(),
        P(None, None, "head"),
        P(None, "head"),
        P(None, "head"),
        P(None, "head"),
        P("head"),
        P(),
        P(),
        P("head"),
        P("head"),
        P("head", None),
        P(None, "seq", None),
    )
    out_specs = (
        P(None, "seq", None),
        P(None, "seq", None),
        P(),
        P(None, "head"),
        P(None, "head"),
        P(),
        P(None, None, "head"),
        P(None, "head"),
        P(None, "head"),
        P(None, "head"),
        P("head"),
        P(),
        P(),
        P("head"),
        P("head"),
        P("head", None),
    )
    return jax.shard_map(local, mesh=mesh, in_specs=in_specs, out_specs=out_specs, check_vma=False)
```

```python
from functools import partial

import jax
import jax.numpy as jnp
from jax import lax
from jax.experimental import pallas as pl
from jax.experimental.pallas import tpu as pltpu
from jax.sharding import PartitionSpec as P

EPSILON = 1e-05
HIGH = lax.Precision.HIGH
F32 = jnp.float32
BF16 = jnp.bfloat16
LANES = 128
WIDE = 256
CHUNK = 128
EDGE = 8
PARAMS = pltpu.CompilerParams(vmem_limit_bytes=56 * 1024 * 1024)


def dot(left, right, over_left=1, over_right=0, precision=HIGH):
    return lax.dot_general(
        left,
        right,
        (((over_left,), (over_right,)), ((), ())),
        precision=precision,
        preferred_element_type=F32,
    )


def split(x):
    top = x.astype(BF16)
    return top, (x - top.astype(F32)).astype(BF16)


def dot_bf16(left, right, over_left=1, over_right=0):
    return lax.dot_general(
        left,
        right,
        (((over_left,), (over_right,)), ((), ())),
        preferred_element_type=F32,
    )


def spread(first, head_size, both):
    rows = lax.broadcasted_iota(jnp.int32, (2 * both, WIDE), 0)
    columns = lax.broadcasted_iota(jnp.int32, (2 * both, WIDE), 1)
    return (lax.rem(rows, both) == first + columns // head_size).astype(BF16)


def gather_heads(first, head_size, both, parts=2):
    rows = lax.broadcasted_iota(jnp.int32, (parts * WIDE, both), 0)
    columns = lax.broadcasted_iota(jnp.int32, (parts * WIDE, both), 1)
    return (columns == first + lax.rem(rows, WIDE) // head_size).astype(BF16)


def split3(x):
    top = x.astype(BF16)
    rest = x - top.astype(F32)
    middle = rest.astype(BF16)
    return top, middle, (rest - middle.astype(F32)).astype(BF16)


def halves(x):
    return jnp.concatenate(split(x), axis=1)


def triangle(size, keep):
    rows = lax.broadcasted_iota(jnp.int32, (size, size), 0)
    columns = lax.broadcasted_iota(jnp.int32, (size, size), 1)
    return keep(rows, columns)


def exact_sum(zero_one, x):
    a, b, c = split3(x)
    return dot_bf16(zero_one, a) + dot_bf16(zero_one, b) + dot_bf16(zero_one, c)


def flip(x):
    size = x.shape[1]
    one = triangle(size, lambda r, c: r == c).astype(BF16)
    a, b, c = split3(x)
    return dot_bf16(one, a, 1, 1) + dot_bf16(one, b, 1, 1) + dot_bf16(one, c, 1, 1)


def sigmoid(x):
    return 1.0 / (1.0 + jnp.exp(-x))


def softplus(x):
    return jnp.maximum(x, 0.0) + jnp.log1p(jnp.exp(-jnp.abs(x)))


def bounds_of(lengths, i):
    ends = []
    total = jnp.int32(0)
    for k in range(lengths.shape[1]):
        total = total + lengths[i, k]
        ends.append(total)
    return ends


def document(places, ends):
    found = sum(jnp.where(places >= end, 1, 0) for end in ends)
    return jnp.where(places < 0, -1, jnp.where(places >= ends[-1], -2, found))


def same_document(first, ends, length):
    rows = document(first + lax.broadcasted_iota(jnp.int32, (length, LANES), 0), ends)
    columns = document(first + lax.broadcasted_iota(jnp.int32, (1, length), 1), ends)
    return jnp.concatenate([rows] * (length // LANES), axis=1) == columns


def fill_masks(masks, documents, first, ends, start, rows, reach_cells):
    total = documents.shape[0]
    documents[...] = document(
        first - 2 * EDGE + lax.broadcasted_iota(jnp.int32, (total, LANES), 0), ends
    )
    center = documents[EDGE + start : EDGE + start + rows]
    for o in range(2 * reach_cells + 1):
        at = EDGE + start + o - reach_cells
        masks[o] = (documents[at : at + rows] == center).astype(F32)


def left3(x):
    top = x.astype(BF16).astype(F32)
    return jnp.concatenate([top, top, x - top], axis=1).astype(BF16)


def right3(x):
    top, low = split(x)
    return jnp.concatenate([top, low, top], axis=0)


def stacked(x):
    return jnp.concatenate(split(x), axis=0)


def front_kernel(
    dims,
    place,
    lengths,
    before,
    hidden,
    after,
    prenorm,
    values,
    states,
    stepper,
    filters,
    kernels,
    shifts,
    biases,
    offsets,
    decays,
    normed,
    mixed,
    conv,
    act,
    maps_t,
    z_out,
    run,
    late,
    run_rows,
    late_rows,
    reach,
    tail,
    keep,
    taps,
    pay,
    documents,
    masks,
):
    length, inner, heads, state, reach_cells, rows = dims
    head_size = inner // heads
    both = 2 * heads
    maps_width = 4 * state
    width = inner + maps_width
    offsets_count = 2 * reach_cells + 1
    i = pl.program_id(0)
    ends = bounds_of(lengths, i)
    first = place[0] * length
    fill_masks(masks, documents, first, ends, EDGE, length, reach_cells)

    gain = prenorm[...]

    def norm(x):
        mean = jnp.sum(x * x, axis=1, keepdims=True) / x.shape[1]
        return x * lax.rsqrt(mean + EPSILON) * gain

    normed[0, :EDGE] = norm(before[0])
    for r in range(0, length, 64):
        normed[0, EDGE + r : EDGE + r + 64] = norm(hidden[0, r : r + 64])
    normed[0, EDGE + length :] = norm(after[0])

    whole = normed[0]
    for t in range(inner // WIDE):
        at = slice(t * WIDE, (t + 1) * WIDE)
        mixed[0, :, at] = dot(whole, values[:, at])
    mixed[0, :, inner:] = dot(whole, states[...])
    raw = dot(normed[0, EDGE : EDGE + length], stepper[...])

    taps[:offsets_count, :inner] = filters[...]
    taps[offsets_count:, :inner] = shifts[...]
    for k in range(4):
        at = slice(inner + k * state, inner + (k + 1) * state)
        taps[:offsets_count, at] = kernels[:, k, :]
        taps[offsets_count:, at] = biases[k : k + 1, :]

    for t in range(width // WIDE):
        at = slice(t * WIDE, (t + 1) * WIDE)
        for r in range(0, length, CHUNK):
            total = jnp.broadcast_to(taps[offsets_count:, at], (CHUNK, WIDE))
            for o in range(offsets_count):
                begin = EDGE - reach_cells + o + r
                mask = masks[o, r : r + CHUNK]
                total = total + (mixed[0, begin : begin + CHUNK, at] * taps[o : o + 1, at]) * (
                    jnp.concatenate([mask] * (WIDE // LANES), axis=1)
                )
            conv[0, r : r + CHUNK, at] = total
            act[0, r : r + CHUNK, at] = total * sigmoid(total)
    flipped = jnp.transpose(act[0, :, inner:])
    maps_t[0] = flipped

    ahead = lax.broadcasted_iota(jnp.int32, (length, both), 1) < heads
    ahead_row = ahead[:1]
    z = raw + jnp.concatenate([offsets[0:1, :], offsets[1:2, :]], axis=1)
    rates = jnp.exp(jnp.concatenate([decays[0:1, :], decays[1:2, :]], axis=1))
    step = softplus(z)
    decay = -step * rates
    lower = triangle(length, lambda r, c: r >= c).astype(BF16)
    upper = triangle(length, lambda r, c: r <= c).astype(BF16)
    running = jnp.where(ahead, exact_sum(lower, decay), exact_sum(upper, decay))
    edge = jnp.where(ahead_row, running[length - 1 :], running[:1])
    here = document(first + lax.broadcasted_iota(jnp.int32, (length, both), 0), ends)
    seg_before = document(first - 1, ends)
    seg_after = document(first + length, ends)
    seg_first = document(first, ends)
    seg_last = document(first + length - 1, ends)
    enter = (here == jnp.where(ahead, seg_before, seg_after)).astype(F32)
    leave = (here == jnp.where(ahead, seg_last, seg_first)).astype(F32)
    keep_mask = jnp.where(
        ahead_row,
        jnp.where(seg_last == seg_before, 1.0, 0.0),
        jnp.where(seg_first == seg_after, 1.0, 0.0),
    )
    reach_now = enter * jnp.exp(running)
    tail_now = leave * jnp.exp(edge - running) * step
    keep_now = keep_mask * jnp.exp(edge)
    late_now = running - jnp.log(jnp.maximum(step, 1e-37))
    z_out[0] = z
    run[0] = running
    late[0] = late_now
    reach[0] = reach_now
    tail[0] = tail_now
    run_rows[0] = flip(running)
    late_rows[0] = flip(late_now)
    keep[0] = keep_now

    tail_halves = halves(tail_now)
    keep_halves = halves(jnp.broadcast_to(keep_now, (EDGE, both)))
    pieces = state // rows
    per_tile = WIDE // head_size
    for d in range(2):
        maps_now = stacked(flipped[2 * d * state : (2 * d + 1) * state])
        keeps = []
        for t in range(inner // WIDE):
            grow = spread(d * heads + t * per_tile, head_size, both)
            weighted = act[0, :, t * WIDE : (t + 1) * WIDE] * dot_bf16(tail_halves, grow)
            put_states(pay, d, t, product_of_stack(maps_now, weighted, state), pieces, rows)
            keep_wide = dot_bf16(keep_halves, grow)[:1]
            keeps += [keep_wide[:, k * LANES : (k + 1) * LANES] for k in range(WIDE // LANES)]
        tiles = inner // LANES
        keeps.append(jnp.zeros((EDGE - tiles, LANES), F32))
        keep_block = jnp.concatenate(keeps, axis=0)
        for j in range(pieces):
            pay[d * pieces + j, tiles * rows :, :] = keep_block


def product_of_stack(stack, x, size):
    top, low = split(x)
    twice = dot_bf16(stack, top)
    return twice[:size] + twice[size:] + dot_bf16(stack[:size], low)


def put_states(pay, d, t, own, pieces, rows):
    for k in range(WIDE // LANES):
        at = (t * (WIDE // LANES) + k) * rows
        for j in range(pieces):
            pay[d * pieces + j, at : at + rows, :] = own[
                j * rows : (j + 1) * rows, k * LANES : (k + 1) * LANES
            ]


def prefix_kernel(tiles, rows, flipped, terms, keeps, into):
    peers = terms.shape[0]
    back = flipped[0] != 0

    def turn(i, carry):
        at = jnp.where(back, peers - 1 - i, i)
        factor = keeps[at, tiles * rows :, :]
        new = []
        for t in range(tiles):
            into[at, t * rows : (t + 1) * rows, :] = carry[t]
            new.append(
                carry[t] * factor[t : t + 1] + terms[at, t * rows : (t + 1) * rows, :]
            )
        return tuple(new)

    lax.fori_loop(0, peers, turn, tuple(jnp.zeros((rows, LANES), F32) for _ in range(tiles)))


def scores_of(act, ends, first, inner, state, length):
    def part(k):
        return act[0, :, inner + k * state : inner + (k + 1) * state]

    same = same_document(first, ends, length)
    below = triangle(length, lambda r, c: r > c)
    above = triangle(length, lambda r, c: r < c)
    return part, same, below, above


def inside_kernel(dims, place, lengths, act, run, late_rows, inside):
    length, inner, heads, state, _, _ = dims
    head_size = inner // heads
    per_tile = LANES // head_size
    ends = bounds_of(lengths, pl.program_id(0))
    part, same, below, above = scores_of(act, ends, place[0] * length, inner, state, length)
    scores = jnp.where(below & same, dot(part(1), part(0), 1, 1), 0.0) + jnp.where(
        above & same, dot(part(3), part(2), 1, 1), 0.0
    )
    run_at = run[0]
    lane = lax.broadcasted_iota(jnp.int32, (length, LANES), 1) // head_size
    for t in range(inner // LANES):
        top, low = split(act[0, :, t * LANES : (t + 1) * LANES])
        pair = jnp.concatenate([top, low], axis=1)
        total = jnp.zeros((length, LANES), F32)
        for k in range(per_tile):
            h = t * per_tile + k
            weights = jnp.exp(
                jnp.where(
                    below,
                    run_at[:, h : h + 1] - late_rows[0, h : h + 1, :],
                    run_at[:, heads + h : heads + h + 1]
                    - late_rows[0, heads + h : heads + h + 1, :],
                )
            )
            m_top, m_low = split(scores * weights)
            wide = dot_bf16(m_top, pair)
            now = wide[:, :LANES] + wide[:, LANES:] + dot_bf16(m_low, top)
            total = jnp.where(lane == k, now, total)
        inside[0, :, t * LANES : (t + 1) * LANES] = total


def unpack(pay, into, tiles, rows, state):
    pieces = state // rows
    for d in range(2):
        for j in range(pieces):
            for t in range(tiles):
                into[d, j * rows : (j + 1) * rows, t * LANES : (t + 1) * LANES] = pay[
                    d * pieces + j, t * rows : (t + 1) * rows, :
                ]


def join_kernel(
    dims, inside, pay, act, reach, gate, back, direct, postnorm, mixed_y, sums, states
):
    length, inner, heads, state, _, rows = dims
    head_size = inner // heads
    both = 2 * heads
    per_tile = WIDE // head_size
    unpack(pay, states.at[0], inner // LANES, rows, state)
    reach_halves = halves(reach[0])
    readers = [left3(act[0, :, inner + k * state : inner + (k + 1) * state]) for k in (1, 3)]
    squares = jnp.zeros((length, WIDE), F32)
    crossed = jnp.zeros((length, WIDE), F32)
    for t in range(inner // WIDE):
        at = slice(t * WIDE, (t + 1) * WIDE)
        total = inside[0, :, at] + direct[:, at] * act[0, :, at]
        for d in range(2):
            grow = spread(d * heads + t * per_tile, head_size, both)
            total = total + dot_bf16(readers[d], right3(states[0, d, :, at])) * dot_bf16(
                reach_halves, grow
            )
        mixed_y[0, :, at] = total
        gate_now = gate[0, EDGE : EDGE + length, at]
        gated = total * (gate_now * sigmoid(gate_now))
        squares = squares + gated * gated
        crossed = crossed + gated * postnorm[:, at] * back[0, :, at]
    lane = lax.broadcasted_iota(jnp.int32, (length, LANES), 1)
    sums[0] = jnp.where(
        lane == 0,
        jnp.sum(squares, axis=1, keepdims=True),
        jnp.sum(crossed, axis=1, keepdims=True),
    )


def norm_of(sums, peer_sums, inner_all, length):
    both_sums = sums[0] + peer_sums[0]
    q = lax.rsqrt(both_sums[:, 0:1] / inner_all + EPSILON)
    pull = both_sums[:, 1:2] * (q * q * q) / inner_all
    return (
        jnp.broadcast_to(q, (length, LANES)),
        jnp.broadcast_to(pull, (length, LANES)),
    )


def turn_kernel(
    dims,
    inner_all,
    sums,
    peer_sums,
    mixed_y,
    gate,
    back,
    maps_t,
    reach,
    postnorm,
    grad_y,
    normal,
    pay,
):
    length, inner, heads, state, _, rows = dims
    head_size = inner // heads
    both = 2 * heads
    per_tile = WIDE // head_size
    pieces = state // rows
    q, pull = norm_of(sums, peer_sums, inner_all, length)
    reach_halves = halves(reach[0])
    readers = [stacked(maps_t[0, k * state : (k + 1) * state]) for k in (1, 3)]
    for t in range(inner // WIDE):
        upstreams = []
        for k in range(WIDE // LANES):
            at = slice(t * WIDE + k * LANES, t * WIDE + (k + 1) * LANES)
            gate_now = gate[0, EDGE : EDGE + length, at]
            opened = gate_now * sigmoid(gate_now)
            gated = mixed_y[0, :, at] * opened
            post = postnorm[:, at]
            upstream = (q * back[0, :, at] * post - pull * gated) * opened
            grad_y[0, :, at] = upstream
            normal[0, :, at] = gated * post * q
            upstreams.append(upstream)
        upstream = jnp.concatenate(upstreams, axis=1)
        for d in range(2):
            grow = spread(d * heads + t * per_tile, head_size, both)
            seed = product_of_stack(readers[d], upstream * dot_bf16(reach_halves, grow), state)
            put_states(pay, d, t, seed, pieces, rows)


def side_kernel(
    dims,
    inner_all,
    sums,
    peer_sums,
    mixed_y,
    gate,
    back,
    act,
    grad_y,
    postnorm,
    grad_gate,
    smalls,
):
    length, inner, heads, _, _, _ = dims
    q, pull = norm_of(sums, peer_sums, inner_all, length)
    grad_gate[0, :EDGE] = jnp.zeros((EDGE, inner), F32)
    grad_gate[0, EDGE + length :] = jnp.zeros((EDGE, inner), F32)
    smalls[0] = jnp.zeros((EDGE, inner), F32)
    for t in range(inner // LANES):
        at = slice(t * LANES, (t + 1) * LANES)
        y = mixed_y[0, :, at]
        gate_now = gate[0, EDGE : EDGE + length, at]
        chance = sigmoid(gate_now)
        gated = y * (gate_now * chance)
        scaled = q * back[0, :, at]
        grad_gated = scaled * postnorm[:, at] - pull * gated
        grad_gate[0, EDGE : EDGE + length, at] = (
            grad_gated * y * (chance * (1.0 + gate_now * (1.0 - chance)))
        )
        smalls[0, 0:1, at] = jnp.sum(scaled * gated, axis=0, keepdims=True)
        smalls[0, 1:2, at] = jnp.sum(grad_y[0, :, at] * act[0, :, at], axis=0, keepdims=True)


def inside_back_kernel(
    dims,
    place,
    lengths,
    act,
    grad_y,
    late,
    run_rows,
    reach,
    states,
    direct,
    grad_signal,
    grad_maps,
    own,
    column_sums,
    read_parts,
):
    length, inner, heads, state, _, _ = dims
    head_size = inner // heads
    per_tile = LANES // head_size
    both = 2 * heads
    ends = bounds_of(lengths, pl.program_id(0))
    part, same, below, above = scores_of(act, ends, place[0] * length, inner, state, length)
    scores = jnp.where(above & same, dot(part(0), part(1), 1, 1), 0.0) + jnp.where(
        below & same, dot(part(2), part(3), 1, 1), 0.0
    )
    late_at = late[0]
    lane = lax.broadcasted_iota(jnp.int32, (length, LANES), 1)
    write_sums = jnp.zeros((length, LANES), F32)
    grad_scores = jnp.zeros((length, length), F32)
    zero = jnp.zeros((length, LANES), BF16)
    for t in range(inner // LANES):
        at = slice(t * LANES, (t + 1) * LANES)
        s_top, s_low = split(act[0, :, at])
        g_top, g_low = split(grad_y[0, :, at])
        pair = jnp.concatenate([g_top, g_low], axis=1)
        two = jnp.concatenate([g_top, g_top], axis=1)
        total = jnp.zeros((length, LANES), F32)
        for k in range(per_tile):
            h = t * per_tile + k
            weights = jnp.exp(
                jnp.where(
                    above,
                    run_rows[0, h : h + 1, :] - late_at[:, h : h + 1],
                    run_rows[0, heads + h : heads + h + 1, :]
                    - late_at[:, heads + h : heads + h + 1],
                )
            )
            mine = lane // head_size == k
            i_top = jnp.where(mine, s_top, zero)
            i_low = jnp.where(mine, s_low, zero)
            overlap = dot_bf16(jnp.concatenate([i_top, i_low], axis=1), two, 1, 1) + dot_bf16(
                i_top, g_low, 1, 1
            )
            product = weights * overlap
            grad_scores = grad_scores + product
            whole = product * scores
            ahead = jnp.where(above, whole, 0.0)
            ahead_writes = jnp.sum(ahead, axis=1, keepdims=True)
            all_writes = jnp.sum(whole, axis=1, keepdims=True)
            write_sums = jnp.where(lane == h, ahead_writes, write_sums)
            write_sums = jnp.where(lane == heads + h, all_writes - ahead_writes, write_sums)
            ahead_reads = jnp.sum(ahead, axis=0, keepdims=True)
            read_parts[h : h + 1, :] = ahead_reads
            read_parts[heads + h : heads + h + 1, :] = (
                jnp.sum(whole, axis=0, keepdims=True) - ahead_reads
            )
            m_top, m_low = split(scores * weights)
            wide = dot_bf16(m_top, pair)
            now = wide[:, :LANES] + wide[:, LANES:] + dot_bf16(m_low, g_top)
            total = jnp.where(mine, now, total)
        grad_signal[0, :, at] = total + direct[:, at] * grad_y[0, :, at]

    writes = write_sums[:, :both]
    column_sums[0] = writes
    total_own = flip_back(read_parts[...]) - writes
    reach_halves = halves(reach[0])
    per_wide = WIDE // head_size
    for d in range(2):
        side = (above, below)[d]
        grads = jnp.where(side & same, grad_scores, 0.0)
        reader = part(2 * d + 1)
        reader3 = left3(reader)
        grad_reader = dot(grads, part(2 * d), 0, 0)
        for t in range(inner // WIDE):
            at = slice(t * WIDE, (t + 1) * WIDE)
            first = d * heads + t * per_wide
            before = states[0, d, :, at]
            reached = grad_y[0, :, at] * dot_bf16(
                reach_halves, spread(first, head_size, both)
            )
            seen = dot_bf16(reader3, right3(before))
            total_own = total_own + dot_bf16(
                halves(reached * seen), gather_heads(first, head_size, both)
            )
            grad_reader = grad_reader + product_with(reached, stacked(before), state)
        grad_maps[0, :, 2 * d * state : (2 * d + 1) * state] = dot(grads, reader)
        grad_maps[0, :, (2 * d + 1) * state : (2 * d + 2) * state] = grad_reader
    own[0] = total_own


def product_with(x, stack, size):
    top, low = split(x)
    twice = dot_bf16(top, stack, 1, 1)
    return twice[:, :size] + twice[:, size:] + dot_bf16(low, stack[:size], 1, 1)


def flip_back(x):
    size = x.shape[0]
    one = triangle(size, lambda r, c: r == c).astype(BF16)
    a, b, c = split3(x)
    return dot_bf16(a, one, 0, 0) + dot_bf16(b, one, 0, 0) + dot_bf16(c, one, 0, 0)


def fold_rows(x):
    total = x[:EDGE]
    for r in range(EDGE, x.shape[0], EDGE):
        total = total + x[r : r + EDGE]
    return total


def end_kernel(
    dims,
    place,
    lengths,
    pay,
    act,
    z_in,
    tail,
    conv,
    states,
    keep,
    grad_inside,
    grad_maps,
    own,
    column_sums,
    mixed,
    taps,
    decays,
    grad_values,
    grad_states,
    grad_raw,
    smalls,
    later,
    grad_act,
    documents,
    masks,
):
    length, inner, heads, state, reach_cells, rows = dims
    head_size = inner // heads
    both = 2 * heads
    per_tile = WIDE // head_size
    width = inner + 4 * state
    offsets_count = 2 * reach_cells + 1
    long = length + 2 * EDGE
    first_row = EDGE - reach_cells
    unpack(pay, later, inner // LANES, rows, state)
    ends = bounds_of(lengths, pl.program_id(0))
    fill_masks(masks, documents, place[0] * length, ends, EDGE, length, reach_cells)

    tail_halves = halves(tail[0])
    leave = jnp.zeros((length, both), F32)
    through = jnp.zeros((1, both), F32)
    for d in range(2):
        writer3 = left3(act[0, :, inner + 2 * d * state : inner + (2 * d + 1) * state])
        grad_writer = grad_maps[0, :, 2 * d * state : (2 * d + 1) * state]
        for t in range(inner // WIDE):
            at = slice(t * WIDE, (t + 1) * WIDE)
            first = d * heads + t * per_tile
            fold = gather_heads(first, head_size, both)
            after = later[d, :, at]
            tails = dot_bf16(tail_halves, spread(first, head_size, both))
            weighted = act[0, :, at] * tails
            pulled = dot_bf16(writer3, right3(after))
            base = grad_inside[0, :, at] if d == 0 else grad_act[:, at]
            grad_act[:, at] = base + tails * pulled
            leave = leave + dot_bf16(halves(weighted * pulled), fold)
            grad_writer = grad_writer + product_with(weighted, stacked(after), state)
            crossed = jnp.sum(states[0, d, :, at] * after, axis=0, keepdims=True)
            through = (
                through + dot_bf16(halves(jnp.broadcast_to(crossed, (EDGE, WIDE))), fold)[:1]
            )
        at = inner + 2 * d * state
        grad_act[:, at : at + state] = grad_writer
        grad_act[:, at + state : at + 2 * state] = grad_maps[
            0, :, (2 * d + 1) * state : (2 * d + 2) * state
        ]

    grad_values[0] = jnp.zeros((long, inner), F32)
    grad_states[0] = jnp.zeros((long, width - inner), F32)
    def column(t, _, into, shift):
        at = pl.ds(pl.multiple_of(t * WIDE, WIDE), WIDE)
        put = pl.ds(pl.multiple_of((t - shift) * WIDE, WIDE), WIDE)
        bias_sum = jnp.zeros((EDGE, WIDE), F32)
        tap_sums = [jnp.zeros((EDGE, WIDE), F32) for _ in range(offsets_count)]
        for r in range(0, length, CHUNK):
            value = conv[0, r : r + CHUNK, at]
            chance = sigmoid(value)
            grad = grad_act[r : r + CHUNK, at] * (chance * (1.0 + value * (1.0 - chance)))
            bias_sum = bias_sum + fold_rows(grad)
            for o in range(offsets_count):
                begin = first_row + o + r
                mask = masks[o, r : r + CHUNK]
                now = grad * jnp.concatenate([mask] * (WIDE // LANES), axis=1)
                into[0, begin : begin + CHUNK, put] += now * taps[o : o + 1, at]
                tap_sums[o] = tap_sums[o] + fold_rows(now * mixed[0, begin : begin + CHUNK, at])
        smalls[0, offsets_count : offsets_count + 1, at] = jnp.sum(bias_sum, axis=0, keepdims=True)
        for o in range(offsets_count):
            smalls[0, o : o + 1, at] = jnp.sum(tap_sums[o], axis=0, keepdims=True)
        return 0

    split_at = inner // WIDE
    lax.fori_loop(0, split_at, partial(column, into=grad_values, shift=0), 0)
    lax.fori_loop(
        split_at, width // WIDE, partial(column, into=grad_states, shift=split_at), 0
    )

    ahead = lax.broadcasted_iota(jnp.int32, (length, both), 1) < heads
    from_here = triangle(length, lambda r, c: c >= r).astype(BF16)
    to_here = triangle(length, lambda r, c: c <= r).astype(BF16)
    before_here = triangle(length, lambda r, c: c < r).astype(BF16)
    after_here = triangle(length, lambda r, c: c > r).astype(BF16)
    entered = own[0]
    grad_decay = (
        jnp.where(
            ahead,
            exact_sum(from_here, entered) + exact_sum(before_here, leave),
            exact_sum(to_here, entered) + exact_sum(after_here, leave),
        )
        + through * keep[0]
    )
    z = z_in[0]
    step = softplus(z)
    chance = sigmoid(z)
    rates = jnp.exp(jnp.concatenate([decays[0:1, :], decays[1:2, :]], axis=1))
    ratio = jnp.where(step > 1e-30, chance / jnp.maximum(step, 1e-30), 1.0)
    grad_z = (leave + column_sums[0]) * ratio - rates * grad_decay * chance
    grad_raw[0, :EDGE] = jnp.zeros((EDGE, both), F32)
    grad_raw[0, EDGE + length :] = jnp.zeros((EDGE, both), F32)
    grad_raw[0, EDGE : EDGE + length] = grad_z
    smalls[0, EDGE:, :] = jnp.zeros((EDGE, width), F32)
    smalls[0, EDGE : EDGE + 1, :both] = jnp.sum(grad_z, axis=0, keepdims=True)
    smalls[0, EDGE + 1 : EDGE + 2, :both] = -rates * jnp.sum(
        step * grad_decay, axis=0, keepdims=True
    )


def pack_kernel(
    dims, rest, own_states, smalls, side_smalls, grad_stepper, grad_prenorm, packed
):
    _, inner, _, state, reach_cells, _ = dims
    both = grad_stepper.shape[0]
    small = smalls[0]
    side = side_smalls[0]
    for i in range(1, smalls.shape[0]):
        small = small + smalls[i]
        side = side + side_smalls[i]
    at = rest.shape[0]
    packed[:at] = rest[...]
    cut = own_states.shape[0]
    packed[at : at + cut] = own_states[...]
    at += cut
    packed[at:] = jnp.zeros((packed.shape[0] - at, inner), F32)
    packed[at : at + both] = grad_stepper[...]
    at += both
    packed[at : at + EDGE] = small[:EDGE, :inner]
    packed[at + EDGE : at + 2 * EDGE, : 4 * state] = small[:EDGE, inner:]
    packed[at + 2 * EDGE : at + 2 * EDGE + 2, :] = side[:2]
    packed[at + 2 * EDGE + 2 : at + 2 * EDGE + 4, :] = small[EDGE : EDGE + 2, :inner]
    packed[at + 2 * EDGE + 4 : at + 2 * EDGE + 5, :] = grad_prenorm[...]


def unpack_kernel(
    dims,
    mine,
    peer,
    filters,
    shifts,
    kernels,
    biases,
    postnorm,
    direct,
    offsets,
    decays,
    prenorm,
):
    _, inner, heads, state, reach_cells, _ = dims
    head_size = inner // heads
    count = 2 * reach_cells + 1
    at = 2 * state + 2 * heads
    filters[...] = mine[at : at + count]
    shifts[...] = mine[at + count]
    at += EDGE
    shared = mine[at : at + EDGE, : 4 * state] + peer[at : at + EDGE, : 4 * state]
    for k in range(4):
        kernels[:, k, :] = shared[:count, k * state : (k + 1) * state]
        biases[k : k + 1, :] = shared[count:, k * state : (k + 1) * state]
    at += EDGE
    postnorm[...] = mine[at]
    fold = jnp.zeros((EDGE, heads), F32)
    for t in range(inner // WIDE):
        row = jnp.broadcast_to(mine[at + 1 : at + 2, t * WIDE : (t + 1) * WIDE], (EDGE, WIDE))
        fold = fold + dot_bf16(
            jnp.concatenate(split3(row), axis=1),
            gather_heads(t * (WIDE // head_size), head_size, heads, 3),
        )
    direct[...] = fold[0]
    for d in range(2):
        offsets[d : d + 1, :] = mine[at + 2 : at + 3, d * heads : (d + 1) * heads]
        decays[d : d + 1, :] = mine[at + 3 : at + 4, d * heads : (d + 1) * heads]
    prenorm[...] = mine[at + 4] + peer[at + 4]


def exchange(x, axis, bit):
    peers = lax.axis_size(axis)
    return lax.ppermute(x, axis, [(i, i ^ (1 << bit)) for i in range(peers)])


def bit_of(place, bit):
    return (place >> bit) & 1


def join_halves(mine, own, other):
    return jnp.where(
        mine == 0, jnp.concatenate([own, other]), jnp.concatenate([other, own])
    )


def tie(*arrays):
    return lax.optimization_barrier(arrays)


class PairTotal:
    def __init__(self, axis):
        self.axis = axis
        self.place = lax.axis_index(axis)
        bits = lax.axis_size(axis).bit_length() - 1
        down = [(0, 1), (1, 0), (2,)] + [(bit,) for bit in range(3, bits)]
        self.steps = [("halve", order) for order in down]
        self.steps += [("join", order) for order in reversed(down)]
        self.at = 0
        self.now = [None, None]
        self.came = [None, None]

    def mine(self, bit):
        return bit_of(self.place, bit)

    def outgoing(self, k=None):
        kind, order = self.steps[self.at]
        which = range(len(order)) if k is None else (k,)
        out = []
        for i in which:
            x, mine = self.now[i], self.mine(order[i])
            if kind == "join":
                out.append(x)
            elif order == (2,):
                out.append(jnp.where(mine == 0, self.now[1], self.now[0]))
            else:
                half = x.shape[0] // 2
                out.append(lax.dynamic_slice_in_dim(x, (1 - mine) * half, half))
        return out

    def go(self, sent, k=None):
        _, order = self.steps[self.at]
        which = range(len(order)) if k is None else (k,)
        for i, x in zip(which, sent):
            self.came[i] = exchange(x, self.axis, order[i])

    def take(self, *others):
        kind, order = self.steps[self.at]
        came = [c for c in self.came[: len(order)]]
        if others:
            came = list(tie(*came, *others)[: len(order)])
        now = []
        for i, bit in enumerate(order):
            x, mine, c = self.now[i], self.mine(bit), came[i]
            if order == (2,):
                if kind == "halve":
                    now = [jnp.where(mine == 0, self.now[0], self.now[1]) + c]
                else:
                    now = [jnp.where(mine == 0, x, c), jnp.where(mine == 0, c, x)]
            elif kind == "halve":
                half = x.shape[0] // 2
                now.append(lax.dynamic_slice_in_dim(x, mine * half, half) + c)
            else:
                now.append(join_halves(mine, x, c))
        self.now = now
        self.at += 1

    def ahead_of(self, array, k=None):
        sent = self.outgoing(k)
        self.go(sent, k)
        return tie(array, *sent)[0]

    @property
    def done(self):
        return self.at == len(self.steps)

    def turn(self, *others):
        if self.done:
            return self.now[0]
        self.take(*others)
        if not self.done:
            sent = self.outgoing()
            self.go(sent)
            return sent[0]
        return self.now[0]


def local(
    hidden,
    lengths,
    prenorm,
    gating,
    values,
    states,
    stepper,
    offsets,
    decays,
    filters,
    shifts,
    kernels,
    biases,
    direct,
    postnorm,
    output,
    cotangent,
):
    micro, length, model = hidden.shape
    inner = gating.shape[1]
    heads = direct.shape[0]
    both = 2 * heads
    head_size = inner // heads
    state = states.shape[2]
    reach_cells = (filters.shape[0] - 1) // 2
    count = 2 * reach_cells + 1
    peers = lax.axis_size("seq")
    place = lax.axis_index("seq")
    head_place = lax.axis_index("head")
    inner_all = inner * lax.axis_size("head")
    rows = micro * 2 * state // peers
    tiles = inner // LANES
    dims = (length, inner, heads, state, reach_cells, rows)
    maps_width = 4 * state
    width = inner + maps_width
    long = length + 2 * EDGE
    half_peers = peers // micro
    where = place.reshape(1).astype(jnp.int32)

    up = [(i, i + 1) for i in range(peers - 1)]
    down = [(i + 1, i) for i in range(peers - 1)]
    swap = [(0, 1), (1, 0)]
    before = lax.ppermute(hidden[:, length - EDGE :], "seq", up)
    after = lax.ppermute(hidden[:, :EDGE], "seq", down)
    states_flat = states.reshape(model, maps_width)
    stepper_flat = stepper.reshape(model, both)
    direct_row = jnp.repeat(direct, head_size)[None]
    post_row = postnorm[None]

    def spec(*block):
        return pl.BlockSpec((1,) + block, lambda i: (i,) + (0,) * len(block))

    def fixed(*block):
        return pl.BlockSpec(block, lambda i: (0,) * len(block))

    def shape(*dims):
        return jax.ShapeDtypeStruct(dims, F32)

    smem = pl.BlockSpec(memory_space=pltpu.SMEM)
    vmem = pl.BlockSpec(memory_space=pltpu.VMEM)
    packed = tiles * rows + EDGE
    pay_spec = pl.BlockSpec((half_peers, packed, LANES), lambda i: (i, 0, 0))
    plain_spec = pl.BlockSpec((half_peers, tiles * rows, LANES), lambda i: (i, 0, 0))
    small = spec(length, both)
    wide = spec(length, inner)
    acts = spec(length, width)
    row = fixed(1, inner)
    flat = spec(both, length)

    (
        normed,
        mixed,
        conv,
        act,
        maps_t,
        z,
        run,
        late,
        run_rows,
        late_rows,
        reach,
        tail,
        keep,
        taps,
        pay,
    ) = pl.pallas_call(
        partial(front_kernel, dims),
        grid=(micro,),
        in_specs=[
            smem,
            smem,
            spec(EDGE, model),
            spec(length, model),
            spec(EDGE, model),
            fixed(1, model),
            fixed(model, inner),
            fixed(model, maps_width),
            fixed(model, both),
            fixed(count, inner),
            fixed(count, 4, state),
            fixed(1, inner),
            fixed(4, state),
            fixed(2, heads),
            fixed(2, heads),
        ],
        out_specs=[
            spec(long, model),
            spec(long, width),
            acts,
            acts,
            spec(maps_width, length),
            small,
            small,
            small,
            flat,
            flat,
            small,
            small,
            spec(1, both),
            fixed(EDGE, width),
            pay_spec,
        ],
        out_shape=[
            shape(micro, long, model),
            shape(micro, long, width),
            shape(micro, length, width),
            shape(micro, length, width),
            shape(micro, maps_width, length),
            shape(micro, length, both),
            shape(micro, length, both),
            shape(micro, length, both),
            shape(micro, both, length),
            shape(micro, both, length),
            shape(micro, length, both),
            shape(micro, length, both),
            shape(micro, 1, both),
            shape(EDGE, width),
            shape(peers, packed, LANES),
        ],
        scratch_shapes=[
            pltpu.VMEM((long + 2 * EDGE, LANES), jnp.int32),
            pltpu.VMEM((count, length, LANES), F32),
        ],
        compiler_params=PARAMS,
        name="front",
    )(
        where,
        lengths,
        before,
        hidden,
        after,
        prenorm[None],
        values,
        states_flat,
        stepper_flat,
        filters,
        kernels,
        shifts[None],
        biases,
        offsets,
        decays,
    )

    direction = lax.rem(place // (peers // (2 * micro)), 2)

    def prefix(terms, keeps, flipped):
        return pl.pallas_call(
            partial(prefix_kernel, tiles, rows),
            grid=(1,),
            in_specs=[smem, fixed(*terms.shape), fixed(*keeps.shape)],
            out_specs=fixed(peers, tiles * rows, LANES),
            out_shape=shape(peers, tiles * rows, LANES),
            compiler_params=PARAMS,
            name="prefix",
        )(flipped.reshape(1).astype(jnp.int32), terms, keeps)

    def swap_all(x):
        return lax.all_to_all(x, "seq", 0, 0, tiled=True)

    terms = swap_all(pay)
    arrived = swap_all(prefix(terms, terms, direction))

    normed_flat = normed.reshape(micro * long, model)
    cotangent_flat = cotangent.reshape(micro * length, model)
    back = dot(cotangent_flat, output, 1, 1).reshape(micro, length, inner)
    inside = pl.pallas_call(
        partial(inside_kernel, dims),
        grid=(micro,),
        in_specs=[smem, smem, acts, small, flat],
        out_specs=wide,
        out_shape=shape(micro, length, inner),
        compiler_params=PARAMS,
        name="inside",
    )(where, lengths, act, run, late_rows)
    gate = dot(normed_flat, gating).reshape(micro, long, inner)

    gates = spec(long, inner)
    sum_spec = spec(length, LANES)
    state_spec = spec(2, state, inner)
    mixed_y, sums, before_states = pl.pallas_call(
        partial(join_kernel, dims),
        grid=(micro,),
        in_specs=[wide, plain_spec, acts, small, gates, wide, row, row],
        out_specs=[wide, sum_spec, state_spec],
        out_shape=[
            shape(micro, length, inner),
            shape(micro, length, LANES),
            shape(micro, 2, state, inner),
        ],
        compiler_params=PARAMS,
        name="join",
    )(inside, arrived, act, reach, gate, back, direct_row, post_row)
    peer_sums = lax.ppermute(sums, "head", swap)

    grad_y, normal, pay_back = pl.pallas_call(
        partial(turn_kernel, dims, inner_all),
        grid=(micro,),
        in_specs=[
            sum_spec,
            sum_spec,
            wide,
            gates,
            wide,
            spec(maps_width, length),
            small,
            row,
        ],
        out_specs=[wide, wide, plain_spec],
        out_shape=[
            shape(micro, length, inner),
            shape(micro, length, inner),
            shape(peers, tiles * rows, LANES),
        ],
        compiler_params=PARAMS,
        name="turn",
    )(sums, peer_sums, mixed_y, gate, back, maps_t, reach, post_row)

    back_terms = swap_all(pay_back)

    normal_flat = normal.reshape(micro * length, inner)
    grad_output = dot(normal_flat, cotangent_flat, 0, 0)

    grad_gate, side_smalls = pl.pallas_call(
        partial(side_kernel, dims, inner_all),
        grid=(micro,),
        in_specs=[sum_spec, sum_spec, wide, gates, wide, acts, wide, row],
        out_specs=[gates, spec(EDGE, inner)],
        out_shape=[shape(micro, long, inner), shape(micro, EDGE, inner)],
        compiler_params=PARAMS,
        name="side",
    )(sums, peer_sums, mixed_y, gate, back, act, grad_y, post_row)
    grad_gate_flat = grad_gate.reshape(micro * long, inner)
    grad_gating = dot(normed_flat, grad_gate_flat, 0, 0)
    early = PairTotal("seq")
    early.now = [grad_output, grad_gating]
    back_terms = early.ahead_of(back_terms)
    prefixed = prefix(back_terms, terms, 1 - direction)
    back_arrived = swap_all(prefixed)
    grad_y = tie(grad_y, prefixed)[0]

    grad_inside, grad_maps, own, column_sums = pl.pallas_call(
        partial(inside_back_kernel, dims),
        grid=(micro,),
        in_specs=[smem, smem, acts, wide, small, flat, small, state_spec, row],
        out_specs=[wide, spec(length, maps_width), small, small],
        out_shape=[
            shape(micro, length, inner),
            shape(micro, length, maps_width),
            shape(micro, length, both),
            shape(micro, length, both),
        ],
        scratch_shapes=[pltpu.VMEM((both, length), F32)],
        compiler_params=PARAMS,
        name="inside_back",
    )(where, lengths, act, grad_y, late, run_rows, reach, before_states, direct_row)

    grad_normed_gate = dot(grad_gate_flat, gating, 1, 1)
    back_arrived = tie(back_arrived, own, grad_normed_gate)[0]

    grad_mixed, grad_mixed_maps, grad_raw, smalls = pl.pallas_call(
        partial(end_kernel, dims),
        grid=(micro,),
        in_specs=[
            smem,
            smem,
            plain_spec,
            acts,
            small,
            small,
            acts,
            state_spec,
            spec(1, both),
            wide,
            spec(length, maps_width),
            small,
            small,
            spec(long, width),
            fixed(EDGE, width),
            fixed(2, heads),
        ],
        out_specs=[gates, spec(long, maps_width), spec(long, both), spec(2 * EDGE, width)],
        out_shape=[
            shape(micro, long, inner),
            shape(micro, long, maps_width),
            shape(micro, long, both),
            shape(micro, 2 * EDGE, width),
        ],
        scratch_shapes=[
            pltpu.VMEM((2, state, inner), F32),
            pltpu.VMEM((length, width), F32),
            pltpu.VMEM((long + 2 * EDGE, LANES), jnp.int32),
            pltpu.VMEM((count, length, LANES), F32),
        ],
        compiler_params=PARAMS,
        name="end",
    )(
        where,
        lengths,
        back_arrived,
        act,
        z,
        tail,
        conv,
        before_states,
        keep,
        grad_inside,
        grad_maps,
        own,
        column_sums,
        mixed,
        taps,
        decays,
    )
    all_maps = grad_mixed_maps.reshape(micro * long, maps_width)
    all_maps = all_maps + lax.ppermute(all_maps, "head", swap)

    early.take(grad_raw)
    grad_mixed = early.ahead_of(grad_mixed)
    grad_mixed = grad_mixed.reshape(micro * long, inner)
    grad_mixed_maps = grad_mixed_maps.reshape(micro * long, maps_width)
    grad_raw = grad_raw.reshape(micro * long, both)
    cut = maps_width // 2
    most = (model + cut + cut) // 2
    late_total = PairTotal("seq")
    late_total.now = [dot(normed_flat[:, :most], grad_mixed, 0, 0), None]
    grad_normed = (
        dot(grad_mixed, values, 1, 1)
        + dot(grad_mixed_maps, states_flat, 1, 1)
        + grad_normed_gate
        + dot(grad_raw, stepper_flat, 1, 1)
    )
    grad_prenorm = jnp.sum(grad_normed * normed_flat, axis=0, keepdims=True) / prenorm[None]
    early.take(grad_prenorm, late_total.now[0])
    normed_flat = early.ahead_of(normed_flat)
    own_maps = lax.dynamic_slice_in_dim(all_maps, head_place * cut, cut, 1)
    second_late = pl.pallas_call(
        partial(pack_kernel, dims),
        in_specs=[vmem] * 6,
        out_specs=vmem,
        out_shape=shape(most, inner),
        compiler_params=PARAMS,
        name="pack",
    )(
        dot(normed_flat[:, most:], grad_mixed, 0, 0),
        dot(own_maps, normed_flat, 0, 0),
        smalls,
        side_smalls,
        dot(grad_raw, normed_flat, 0, 0),
        grad_prenorm,
    )
    late_total.now[1] = second_late
    grad_normed = late_total.ahead_of(grad_normed)

    grad_normed = grad_normed.reshape(micro, long, model)
    grad_normed = grad_normed + lax.ppermute(grad_normed, "head", swap)
    from_after = lax.ppermute(grad_normed[:, :EDGE], "seq", down)
    from_before = lax.ppermute(grad_normed[:, EDGE + length :], "seq", up)
    grad_here = grad_normed[:, EDGE : EDGE + length] + jnp.concatenate(
        [from_before, jnp.zeros((micro, length - 2 * EDGE, model), F32), from_after], axis=1
    )
    scale = lax.rsqrt(jnp.mean(hidden * hidden, axis=2, keepdims=True) + EPSILON)
    pulled = grad_here * prenorm
    grad_hidden = (
        cotangent
        + scale * pulled
        - hidden * (scale**3 * jnp.sum(pulled * hidden, axis=2, keepdims=True) / model)
    )

    normal_flat = tie(normal_flat, second_late)[0]
    projected = dot(normal_flat, output)
    result = hidden + (projected + lax.ppermute(projected, "head", swap)).reshape(hidden.shape)

    held = second_late
    for mine in "eelelellellel":
        total = late_total if mine == "l" else early
        held = total.turn(held)
    while late_total.at < len(late_total.steps) - 1:
        held = late_total.turn(held)
        held = early.turn(held)
    while not early.done:
        held = early.turn(held)
    late_total.take(held, grad_hidden, result)
    late_done = late_total.now
    grad_output, grad_gating = early.now
    last = late_done[1][model - most :]
    peer_last = lax.ppermute(last, "head", swap)
    own_states, other_states = last[:cut], peer_last[:cut]
    grad_states = jnp.where(
        head_place == 0,
        jnp.concatenate([own_states, other_states]),
        jnp.concatenate([other_states, own_states]),
    ).T.reshape(states.shape)
    grad_stepper = last[cut : cut + both].T.reshape(stepper.shape)
    (
        grad_filters,
        grad_shifts,
        grad_kernels,
        grad_biases,
        grad_postnorm,
        grad_direct,
        grad_offsets,
        grad_decays,
        grad_prenorm,
    ) = pl.pallas_call(
        partial(unpack_kernel, dims),
        in_specs=[vmem, vmem],
        out_specs=[vmem] * 9,
        out_shape=[
            shape(count, inner),
            shape(inner),
            shape(*kernels.shape),
            shape(*biases.shape),
            shape(inner),
            shape(heads),
            shape(*offsets.shape),
            shape(*decays.shape),
            shape(model),
        ],
        compiler_params=PARAMS,
        name="unpack",
    )(last, peer_last)
    late_done = jnp.concatenate([late_done[0], late_done[1][: model - most]], axis=0)
    return (
        result,
        grad_hidden,
        grad_prenorm,
        grad_gating,
        late_done,
        grad_states,
        grad_stepper,
        grad_offsets,
        grad_decays,
        grad_filters,
        grad_shifts,
        grad_kernels,
        grad_biases,
        grad_direct,
        grad_postnorm,
        grad_output,
    )


def solution(mesh):
    in_specs = (
        P(None, "seq", None),
        P(),
        P(),
        P(None, "head"),
        P(None, "head"),
        P(),
        P(None, None, "head"),
        P(None, "head"),
        P(None, "head"),
        P(None, "head"),
        P("head"),
        P(),
        P(),
        P("head"),
        P("head"),
        P("head", None),
        P(None, "seq", None),
    )
    out_specs = (
        P(None, "seq", None),
        P(None, "seq", None),
        P(),
        P(None, "head"),
        P(None, "head"),
        P(),
        P(None, None, "head"),
        P(None, "head"),
        P(None, "head"),
        P(None, "head"),
        P("head"),
        P(),
        P(),
        P("head"),
        P("head"),
        P("head", None),
    )
    return jax.shard_map(local, mesh=mesh, in_specs=in_specs, out_specs=out_specs, check_vma=False)
```

```python
from functools import partial

import jax
import jax.numpy as jnp
from jax import lax
from jax.experimental import pallas as pl
from jax.experimental.pallas import tpu as pltpu
from jax.sharding import PartitionSpec as P

EPSILON = 1e-05
HIGH = lax.Precision.HIGH
F32 = jnp.float32
BF16 = jnp.bfloat16
LANES = 128
WIDE = 256
CHUNK = 128
EDGE = 8
PARAMS = pltpu.CompilerParams(vmem_limit_bytes=56 * 1024 * 1024)


def dot(left, right, over_left=1, over_right=0, precision=HIGH):
    return lax.dot_general(
        left,
        right,
        (((over_left,), (over_right,)), ((), ())),
        precision=precision,
        preferred_element_type=F32,
    )


def split(x):
    top = x.astype(BF16)
    return top, (x - top.astype(F32)).astype(BF16)


def dot_bf16(left, right, over_left=1, over_right=0):
    return lax.dot_general(
        left,
        right,
        (((over_left,), (over_right,)), ((), ())),
        preferred_element_type=F32,
    )


def spread(first, head_size, both):
    rows = lax.broadcasted_iota(jnp.int32, (2 * both, WIDE), 0)
    columns = lax.broadcasted_iota(jnp.int32, (2 * both, WIDE), 1)
    return (lax.rem(rows, both) == first + columns // head_size).astype(BF16)


def gather_heads(first, head_size, both, parts=2):
    rows = lax.broadcasted_iota(jnp.int32, (parts * WIDE, both), 0)
    columns = lax.broadcasted_iota(jnp.int32, (parts * WIDE, both), 1)
    return (columns == first + lax.rem(rows, WIDE) // head_size).astype(BF16)


def split3(x):
    top = x.astype(BF16)
    rest = x - top.astype(F32)
    middle = rest.astype(BF16)
    return top, middle, (rest - middle.astype(F32)).astype(BF16)


def halves(x):
    return jnp.concatenate(split(x), axis=1)


def triangle(size, keep):
    rows = lax.broadcasted_iota(jnp.int32, (size, size), 0)
    columns = lax.broadcasted_iota(jnp.int32, (size, size), 1)
    return keep(rows, columns)


def exact_sum(zero_one, x):
    a, b, c = split3(x)
    return dot_bf16(zero_one, a) + dot_bf16(zero_one, b) + dot_bf16(zero_one, c)


def flip(x):
    size = x.shape[1]
    one = triangle(size, lambda r, c: r == c).astype(BF16)
    a, b, c = split3(x)
    return dot_bf16(one, a, 1, 1) + dot_bf16(one, b, 1, 1) + dot_bf16(one, c, 1, 1)


def sigmoid(x):
    return 1.0 / (1.0 + jnp.exp(-x))


def softplus(x):
    return jnp.maximum(x, 0.0) + jnp.log1p(jnp.exp(-jnp.abs(x)))


def bounds_of(lengths, i):
    ends = []
    total = jnp.int32(0)
    for k in range(lengths.shape[1]):
        total = total + lengths[i, k]
        ends.append(total)
    return ends


def document(places, ends):
    found = sum(jnp.where(places >= end, 1, 0) for end in ends)
    return jnp.where(places < 0, -1, jnp.where(places >= ends[-1], -2, found))


def same_document(first, ends, length):
    rows = document(first + lax.broadcasted_iota(jnp.int32, (length, LANES), 0), ends)
    columns = document(first + lax.broadcasted_iota(jnp.int32, (1, length), 1), ends)
    return jnp.concatenate([rows] * (length // LANES), axis=1) == columns


def fill_masks(masks, documents, first, ends, start, rows, reach_cells):
    total = documents.shape[0]
    documents[...] = document(
        first - 2 * EDGE + lax.broadcasted_iota(jnp.int32, (total, LANES), 0), ends
    )
    center = documents[EDGE + start : EDGE + start + rows]
    for o in range(2 * reach_cells + 1):
        at = EDGE + start + o - reach_cells
        masks[o] = (documents[at : at + rows] == center).astype(F32)


def left3(x):
    top = x.astype(BF16).astype(F32)
    return jnp.concatenate([top, top, x - top], axis=1).astype(BF16)


def right3(x):
    top, low = split(x)
    return jnp.concatenate([top, low, top], axis=0)


def stacked(x):
    return jnp.concatenate(split(x), axis=0)


def front_kernel(
    dims,
    place,
    lengths,
    before,
    hidden,
    after,
    prenorm,
    values,
    states,
    stepper,
    filters,
    kernels,
    shifts,
    biases,
    offsets,
    decays,
    normed,
    mixed,
    conv,
    act,
    maps_t,
    z_out,
    run,
    late,
    run_rows,
    late_rows,
    reach,
    tail,
    keep,
    taps,
    pay,
    documents,
    masks,
):
    length, inner, heads, state, reach_cells, rows = dims
    head_size = inner // heads
    both = 2 * heads
    maps_width = 4 * state
    width = inner + maps_width
    offsets_count = 2 * reach_cells + 1
    i = pl.program_id(0)
    ends = bounds_of(lengths, i)
    first = place[0] * length
    fill_masks(masks, documents, first, ends, EDGE, length, reach_cells)

    gain = prenorm[...][None]

    def norm(x):
        mean = jnp.sum(x * x, axis=1, keepdims=True) / x.shape[1]
        return x * lax.rsqrt(mean + EPSILON) * gain

    normed[0, :EDGE] = norm(before[0])
    for r in range(0, length, 64):
        normed[0, EDGE + r : EDGE + r + 64] = norm(hidden[0, r : r + 64])
    normed[0, EDGE + length :] = norm(after[0])

    whole = normed[0]
    for t in range(inner // WIDE):
        at = slice(t * WIDE, (t + 1) * WIDE)
        mixed[0, :, at] = dot(whole, values[:, at])
    mixed[0, :, inner:] = dot(whole, states[...])
    raw = dot(normed[0, EDGE : EDGE + length], stepper[...])

    taps[:offsets_count, :inner] = filters[...]
    taps[offsets_count:, :inner] = shifts[...][None]
    for k in range(4):
        at = slice(inner + k * state, inner + (k + 1) * state)
        taps[:offsets_count, at] = kernels[:, k, :]
        taps[offsets_count:, at] = biases[k : k + 1, :]

    for t in range(width // WIDE):
        at = slice(t * WIDE, (t + 1) * WIDE)
        for r in range(0, length, CHUNK):
            total = jnp.broadcast_to(taps[offsets_count:, at], (CHUNK, WIDE))
            for o in range(offsets_count):
                begin = EDGE - reach_cells + o + r
                mask = masks[o, r : r + CHUNK]
                total = total + (mixed[0, begin : begin + CHUNK, at] * taps[o : o + 1, at]) * (
                    jnp.concatenate([mask] * (WIDE // LANES), axis=1)
                )
            conv[0, r : r + CHUNK, at] = total
            act[0, r : r + CHUNK, at] = total * sigmoid(total)
    flipped = jnp.transpose(act[0, :, inner:])
    maps_t[0] = flipped

    ahead = lax.broadcasted_iota(jnp.int32, (length, both), 1) < heads
    ahead_row = ahead[:1]
    z = raw + jnp.concatenate([offsets[0:1, :], offsets[1:2, :]], axis=1)
    rates = jnp.exp(jnp.concatenate([decays[0:1, :], decays[1:2, :]], axis=1))
    step = softplus(z)
    decay = -step * rates
    lower = triangle(length, lambda r, c: r >= c).astype(BF16)
    upper = triangle(length, lambda r, c: r <= c).astype(BF16)
    running = jnp.where(ahead, exact_sum(lower, decay), exact_sum(upper, decay))
    edge = jnp.where(ahead_row, running[length - 1 :], running[:1])
    here = document(first + lax.broadcasted_iota(jnp.int32, (length, both), 0), ends)
    seg_before = document(first - 1, ends)
    seg_after = document(first + length, ends)
    seg_first = document(first, ends)
    seg_last = document(first + length - 1, ends)
    enter = (here == jnp.where(ahead, seg_before, seg_after)).astype(F32)
    leave = (here == jnp.where(ahead, seg_last, seg_first)).astype(F32)
    keep_mask = jnp.where(
        ahead_row,
        jnp.where(seg_last == seg_before, 1.0, 0.0),
        jnp.where(seg_first == seg_after, 1.0, 0.0),
    )
    reach_now = enter * jnp.exp(running)
    tail_now = leave * jnp.exp(edge - running) * step
    keep_now = keep_mask * jnp.exp(edge)
    late_now = running - jnp.log(jnp.maximum(step, 1e-37))
    z_out[0] = z
    run[0] = running
    late[0] = late_now
    reach[0] = reach_now
    tail[0] = tail_now
    run_rows[0] = flip(running)
    late_rows[0] = flip(late_now)
    keep[0] = keep_now

    tail_halves = halves(tail_now)
    keep_halves = halves(jnp.broadcast_to(keep_now, (EDGE, both)))
    pieces = state // rows
    per_tile = WIDE // head_size
    for d in range(2):
        maps_now = stacked(flipped[2 * d * state : (2 * d + 1) * state])
        keeps = []
        for t in range(inner // WIDE):
            grow = spread(d * heads + t * per_tile, head_size, both)
            weighted = act[0, :, t * WIDE : (t + 1) * WIDE] * dot_bf16(tail_halves, grow)
            put_states(pay, d, t, product_of_stack(maps_now, weighted, state), pieces, rows)
            keep_wide = dot_bf16(keep_halves, grow)[:1]
            keeps += [keep_wide[:, k * LANES : (k + 1) * LANES] for k in range(WIDE // LANES)]
        tiles = inner // LANES
        keeps.append(jnp.zeros((EDGE - tiles, LANES), F32))
        keep_block = jnp.concatenate(keeps, axis=0)
        for j in range(pieces):
            pay[d * pieces + j, tiles * rows :, :] = keep_block


def product_of_stack(stack, x, size):
    top, low = split(x)
    twice = dot_bf16(stack, top)
    return twice[:size] + twice[size:] + dot_bf16(stack[:size], low)


def put_states(pay, d, t, own, pieces, rows):
    for k in range(WIDE // LANES):
        at = (t * (WIDE // LANES) + k) * rows
        for j in range(pieces):
            pay[d * pieces + j, at : at + rows, :] = own[
                j * rows : (j + 1) * rows, k * LANES : (k + 1) * LANES
            ]


def prefix_kernel(tiles, rows, flipped, terms, keeps, into):
    peers = terms.shape[0]
    back = flipped[0] != 0

    def turn(i, carry):
        at = jnp.where(back, peers - 1 - i, i)
        factor = keeps[at, tiles * rows :, :]
        new = []
        for t in range(tiles):
            into[at, t * rows : (t + 1) * rows, :] = carry[t]
            new.append(
                carry[t] * factor[t : t + 1] + terms[at, t * rows : (t + 1) * rows, :]
            )
        return tuple(new)

    lax.fori_loop(0, peers, turn, tuple(jnp.zeros((rows, LANES), F32) for _ in range(tiles)))


def scores_of(act, ends, first, inner, state, length):
    def part(k):
        return act[0, :, inner + k * state : inner + (k + 1) * state]

    same = same_document(first, ends, length)
    below = triangle(length, lambda r, c: r > c)
    above = triangle(length, lambda r, c: r < c)
    return part, same, below, above


def inside_kernel(dims, place, lengths, act, run, late_rows, inside):
    length, inner, heads, state, _, _ = dims
    head_size = inner // heads
    per_tile = LANES // head_size
    ends = bounds_of(lengths, pl.program_id(0))
    part, same, below, above = scores_of(act, ends, place[0] * length, inner, state, length)
    scores = jnp.where(below & same, dot(part(1), part(0), 1, 1), 0.0) + jnp.where(
        above & same, dot(part(3), part(2), 1, 1), 0.0
    )
    run_at = run[0]
    lane = lax.broadcasted_iota(jnp.int32, (length, LANES), 1) // head_size
    for t in range(inner // LANES):
        top, low = split(act[0, :, t * LANES : (t + 1) * LANES])
        pair = jnp.concatenate([top, low], axis=1)
        total = jnp.zeros((length, LANES), F32)
        for k in range(per_tile):
            h = t * per_tile + k
            weights = jnp.exp(
                jnp.where(
                    below,
                    run_at[:, h : h + 1] - late_rows[0, h : h + 1, :],
                    run_at[:, heads + h : heads + h + 1]
                    - late_rows[0, heads + h : heads + h + 1, :],
                )
            )
            m_top, m_low = split(scores * weights)
            wide = dot_bf16(m_top, pair)
            now = wide[:, :LANES] + wide[:, LANES:] + dot_bf16(m_low, top)
            total = jnp.where(lane == k, now, total)
        inside[0, :, t * LANES : (t + 1) * LANES] = total


def unpack(pay, into, tiles, rows, state):
    pieces = state // rows
    for d in range(2):
        for j in range(pieces):
            for t in range(tiles):
                into[d, j * rows : (j + 1) * rows, t * LANES : (t + 1) * LANES] = pay[
                    d * pieces + j, t * rows : (t + 1) * rows, :
                ]


def join_kernel(
    dims, inside, pay, act, reach, gate, back, direct, postnorm, mixed_y, sums, states
):
    length, inner, heads, state, _, rows = dims
    head_size = inner // heads
    both = 2 * heads
    per_tile = WIDE // head_size
    unpack(pay, states.at[0], inner // LANES, rows, state)
    reach_halves = halves(reach[0])
    readers = [left3(act[0, :, inner + k * state : inner + (k + 1) * state]) for k in (1, 3)]
    squares = jnp.zeros((length, WIDE), F32)
    crossed = jnp.zeros((length, WIDE), F32)
    for t in range(inner // WIDE):
        at = slice(t * WIDE, (t + 1) * WIDE)
        total = inside[0, :, at] + direct[:, at] * act[0, :, at]
        for d in range(2):
            grow = spread(d * heads + t * per_tile, head_size, both)
            total = total + dot_bf16(readers[d], right3(states[0, d, :, at])) * dot_bf16(
                reach_halves, grow
            )
        mixed_y[0, :, at] = total
        gate_now = gate[0, EDGE : EDGE + length, at]
        gated = total * (gate_now * sigmoid(gate_now))
        squares = squares + gated * gated
        crossed = crossed + gated * postnorm[:, at] * back[0, :, at]
    lane = lax.broadcasted_iota(jnp.int32, (length, LANES), 1)
    sums[0] = jnp.where(
        lane == 0,
        jnp.sum(squares, axis=1, keepdims=True),
        jnp.sum(crossed, axis=1, keepdims=True),
    )


def norm_of(sums, peer_sums, inner_all, length):
    both_sums = sums[0] + peer_sums[0]
    q = lax.rsqrt(both_sums[:, 0:1] / inner_all + EPSILON)
    pull = both_sums[:, 1:2] * (q * q * q) / inner_all
    return (
        jnp.broadcast_to(q, (length, LANES)),
        jnp.broadcast_to(pull, (length, LANES)),
    )


def turn_kernel(
    dims,
    inner_all,
    sums,
    peer_sums,
    mixed_y,
    gate,
    back,
    maps_t,
    reach,
    postnorm,
    grad_y,
    normal,
    pay,
):
    length, inner, heads, state, _, rows = dims
    head_size = inner // heads
    both = 2 * heads
    per_tile = WIDE // head_size
    pieces = state // rows
    q, pull = norm_of(sums, peer_sums, inner_all, length)
    reach_halves = halves(reach[0])
    readers = [stacked(maps_t[0, k * state : (k + 1) * state]) for k in (1, 3)]
    for t in range(inner // WIDE):
        upstreams = []
        for k in range(WIDE // LANES):
            at = slice(t * WIDE + k * LANES, t * WIDE + (k + 1) * LANES)
            gate_now = gate[0, EDGE : EDGE + length, at]
            opened = gate_now * sigmoid(gate_now)
            gated = mixed_y[0, :, at] * opened
            post = postnorm[:, at]
            upstream = (q * back[0, :, at] * post - pull * gated) * opened
            grad_y[0, :, at] = upstream
            normal[0, :, at] = gated * post * q
            upstreams.append(upstream)
        upstream = jnp.concatenate(upstreams, axis=1)
        for d in range(2):
            grow = spread(d * heads + t * per_tile, head_size, both)
            seed = product_of_stack(readers[d], upstream * dot_bf16(reach_halves, grow), state)
            put_states(pay, d, t, seed, pieces, rows)


def side_kernel(
    dims,
    inner_all,
    sums,
    peer_sums,
    mixed_y,
    gate,
    back,
    act,
    grad_y,
    postnorm,
    grad_gate,
    smalls,
):
    length, inner, heads, _, _, _ = dims
    q, pull = norm_of(sums, peer_sums, inner_all, length)
    grad_gate[0, :EDGE] = jnp.zeros((EDGE, inner), F32)
    grad_gate[0, EDGE + length :] = jnp.zeros((EDGE, inner), F32)
    smalls[0] = jnp.zeros((EDGE, inner), F32)
    for t in range(inner // LANES):
        at = slice(t * LANES, (t + 1) * LANES)
        y = mixed_y[0, :, at]
        gate_now = gate[0, EDGE : EDGE + length, at]
        chance = sigmoid(gate_now)
        gated = y * (gate_now * chance)
        scaled = q * back[0, :, at]
        grad_gated = scaled * postnorm[:, at] - pull * gated
        grad_gate[0, EDGE : EDGE + length, at] = (
            grad_gated * y * (chance * (1.0 + gate_now * (1.0 - chance)))
        )
        smalls[0, 0:1, at] = jnp.sum(scaled * gated, axis=0, keepdims=True)
        smalls[0, 1:2, at] = jnp.sum(grad_y[0, :, at] * act[0, :, at], axis=0, keepdims=True)


def inside_back_kernel(
    dims,
    place,
    lengths,
    act,
    grad_y,
    late,
    run_rows,
    reach,
    states,
    direct,
    grad_signal,
    grad_maps,
    own,
    column_sums,
    read_parts,
):
    length, inner, heads, state, _, _ = dims
    head_size = inner // heads
    per_tile = LANES // head_size
    both = 2 * heads
    ends = bounds_of(lengths, pl.program_id(0))
    part, same, below, above = scores_of(act, ends, place[0] * length, inner, state, length)
    scores = jnp.where(above & same, dot(part(0), part(1), 1, 1), 0.0) + jnp.where(
        below & same, dot(part(2), part(3), 1, 1), 0.0
    )
    late_at = late[0]
    lane = lax.broadcasted_iota(jnp.int32, (length, LANES), 1)
    write_sums = jnp.zeros((length, LANES), F32)
    grad_scores = jnp.zeros((length, length), F32)
    zero = jnp.zeros((length, LANES), BF16)
    for t in range(inner // LANES):
        at = slice(t * LANES, (t + 1) * LANES)
        s_top, s_low = split(act[0, :, at])
        g_top, g_low = split(grad_y[0, :, at])
        pair = jnp.concatenate([g_top, g_low], axis=1)
        two = jnp.concatenate([g_top, g_top], axis=1)
        total = jnp.zeros((length, LANES), F32)
        for k in range(per_tile):
            h = t * per_tile + k
            weights = jnp.exp(
                jnp.where(
                    above,
                    run_rows[0, h : h + 1, :] - late_at[:, h : h + 1],
                    run_rows[0, heads + h : heads + h + 1, :]
                    - late_at[:, heads + h : heads + h + 1],
                )
            )
            mine = lane // head_size == k
            i_top = jnp.where(mine, s_top, zero)
            i_low = jnp.where(mine, s_low, zero)
            overlap = dot_bf16(jnp.concatenate([i_top, i_low], axis=1), two, 1, 1) + dot_bf16(
                i_top, g_low, 1, 1
            )
            product = weights * overlap
            grad_scores = grad_scores + product
            whole = product * scores
            ahead = jnp.where(above, whole, 0.0)
            ahead_writes = jnp.sum(ahead, axis=1, keepdims=True)
            all_writes = jnp.sum(whole, axis=1, keepdims=True)
            write_sums = jnp.where(lane == h, ahead_writes, write_sums)
            write_sums = jnp.where(lane == heads + h, all_writes - ahead_writes, write_sums)
            ahead_reads = jnp.sum(ahead, axis=0, keepdims=True)
            read_parts[h : h + 1, :] = ahead_reads
            read_parts[heads + h : heads + h + 1, :] = (
                jnp.sum(whole, axis=0, keepdims=True) - ahead_reads
            )
            m_top, m_low = split(scores * weights)
            wide = dot_bf16(m_top, pair)
            now = wide[:, :LANES] + wide[:, LANES:] + dot_bf16(m_low, g_top)
            total = jnp.where(mine, now, total)
        grad_signal[0, :, at] = total + direct[:, at] * grad_y[0, :, at]

    writes = write_sums[:, :both]
    column_sums[0] = writes
    total_own = flip_back(read_parts[...]) - writes
    reach_halves = halves(reach[0])
    per_wide = WIDE // head_size
    for d in range(2):
        side = (above, below)[d]
        grads = jnp.where(side & same, grad_scores, 0.0)
        reader = part(2 * d + 1)
        reader3 = left3(reader)
        grad_reader = dot(grads, part(2 * d), 0, 0)
        for t in range(inner // WIDE):
            at = slice(t * WIDE, (t + 1) * WIDE)
            first = d * heads + t * per_wide
            before = states[0, d, :, at]
            reached = grad_y[0, :, at] * dot_bf16(
                reach_halves, spread(first, head_size, both)
            )
            seen = dot_bf16(reader3, right3(before))
            total_own = total_own + dot_bf16(
                halves(reached * seen), gather_heads(first, head_size, both)
            )
            grad_reader = grad_reader + product_with(reached, stacked(before), state)
        grad_maps[0, :, 2 * d * state : (2 * d + 1) * state] = dot(grads, reader)
        grad_maps[0, :, (2 * d + 1) * state : (2 * d + 2) * state] = grad_reader
    own[0] = total_own


def product_with(x, stack, size):
    top, low = split(x)
    twice = dot_bf16(top, stack, 1, 1)
    return twice[:, :size] + twice[:, size:] + dot_bf16(low, stack[:size], 1, 1)


def flip_back(x):
    size = x.shape[0]
    one = triangle(size, lambda r, c: r == c).astype(BF16)
    a, b, c = split3(x)
    return dot_bf16(a, one, 0, 0) + dot_bf16(b, one, 0, 0) + dot_bf16(c, one, 0, 0)


def fold_rows(x):
    total = x[:EDGE]
    for r in range(EDGE, x.shape[0], EDGE):
        total = total + x[r : r + EDGE]
    return total


def end_kernel(
    dims,
    place,
    lengths,
    pay,
    act,
    z_in,
    tail,
    conv,
    states,
    keep,
    grad_inside,
    grad_maps,
    own,
    column_sums,
    mixed,
    taps,
    decays,
    grad_values,
    grad_states,
    grad_raw,
    smalls,
    later,
    grad_act,
    documents,
    masks,
):
    length, inner, heads, state, reach_cells, rows = dims
    head_size = inner // heads
    both = 2 * heads
    per_tile = WIDE // head_size
    width = inner + 4 * state
    offsets_count = 2 * reach_cells + 1
    long = length + 2 * EDGE
    first_row = EDGE - reach_cells
    unpack(pay, later, inner // LANES, rows, state)
    ends = bounds_of(lengths, pl.program_id(0))
    fill_masks(masks, documents, place[0] * length, ends, EDGE, length, reach_cells)

    tail_halves = halves(tail[0])
    leave = jnp.zeros((length, both), F32)
    through = jnp.zeros((1, both), F32)
    for d in range(2):
        writer3 = left3(act[0, :, inner + 2 * d * state : inner + (2 * d + 1) * state])
        grad_writer = grad_maps[0, :, 2 * d * state : (2 * d + 1) * state]
        for t in range(inner // WIDE):
            at = slice(t * WIDE, (t + 1) * WIDE)
            first = d * heads + t * per_tile
            fold = gather_heads(first, head_size, both)
            after = later[d, :, at]
            tails = dot_bf16(tail_halves, spread(first, head_size, both))
            weighted = act[0, :, at] * tails
            pulled = dot_bf16(writer3, right3(after))
            base = grad_inside[0, :, at] if d == 0 else grad_act[:, at]
            grad_act[:, at] = base + tails * pulled
            leave = leave + dot_bf16(halves(weighted * pulled), fold)
            grad_writer = grad_writer + product_with(weighted, stacked(after), state)
            crossed = jnp.sum(states[0, d, :, at] * after, axis=0, keepdims=True)
            through = (
                through + dot_bf16(halves(jnp.broadcast_to(crossed, (EDGE, WIDE))), fold)[:1]
            )
        at = inner + 2 * d * state
        grad_act[:, at : at + state] = grad_writer
        grad_act[:, at + state : at + 2 * state] = grad_maps[
            0, :, (2 * d + 1) * state : (2 * d + 2) * state
        ]

    grad_values[0] = jnp.zeros((long, inner), F32)
    grad_states[0] = jnp.zeros((long, width - inner), F32)
    def column(t, _, into, shift):
        at = pl.ds(pl.multiple_of(t * WIDE, WIDE), WIDE)
        put = pl.ds(pl.multiple_of((t - shift) * WIDE, WIDE), WIDE)
        bias_sum = jnp.zeros((EDGE, WIDE), F32)
        tap_sums = [jnp.zeros((EDGE, WIDE), F32) for _ in range(offsets_count)]
        for r in range(0, length, CHUNK):
            value = conv[0, r : r + CHUNK, at]
            chance = sigmoid(value)
            grad = grad_act[r : r + CHUNK, at] * (chance * (1.0 + value * (1.0 - chance)))
            bias_sum = bias_sum + fold_rows(grad)
            for o in range(offsets_count):
                begin = first_row + o + r
                mask = masks[o, r : r + CHUNK]
                now = grad * jnp.concatenate([mask] * (WIDE // LANES), axis=1)
                into[0, begin : begin + CHUNK, put] += now * taps[o : o + 1, at]
                tap_sums[o] = tap_sums[o] + fold_rows(now * mixed[0, begin : begin + CHUNK, at])
        smalls[0, offsets_count : offsets_count + 1, at] = jnp.sum(bias_sum, axis=0, keepdims=True)
        for o in range(offsets_count):
            smalls[0, o : o + 1, at] = jnp.sum(tap_sums[o], axis=0, keepdims=True)
        return 0

    split_at = inner // WIDE
    lax.fori_loop(0, split_at, partial(column, into=grad_values, shift=0), 0)
    lax.fori_loop(
        split_at, width // WIDE, partial(column, into=grad_states, shift=split_at), 0
    )

    ahead = lax.broadcasted_iota(jnp.int32, (length, both), 1) < heads
    from_here = triangle(length, lambda r, c: c >= r).astype(BF16)
    to_here = triangle(length, lambda r, c: c <= r).astype(BF16)
    before_here = triangle(length, lambda r, c: c < r).astype(BF16)
    after_here = triangle(length, lambda r, c: c > r).astype(BF16)
    entered = own[0]
    grad_decay = (
        jnp.where(
            ahead,
            exact_sum(from_here, entered) + exact_sum(before_here, leave),
            exact_sum(to_here, entered) + exact_sum(after_here, leave),
        )
        + through * keep[0]
    )
    z = z_in[0]
    step = softplus(z)
    chance = sigmoid(z)
    rates = jnp.exp(jnp.concatenate([decays[0:1, :], decays[1:2, :]], axis=1))
    ratio = jnp.where(step > 1e-30, chance / jnp.maximum(step, 1e-30), 1.0)
    grad_z = (leave + column_sums[0]) * ratio - rates * grad_decay * chance
    grad_raw[0, :EDGE] = jnp.zeros((EDGE, both), F32)
    grad_raw[0, EDGE + length :] = jnp.zeros((EDGE, both), F32)
    grad_raw[0, EDGE : EDGE + length] = grad_z
    smalls[0, EDGE:, :] = jnp.zeros((EDGE, width), F32)
    smalls[0, EDGE : EDGE + 1, :both] = jnp.sum(grad_z, axis=0, keepdims=True)
    smalls[0, EDGE + 1 : EDGE + 2, :both] = -rates * jnp.sum(
        step * grad_decay, axis=0, keepdims=True
    )


def pack_kernel(
    dims, rest, own_states, smalls, side_smalls, grad_stepper, grad_prenorm, packed
):
    _, inner, _, state, reach_cells, _ = dims
    both = grad_stepper.shape[0]
    small = smalls[0]
    side = side_smalls[0]
    for i in range(1, smalls.shape[0]):
        small = small + smalls[i]
        side = side + side_smalls[i]
    at = rest.shape[0]
    packed[:at] = rest[...]
    cut = own_states.shape[0]
    packed[at : at + cut] = own_states[...]
    at += cut
    packed[at:] = jnp.zeros((packed.shape[0] - at, inner), F32)
    packed[at : at + both] = grad_stepper[...]
    at += both
    packed[at : at + EDGE] = small[:EDGE, :inner]
    packed[at + EDGE : at + 2 * EDGE, : 4 * state] = small[:EDGE, inner:]
    packed[at + 2 * EDGE : at + 2 * EDGE + 2, :] = side[:2]
    packed[at + 2 * EDGE + 2 : at + 2 * EDGE + 4, :] = small[EDGE : EDGE + 2, :inner]
    packed[at + 2 * EDGE + 4 : at + 2 * EDGE + 5, :] = grad_prenorm[...]


def unpack_kernel(
    dims,
    mine,
    peer,
    filters,
    shifts,
    kernels,
    biases,
    postnorm,
    direct,
    offsets,
    decays,
    prenorm,
):
    _, inner, heads, state, reach_cells, _ = dims
    head_size = inner // heads
    count = 2 * reach_cells + 1
    at = 2 * state + 2 * heads
    filters[...] = mine[at : at + count]
    shifts[...] = mine[at + count]
    at += EDGE
    shared = mine[at : at + EDGE, : 4 * state] + peer[at : at + EDGE, : 4 * state]
    for k in range(4):
        kernels[:, k, :] = shared[:count, k * state : (k + 1) * state]
        biases[k : k + 1, :] = shared[count:, k * state : (k + 1) * state]
    at += EDGE
    postnorm[...] = mine[at]
    fold = jnp.zeros((EDGE, heads), F32)
    for t in range(inner // WIDE):
        row = jnp.broadcast_to(mine[at + 1 : at + 2, t * WIDE : (t + 1) * WIDE], (EDGE, WIDE))
        fold = fold + dot_bf16(
            jnp.concatenate(split3(row), axis=1),
            gather_heads(t * (WIDE // head_size), head_size, heads, 3),
        )
    direct[...] = fold[0]
    for d in range(2):
        offsets[d : d + 1, :] = mine[at + 2 : at + 3, d * heads : (d + 1) * heads]
        decays[d : d + 1, :] = mine[at + 3 : at + 4, d * heads : (d + 1) * heads]
    prenorm[...] = mine[at + 4] + peer[at + 4]


def finish_kernel(bits, own_first, came_first, own_second, came_second, values, last):
    half = own_first.shape[0]
    low = bits[0] == 0
    values[:half] = jnp.where(low, own_first[...], came_first[...])
    values[half : 2 * half] = jnp.where(low, came_first[...], own_first[...])
    low = bits[1] == 0
    values[2 * half :] = jnp.where(low, own_second[...], came_second[...])
    last[...] = jnp.where(low, came_second[...], own_second[...])


def exchange(x, axis, bit):
    peers = lax.axis_size(axis)
    return lax.ppermute(x, axis, [(i, i ^ (1 << bit)) for i in range(peers)])


def bit_of(place, bit):
    return (place >> bit) & 1


def join_halves(mine, own, other):
    return jnp.where(
        mine == 0, jnp.concatenate([own, other]), jnp.concatenate([other, own])
    )


def tie(*arrays):
    return lax.optimization_barrier(arrays)


class PairTotal:
    def __init__(self, axis):
        self.axis = axis
        self.place = lax.axis_index(axis)
        bits = lax.axis_size(axis).bit_length() - 1
        down = [(0, 1), (1, 0), (2,)] + [(bit,) for bit in range(3, bits)]
        self.steps = [("halve", order) for order in down]
        self.steps += [("join", order) for order in reversed(down)]
        self.at = 0
        self.now = [None, None]
        self.came = [None, None]

    def mine(self, bit):
        return bit_of(self.place, bit)

    def outgoing(self, k=None):
        kind, order = self.steps[self.at]
        which = range(len(order)) if k is None else (k,)
        out = []
        for i in which:
            x, mine = self.now[i], self.mine(order[i])
            if kind == "join":
                out.append(x)
            elif order == (2,):
                out.append(jnp.where(mine == 0, self.now[1], self.now[0]))
            else:
                half = x.shape[0] // 2
                out.append(lax.dynamic_slice_in_dim(x, (1 - mine) * half, half))
        return out

    def go(self, sent, k=None):
        _, order = self.steps[self.at]
        which = range(len(order)) if k is None else (k,)
        for i, x in zip(which, sent):
            self.came[i] = exchange(x, self.axis, order[i])

    def take(self, *others):
        kind, order = self.steps[self.at]
        came = [c for c in self.came[: len(order)]]
        if others:
            came = list(tie(*came, *others)[: len(order)])
        now = []
        for i, bit in enumerate(order):
            x, mine, c = self.now[i], self.mine(bit), came[i]
            if order == (2,):
                if kind == "halve":
                    now = [jnp.where(mine == 0, self.now[0], self.now[1]) + c]
                else:
                    now = [jnp.where(mine == 0, x, c), jnp.where(mine == 0, c, x)]
            elif kind == "halve":
                half = x.shape[0] // 2
                now.append(lax.dynamic_slice_in_dim(x, mine * half, half) + c)
            else:
                now.append(join_halves(mine, x, c))
        self.now = now
        self.at += 1

    def ahead_of(self, array, k=None):
        sent = self.outgoing(k)
        self.go(sent, k)
        return tie(array, *sent)[0]

    @property
    def done(self):
        return self.at == len(self.steps)

    def turn(self, *others):
        if self.done:
            return self.now[0]
        self.take(*others)
        if not self.done:
            sent = self.outgoing()
            self.go(sent)
            return sent[0]
        return self.now[0]


def local(
    hidden,
    lengths,
    prenorm,
    gating,
    values,
    states,
    stepper,
    offsets,
    decays,
    filters,
    shifts,
    kernels,
    biases,
    direct,
    postnorm,
    output,
    cotangent,
):
    micro, length, model = hidden.shape
    inner = gating.shape[1]
    heads = direct.shape[0]
    both = 2 * heads
    head_size = inner // heads
    state = states.shape[2]
    reach_cells = (filters.shape[0] - 1) // 2
    count = 2 * reach_cells + 1
    peers = lax.axis_size("seq")
    place = lax.axis_index("seq")
    head_place = lax.axis_index("head")
    inner_all = inner * lax.axis_size("head")
    rows = micro * 2 * state // peers
    tiles = inner // LANES
    dims = (length, inner, heads, state, reach_cells, rows)
    maps_width = 4 * state
    width = inner + maps_width
    long = length + 2 * EDGE
    half_peers = peers // micro
    where = place.reshape(1).astype(jnp.int32)

    up = [(i, i + 1) for i in range(peers - 1)]
    down = [(i + 1, i) for i in range(peers - 1)]
    swap = [(0, 1), (1, 0)]
    before = lax.ppermute(hidden[:, length - EDGE :], "seq", up)
    after = lax.ppermute(hidden[:, :EDGE], "seq", down)
    states_flat = states.reshape(model, maps_width)
    stepper_flat = stepper.reshape(model, both)
    direct_row = jnp.repeat(direct, head_size)[None]
    post_row = postnorm[None]

    def spec(*block):
        return pl.BlockSpec((1,) + block, lambda i: (i,) + (0,) * len(block))

    def fixed(*block):
        return pl.BlockSpec(block, lambda i: (0,) * len(block))

    def shape(*dims):
        return jax.ShapeDtypeStruct(dims, F32)

    smem = pl.BlockSpec(memory_space=pltpu.SMEM)
    vmem = pl.BlockSpec(memory_space=pltpu.VMEM)
    packed = tiles * rows + EDGE
    pay_spec = pl.BlockSpec((half_peers, packed, LANES), lambda i: (i, 0, 0))
    plain_spec = pl.BlockSpec((half_peers, tiles * rows, LANES), lambda i: (i, 0, 0))
    small = spec(length, both)
    wide = spec(length, inner)
    acts = spec(length, width)
    row = fixed(1, inner)
    flat = spec(both, length)

    (
        normed,
        mixed,
        conv,
        act,
        maps_t,
        z,
        run,
        late,
        run_rows,
        late_rows,
        reach,
        tail,
        keep,
        taps,
        pay,
    ) = pl.pallas_call(
        partial(front_kernel, dims),
        grid=(micro,),
        in_specs=[
            smem,
            smem,
            spec(EDGE, model),
            spec(length, model),
            spec(EDGE, model),
            fixed(model),
            fixed(model, inner),
            fixed(model, maps_width),
            fixed(model, both),
            fixed(count, inner),
            fixed(count, 4, state),
            fixed(inner),
            fixed(4, state),
            fixed(2, heads),
            fixed(2, heads),
        ],
        out_specs=[
            spec(long, model),
            spec(long, width),
            acts,
            acts,
            spec(maps_width, length),
            small,
            small,
            small,
            flat,
            flat,
            small,
            small,
            spec(1, both),
            fixed(EDGE, width),
            pay_spec,
        ],
        out_shape=[
            shape(micro, long, model),
            shape(micro, long, width),
            shape(micro, length, width),
            shape(micro, length, width),
            shape(micro, maps_width, length),
            shape(micro, length, both),
            shape(micro, length, both),
            shape(micro, length, both),
            shape(micro, both, length),
            shape(micro, both, length),
            shape(micro, length, both),
            shape(micro, length, both),
            shape(micro, 1, both),
            shape(EDGE, width),
            shape(peers, packed, LANES),
        ],
        scratch_shapes=[
            pltpu.VMEM((long + 2 * EDGE, LANES), jnp.int32),
            pltpu.VMEM((count, length, LANES), F32),
        ],
        compiler_params=PARAMS,
        name="front",
    )(
        where,
        lengths,
        before,
        hidden,
        after,
        prenorm,
        values,
        states_flat,
        stepper_flat,
        filters,
        kernels,
        shifts,
        biases,
        offsets,
        decays,
    )

    direction = lax.rem(place // (peers // (2 * micro)), 2)

    def prefix(terms, keeps, flipped):
        return pl.pallas_call(
            partial(prefix_kernel, tiles, rows),
            grid=(1,),
            in_specs=[smem, fixed(*terms.shape), fixed(*keeps.shape)],
            out_specs=fixed(peers, tiles * rows, LANES),
            out_shape=shape(peers, tiles * rows, LANES),
            compiler_params=PARAMS,
            name="prefix",
        )(flipped.reshape(1).astype(jnp.int32), terms, keeps)

    def swap_all(x):
        return lax.all_to_all(x, "seq", 0, 0, tiled=True)

    terms = swap_all(pay)
    arrived = swap_all(prefix(terms, terms, direction))

    normed_flat = normed.reshape(micro * long, model)
    cotangent_flat = cotangent.reshape(micro * length, model)
    back = dot(cotangent_flat, output, 1, 1).reshape(micro, length, inner)
    inside = pl.pallas_call(
        partial(inside_kernel, dims),
        grid=(micro,),
        in_specs=[smem, smem, acts, small, flat],
        out_specs=wide,
        out_shape=shape(micro, length, inner),
        compiler_params=PARAMS,
        name="inside",
    )(where, lengths, act, run, late_rows)
    gate = dot(normed_flat, gating).reshape(micro, long, inner)

    gates = spec(long, inner)
    sum_spec = spec(length, LANES)
    state_spec = spec(2, state, inner)
    mixed_y, sums, before_states = pl.pallas_call(
        partial(join_kernel, dims),
        grid=(micro,),
        in_specs=[wide, plain_spec, acts, small, gates, wide, row, row],
        out_specs=[wide, sum_spec, state_spec],
        out_shape=[
            shape(micro, length, inner),
            shape(micro, length, LANES),
            shape(micro, 2, state, inner),
        ],
        compiler_params=PARAMS,
        name="join",
    )(inside, arrived, act, reach, gate, back, direct_row, post_row)
    peer_sums = lax.ppermute(sums, "head", swap)

    grad_y, normal, pay_back = pl.pallas_call(
        partial(turn_kernel, dims, inner_all),
        grid=(micro,),
        in_specs=[
            sum_spec,
            sum_spec,
            wide,
            gates,
            wide,
            spec(maps_width, length),
            small,
            row,
        ],
        out_specs=[wide, wide, plain_spec],
        out_shape=[
            shape(micro, length, inner),
            shape(micro, length, inner),
            shape(peers, tiles * rows, LANES),
        ],
        compiler_params=PARAMS,
        name="turn",
    )(sums, peer_sums, mixed_y, gate, back, maps_t, reach, post_row)

    back_terms = swap_all(pay_back)

    normal_flat = normal.reshape(micro * length, inner)
    grad_output = dot(normal_flat, cotangent_flat, 0, 0)

    grad_gate, side_smalls = pl.pallas_call(
        partial(side_kernel, dims, inner_all),
        grid=(micro,),
        in_specs=[sum_spec, sum_spec, wide, gates, wide, acts, wide, row],
        out_specs=[gates, spec(EDGE, inner)],
        out_shape=[shape(micro, long, inner), shape(micro, EDGE, inner)],
        compiler_params=PARAMS,
        name="side",
    )(sums, peer_sums, mixed_y, gate, back, act, grad_y, post_row)
    grad_gate_flat = grad_gate.reshape(micro * long, inner)
    grad_gating = dot(normed_flat, grad_gate_flat, 0, 0)
    early = PairTotal("seq")
    early.now = [grad_output, grad_gating]
    back_terms = early.ahead_of(back_terms)
    prefixed = prefix(back_terms, terms, 1 - direction)
    back_arrived = swap_all(prefixed)
    grad_y = tie(grad_y, prefixed)[0]

    grad_inside, grad_maps, own, column_sums = pl.pallas_call(
        partial(inside_back_kernel, dims),
        grid=(micro,),
        in_specs=[smem, smem, acts, wide, small, flat, small, state_spec, row],
        out_specs=[wide, spec(length, maps_width), small, small],
        out_shape=[
            shape(micro, length, inner),
            shape(micro, length, maps_width),
            shape(micro, length, both),
            shape(micro, length, both),
        ],
        scratch_shapes=[pltpu.VMEM((both, length), F32)],
        compiler_params=PARAMS,
        name="inside_back",
    )(where, lengths, act, grad_y, late, run_rows, reach, before_states, direct_row)

    grad_normed_gate = dot(grad_gate_flat, gating, 1, 1)
    back_arrived = tie(back_arrived, own, grad_normed_gate)[0]

    grad_mixed, grad_mixed_maps, grad_raw, smalls = pl.pallas_call(
        partial(end_kernel, dims),
        grid=(micro,),
        in_specs=[
            smem,
            smem,
            plain_spec,
            acts,
            small,
            small,
            acts,
            state_spec,
            spec(1, both),
            wide,
            spec(length, maps_width),
            small,
            small,
            spec(long, width),
            fixed(EDGE, width),
            fixed(2, heads),
        ],
        out_specs=[gates, spec(long, maps_width), spec(long, both), spec(2 * EDGE, width)],
        out_shape=[
            shape(micro, long, inner),
            shape(micro, long, maps_width),
            shape(micro, long, both),
            shape(micro, 2 * EDGE, width),
        ],
        scratch_shapes=[
            pltpu.VMEM((2, state, inner), F32),
            pltpu.VMEM((length, width), F32),
            pltpu.VMEM((long + 2 * EDGE, LANES), jnp.int32),
            pltpu.VMEM((count, length, LANES), F32),
        ],
        compiler_params=PARAMS,
        name="end",
    )(
        where,
        lengths,
        back_arrived,
        act,
        z,
        tail,
        conv,
        before_states,
        keep,
        grad_inside,
        grad_maps,
        own,
        column_sums,
        mixed,
        taps,
        decays,
    )
    all_maps = grad_mixed_maps.reshape(micro * long, maps_width)
    all_maps = all_maps + lax.ppermute(all_maps, "head", swap)

    early.take(grad_raw)
    grad_mixed = early.ahead_of(grad_mixed)
    grad_mixed = grad_mixed.reshape(micro * long, inner)
    grad_mixed_maps = grad_mixed_maps.reshape(micro * long, maps_width)
    grad_raw = grad_raw.reshape(micro * long, both)
    cut = maps_width // 2
    most = (model + cut + cut) // 2
    assert 3 * (most // 2) == model
    late_total = PairTotal("seq")
    late_total.now = [dot(normed_flat[:, :most], grad_mixed, 0, 0), None]
    grad_normed = (
        dot(grad_mixed, values, 1, 1)
        + dot(grad_mixed_maps, states_flat, 1, 1)
        + grad_normed_gate
        + dot(grad_raw, stepper_flat, 1, 1)
    )
    grad_prenorm = jnp.sum(grad_normed * normed_flat, axis=0, keepdims=True) / prenorm[None]
    early.take(grad_prenorm, late_total.now[0])
    normed_flat = early.ahead_of(normed_flat)
    own_maps = lax.dynamic_slice_in_dim(all_maps, head_place * cut, cut, 1)
    second_late = pl.pallas_call(
        partial(pack_kernel, dims),
        in_specs=[vmem] * 6,
        out_specs=vmem,
        out_shape=shape(most, inner),
        compiler_params=PARAMS,
        name="pack",
    )(
        dot(normed_flat[:, most:], grad_mixed, 0, 0),
        dot(own_maps, normed_flat, 0, 0),
        smalls,
        side_smalls,
        dot(grad_raw, normed_flat, 0, 0),
        grad_prenorm,
    )
    late_total.now[1] = second_late
    grad_normed = late_total.ahead_of(grad_normed)

    grad_normed = grad_normed.reshape(micro, long, model)
    grad_normed = grad_normed + lax.ppermute(grad_normed, "head", swap)
    from_after = lax.ppermute(grad_normed[:, :EDGE], "seq", down)
    from_before = lax.ppermute(grad_normed[:, EDGE + length :], "seq", up)
    grad_here = grad_normed[:, EDGE : EDGE + length] + jnp.concatenate(
        [from_before, jnp.zeros((micro, length - 2 * EDGE, model), F32), from_after], axis=1
    )
    scale = lax.rsqrt(jnp.mean(hidden * hidden, axis=2, keepdims=True) + EPSILON)
    pulled = grad_here * prenorm
    grad_hidden = (
        cotangent
        + scale * pulled
        - hidden * (scale**3 * jnp.sum(pulled * hidden, axis=2, keepdims=True) / model)
    )

    normal_flat = tie(normal_flat, second_late)[0]
    projected = dot(normal_flat, output)
    result = hidden + (projected + lax.ppermute(projected, "head", swap)).reshape(hidden.shape)

    held = second_late
    for mine in "eelelelelllel":
        total = late_total if mine == "l" else early
        held = total.turn(held)
    while late_total.at < len(late_total.steps) - 1:
        held = late_total.turn(held)
        held = early.turn(held)
    while not early.done:
        held = early.turn(held)
    came = tie(*late_total.came, held, grad_hidden, result)[:2]
    _, order = late_total.steps[late_total.at]
    quarter = most // 2
    part = pl.BlockSpec((quarter, WIDE), lambda i: (0, i))
    late_done, last = pl.pallas_call(
        finish_kernel,
        grid=(inner // WIDE,),
        in_specs=[smem] + [part] * 4,
        out_specs=[pl.BlockSpec((3 * quarter, WIDE), lambda i: (0, i)), part],
        out_shape=[shape(3 * quarter, inner), shape(quarter, inner)],
        compiler_params=PARAMS,
        name="finish",
    )(
        jnp.stack([late_total.mine(bit) for bit in order]).astype(jnp.int32),
        late_total.now[0],
        came[0],
        late_total.now[1],
        came[1],
    )
    grad_output, grad_gating = early.now
    peer_last = lax.ppermute(last, "head", swap)
    own_states, other_states = last[:cut], peer_last[:cut]
    grad_states = jnp.where(
        head_place == 0,
        jnp.concatenate([own_states, other_states]),
        jnp.concatenate([other_states, own_states]),
    ).T.reshape(states.shape)
    grad_stepper = last[cut : cut + both].T.reshape(stepper.shape)
    (
        grad_filters,
        grad_shifts,
        grad_kernels,
        grad_biases,
        grad_postnorm,
        grad_direct,
        grad_offsets,
        grad_decays,
        grad_prenorm,
    ) = pl.pallas_call(
        partial(unpack_kernel, dims),
        in_specs=[vmem, vmem],
        out_specs=[vmem] * 9,
        out_shape=[
            shape(count, inner),
            shape(inner),
            shape(*kernels.shape),
            shape(*biases.shape),
            shape(inner),
            shape(heads),
            shape(*offsets.shape),
            shape(*decays.shape),
            shape(model),
        ],
        compiler_params=PARAMS,
        name="unpack",
    )(last, peer_last)
    return (
        result,
        grad_hidden,
        grad_prenorm,
        grad_gating,
        late_done,
        grad_states,
        grad_stepper,
        grad_offsets,
        grad_decays,
        grad_filters,
        grad_shifts,
        grad_kernels,
        grad_biases,
        grad_direct,
        grad_postnorm,
        grad_output,
    )


def solution(mesh):
    in_specs = (
        P(None, "seq", None),
        P(),
        P(),
        P(None, "head"),
        P(None, "head"),
        P(),
        P(None, None, "head"),
        P(None, "head"),
        P(None, "head"),
        P(None, "head"),
        P("head"),
        P(),
        P(),
        P("head"),
        P("head"),
        P("head", None),
        P(None, "seq", None),
    )
    out_specs = (
        P(None, "seq", None),
        P(None, "seq", None),
        P(),
        P(None, "head"),
        P(None, "head"),
        P(),
        P(None, None, "head"),
        P(None, "head"),
        P(None, "head"),
        P(None, "head"),
        P("head"),
        P(),
        P(),
        P("head"),
        P("head"),
        P("head", None),
    )
    return jax.shard_map(local, mesh=mesh, in_specs=in_specs, out_specs=out_specs, check_vma=False)
```

```python
from functools import partial

import jax
import jax.numpy as jnp
from jax import lax
from jax.experimental import pallas as pl
from jax.experimental.pallas import tpu as pltpu
from jax.sharding import PartitionSpec as P

EPSILON = 1e-05
HIGH = lax.Precision.HIGH
F32 = jnp.float32
BF16 = jnp.bfloat16
LANES = 128
WIDE = 256
CHUNK = 128
EDGE = 8
PARAMS = pltpu.CompilerParams(vmem_limit_bytes=53 * 1024 * 1024)


def dot(left, right, over_left=1, over_right=0, precision=HIGH):
    return lax.dot_general(
        left,
        right,
        (((over_left,), (over_right,)), ((), ())),
        precision=precision,
        preferred_element_type=F32,
    )


def split(x):
    top = x.astype(BF16)
    return top, (x - top.astype(F32)).astype(BF16)


def dot_bf16(left, right, over_left=1, over_right=0):
    return lax.dot_general(
        left,
        right,
        (((over_left,), (over_right,)), ((), ())),
        preferred_element_type=F32,
    )


def spread(first, head_size, both):
    rows = lax.broadcasted_iota(jnp.int32, (2 * both, WIDE), 0)
    columns = lax.broadcasted_iota(jnp.int32, (2 * both, WIDE), 1)
    return (lax.rem(rows, both) == first + columns // head_size).astype(BF16)


def gather_heads(first, head_size, both, parts=2):
    rows = lax.broadcasted_iota(jnp.int32, (parts * WIDE, both), 0)
    columns = lax.broadcasted_iota(jnp.int32, (parts * WIDE, both), 1)
    return (columns == first + lax.rem(rows, WIDE) // head_size).astype(BF16)


def split3(x):
    top = x.astype(BF16)
    rest = x - top.astype(F32)
    middle = rest.astype(BF16)
    return top, middle, (rest - middle.astype(F32)).astype(BF16)


def halves(x):
    return jnp.concatenate(split(x), axis=1)


def triangle(size, keep):
    rows = lax.broadcasted_iota(jnp.int32, (size, size), 0)
    columns = lax.broadcasted_iota(jnp.int32, (size, size), 1)
    return keep(rows, columns)


def exact_sum(zero_one, x):
    a, b, c = split3(x)
    return dot_bf16(zero_one, a) + dot_bf16(zero_one, b) + dot_bf16(zero_one, c)


def flip(x):
    size = x.shape[1]
    one = triangle(size, lambda r, c: r == c).astype(BF16)
    a, b, c = split3(x)
    return dot_bf16(one, a, 1, 1) + dot_bf16(one, b, 1, 1) + dot_bf16(one, c, 1, 1)


def sigmoid(x):
    return 1.0 / (1.0 + jnp.exp(-x))


def softplus(x):
    return jnp.maximum(x, 0.0) + jnp.log1p(jnp.exp(-jnp.abs(x)))


def bounds_of(lengths, i):
    ends = []
    total = jnp.int32(0)
    for k in range(lengths.shape[1]):
        total = total + lengths[i, k]
        ends.append(total)
    return ends


def document(places, ends):
    found = sum(jnp.where(places >= end, 1, 0) for end in ends)
    return jnp.where(places < 0, -1, jnp.where(places >= ends[-1], -2, found))


def same_document(first, ends, length):
    rows = document(first + lax.broadcasted_iota(jnp.int32, (length, LANES), 0), ends)
    columns = document(first + lax.broadcasted_iota(jnp.int32, (1, length), 1), ends)
    return jnp.concatenate([rows] * (length // LANES), axis=1) == columns


def fill_masks(masks, documents, first, ends, start, rows, reach_cells):
    total = documents.shape[0]
    documents[...] = document(
        first - 2 * EDGE + lax.broadcasted_iota(jnp.int32, (total, LANES), 0), ends
    )
    center = documents[EDGE + start : EDGE + start + rows]
    for o in range(2 * reach_cells + 1):
        at = EDGE + start + o - reach_cells
        masks[o] = (documents[at : at + rows] == center).astype(F32)


def left3(x):
    top = x.astype(BF16).astype(F32)
    return jnp.concatenate([top, top, x - top], axis=1).astype(BF16)


def right3(x):
    top, low = split(x)
    return jnp.concatenate([top, low, top], axis=0)


def stacked(x):
    return jnp.concatenate(split(x), axis=0)


def front_kernel(
    dims,
    place,
    lengths,
    before,
    hidden,
    after,
    prenorm,
    values,
    states,
    stepper,
    filters,
    kernels,
    shifts,
    biases,
    offsets,
    decays,
    normed,
    mixed,
    conv,
    act,
    maps_t,
    z_out,
    run,
    late,
    run_rows,
    late_rows,
    reach,
    tail,
    keep,
    taps,
    pay,
    documents,
    masks,
):
    length, inner, heads, state, reach_cells, rows = dims
    head_size = inner // heads
    both = 2 * heads
    maps_width = 4 * state
    width = inner + maps_width
    offsets_count = 2 * reach_cells + 1
    i = pl.program_id(0)
    ends = bounds_of(lengths, i)
    first = place[0] * length
    fill_masks(masks, documents, first, ends, EDGE, length, reach_cells)

    gain = prenorm[...][None]

    def norm(x):
        mean = jnp.sum(x * x, axis=1, keepdims=True) / x.shape[1]
        return x * lax.rsqrt(mean + EPSILON) * gain

    normed[0, :EDGE] = norm(before[0])
    for r in range(0, length, 64):
        normed[0, EDGE + r : EDGE + r + 64] = norm(hidden[0, r : r + 64])
    normed[0, EDGE + length :] = norm(after[0])

    whole = normed[0]
    for t in range(inner // WIDE):
        at = slice(t * WIDE, (t + 1) * WIDE)
        mixed[0, :, at] = dot(whole, values[:, at])
    mixed[0, :, inner:] = dot(whole, states[...])
    raw = dot(normed[0, EDGE : EDGE + length], stepper[...])

    taps[:offsets_count, :inner] = filters[...]
    taps[offsets_count:, :inner] = shifts[...][None]
    for k in range(4):
        at = slice(inner + k * state, inner + (k + 1) * state)
        taps[:offsets_count, at] = kernels[:, k, :]
        taps[offsets_count:, at] = biases[k : k + 1, :]

    for t in range(width // WIDE):
        at = slice(t * WIDE, (t + 1) * WIDE)
        for r in range(0, length, CHUNK):
            total = jnp.broadcast_to(taps[offsets_count:, at], (CHUNK, WIDE))
            for o in range(offsets_count):
                begin = EDGE - reach_cells + o + r
                mask = masks[o, r : r + CHUNK]
                total = total + (mixed[0, begin : begin + CHUNK, at] * taps[o : o + 1, at]) * (
                    jnp.concatenate([mask] * (WIDE // LANES), axis=1)
                )
            conv[0, r : r + CHUNK, at] = total
            act[0, r : r + CHUNK, at] = total * sigmoid(total)
    flipped = jnp.transpose(act[0, :, inner:])
    maps_t[0] = flipped

    ahead = lax.broadcasted_iota(jnp.int32, (length, both), 1) < heads
    ahead_row = ahead[:1]
    z = raw + jnp.concatenate([offsets[0:1, :], offsets[1:2, :]], axis=1)
    rates = jnp.exp(jnp.concatenate([decays[0:1, :], decays[1:2, :]], axis=1))
    step = softplus(z)
    decay = -step * rates
    lower = triangle(length, lambda r, c: r >= c).astype(BF16)
    upper = triangle(length, lambda r, c: r <= c).astype(BF16)
    running = jnp.where(ahead, exact_sum(lower, decay), exact_sum(upper, decay))
    edge = jnp.where(ahead_row, running[length - 1 :], running[:1])
    here = document(first + lax.broadcasted_iota(jnp.int32, (length, both), 0), ends)
    seg_before = document(first - 1, ends)
    seg_after = document(first + length, ends)
    seg_first = document(first, ends)
    seg_last = document(first + length - 1, ends)
    enter = (here == jnp.where(ahead, seg_before, seg_after)).astype(F32)
    leave = (here == jnp.where(ahead, seg_last, seg_first)).astype(F32)
    keep_mask = jnp.where(
        ahead_row,
        jnp.where(seg_last == seg_before, 1.0, 0.0),
        jnp.where(seg_first == seg_after, 1.0, 0.0),
    )
    reach_now = enter * jnp.exp(running)
    tail_now = leave * jnp.exp(edge - running) * step
    keep_now = keep_mask * jnp.exp(edge)
    late_now = running - jnp.log(jnp.maximum(step, 1e-37))
    z_out[0] = z
    run[0] = running
    late[0] = late_now
    reach[0] = reach_now
    tail[0] = tail_now
    run_rows[0] = flip(running)
    late_rows[0] = flip(late_now)
    keep[0] = keep_now

    tail_halves = halves(tail_now)
    keep_halves = halves(jnp.broadcast_to(keep_now, (EDGE, both)))
    pieces = state // rows
    per_tile = WIDE // head_size
    for d in range(2):
        maps_now = stacked(flipped[2 * d * state : (2 * d + 1) * state])
        keeps = []
        for t in range(inner // WIDE):
            grow = spread(d * heads + t * per_tile, head_size, both)
            weighted = act[0, :, t * WIDE : (t + 1) * WIDE] * dot_bf16(tail_halves, grow)
            put_states(pay, d, t, product_of_stack(maps_now, weighted, state), pieces, rows)
            keep_wide = dot_bf16(keep_halves, grow)[:1]
            keeps += [keep_wide[:, k * LANES : (k + 1) * LANES] for k in range(WIDE // LANES)]
        tiles = inner // LANES
        keeps.append(jnp.zeros((EDGE - tiles, LANES), F32))
        keep_block = jnp.concatenate(keeps, axis=0)
        for j in range(pieces):
            pay[d * pieces + j, tiles * rows :, :] = keep_block


def product_of_stack(stack, x, size):
    top, low = split(x)
    twice = dot_bf16(stack, top)
    return twice[:size] + twice[size:] + dot_bf16(stack[:size], low)


def put_states(pay, d, t, own, pieces, rows):
    for k in range(WIDE // LANES):
        at = (t * (WIDE // LANES) + k) * rows
        for j in range(pieces):
            pay[d * pieces + j, at : at + rows, :] = own[
                j * rows : (j + 1) * rows, k * LANES : (k + 1) * LANES
            ]


def prefix_kernel(tiles, rows, flipped, terms, keeps, into):
    peers = terms.shape[0]
    back = flipped[0] != 0

    def turn(i, carry):
        at = jnp.where(back, peers - 1 - i, i)
        factor = keeps[at, tiles * rows :, :]
        new = []
        for t in range(tiles):
            into[at, t * rows : (t + 1) * rows, :] = carry[t]
            new.append(
                carry[t] * factor[t : t + 1] + terms[at, t * rows : (t + 1) * rows, :]
            )
        return tuple(new)

    lax.fori_loop(0, peers, turn, tuple(jnp.zeros((rows, LANES), F32) for _ in range(tiles)))


def scores_of(act, ends, first, inner, state, length):
    def part(k):
        return act[0, :, inner + k * state : inner + (k + 1) * state]

    same = same_document(first, ends, length)
    below = triangle(length, lambda r, c: r > c)
    above = triangle(length, lambda r, c: r < c)
    return part, same, below, above


def inside_kernel(dims, place, lengths, act, run, late_rows, inside):
    length, inner, heads, state, _, _ = dims
    head_size = inner // heads
    per_tile = LANES // head_size
    ends = bounds_of(lengths, pl.program_id(0))
    part, same, below, above = scores_of(act, ends, place[0] * length, inner, state, length)
    scores = jnp.where(below & same, dot(part(1), part(0), 1, 1), 0.0) + jnp.where(
        above & same, dot(part(3), part(2), 1, 1), 0.0
    )
    run_at = run[0]
    lane = lax.broadcasted_iota(jnp.int32, (length, LANES), 1) // head_size
    for t in range(inner // LANES):
        top, low = split(act[0, :, t * LANES : (t + 1) * LANES])
        pair = jnp.concatenate([top, low], axis=1)
        total = jnp.zeros((length, LANES), F32)
        for k in range(per_tile):
            h = t * per_tile + k
            weights = jnp.exp(
                jnp.where(
                    below,
                    run_at[:, h : h + 1] - late_rows[0, h : h + 1, :],
                    run_at[:, heads + h : heads + h + 1]
                    - late_rows[0, heads + h : heads + h + 1, :],
                )
            )
            m_top, m_low = split(scores * weights)
            wide = dot_bf16(m_top, pair)
            now = wide[:, :LANES] + wide[:, LANES:] + dot_bf16(m_low, top)
            total = jnp.where(lane == k, now, total)
        inside[0, :, t * LANES : (t + 1) * LANES] = total


def unpack(pay, into, tiles, rows, state):
    pieces = state // rows
    for d in range(2):
        for j in range(pieces):
            for t in range(tiles):
                into[d, j * rows : (j + 1) * rows, t * LANES : (t + 1) * LANES] = pay[
                    d * pieces + j, t * rows : (t + 1) * rows, :
                ]


def join_kernel(
    dims, inside, pay, act, reach, gate, back, direct, postnorm, mixed_y, sums, states
):
    length, inner, heads, state, _, rows = dims
    head_size = inner // heads
    both = 2 * heads
    per_tile = WIDE // head_size
    unpack(pay, states.at[0], inner // LANES, rows, state)
    reach_halves = halves(reach[0])
    readers = [left3(act[0, :, inner + k * state : inner + (k + 1) * state]) for k in (1, 3)]
    squares = jnp.zeros((length, WIDE), F32)
    crossed = jnp.zeros((length, WIDE), F32)
    for t in range(inner // WIDE):
        at = slice(t * WIDE, (t + 1) * WIDE)
        total = inside[0, :, at] + direct[:, at] * act[0, :, at]
        for d in range(2):
            grow = spread(d * heads + t * per_tile, head_size, both)
            total = total + dot_bf16(readers[d], right3(states[0, d, :, at])) * dot_bf16(
                reach_halves, grow
            )
        mixed_y[0, :, at] = total
        gate_now = gate[0, EDGE : EDGE + length, at]
        gated = total * (gate_now * sigmoid(gate_now))
        squares = squares + gated * gated
        crossed = crossed + gated * postnorm[:, at] * back[0, :, at]
    lane = lax.broadcasted_iota(jnp.int32, (length, LANES), 1)
    sums[0] = jnp.where(
        lane == 0,
        jnp.sum(squares, axis=1, keepdims=True),
        jnp.sum(crossed, axis=1, keepdims=True),
    )


def norm_of(sums, peer_sums, inner_all, length):
    both_sums = sums[0] + peer_sums[0]
    q = lax.rsqrt(both_sums[:, 0:1] / inner_all + EPSILON)
    pull = both_sums[:, 1:2] * (q * q * q) / inner_all
    return (
        jnp.broadcast_to(q, (length, LANES)),
        jnp.broadcast_to(pull, (length, LANES)),
    )


def turn_kernel(
    dims,
    inner_all,
    sums,
    peer_sums,
    mixed_y,
    gate,
    back,
    maps_t,
    reach,
    postnorm,
    grad_y,
    normal,
    pay,
):
    length, inner, heads, state, _, rows = dims
    head_size = inner // heads
    both = 2 * heads
    per_tile = WIDE // head_size
    pieces = state // rows
    q, pull = norm_of(sums, peer_sums, inner_all, length)
    reach_halves = halves(reach[0])
    readers = [stacked(maps_t[0, k * state : (k + 1) * state]) for k in (1, 3)]
    for t in range(inner // WIDE):
        upstreams = []
        for k in range(WIDE // LANES):
            at = slice(t * WIDE + k * LANES, t * WIDE + (k + 1) * LANES)
            gate_now = gate[0, EDGE : EDGE + length, at]
            opened = gate_now * sigmoid(gate_now)
            gated = mixed_y[0, :, at] * opened
            post = postnorm[:, at]
            upstream = (q * back[0, :, at] * post - pull * gated) * opened
            grad_y[0, :, at] = upstream
            normal[0, :, at] = gated * post * q
            upstreams.append(upstream)
        upstream = jnp.concatenate(upstreams, axis=1)
        for d in range(2):
            grow = spread(d * heads + t * per_tile, head_size, both)
            seed = product_of_stack(readers[d], upstream * dot_bf16(reach_halves, grow), state)
            put_states(pay, d, t, seed, pieces, rows)


def side_kernel(
    dims,
    inner_all,
    sums,
    peer_sums,
    mixed_y,
    gate,
    back,
    act,
    grad_y,
    postnorm,
    grad_gate,
    smalls,
):
    length, inner, heads, _, _, _ = dims
    q, pull = norm_of(sums, peer_sums, inner_all, length)
    grad_gate[0, :EDGE] = jnp.zeros((EDGE, inner), F32)
    grad_gate[0, EDGE + length :] = jnp.zeros((EDGE, inner), F32)
    smalls[0] = jnp.zeros((EDGE, inner), F32)
    for t in range(inner // LANES):
        at = slice(t * LANES, (t + 1) * LANES)
        y = mixed_y[0, :, at]
        gate_now = gate[0, EDGE : EDGE + length, at]
        chance = sigmoid(gate_now)
        gated = y * (gate_now * chance)
        scaled = q * back[0, :, at]
        grad_gated = scaled * postnorm[:, at] - pull * gated
        grad_gate[0, EDGE : EDGE + length, at] = (
            grad_gated * y * (chance * (1.0 + gate_now * (1.0 - chance)))
        )
        smalls[0, 0:1, at] = jnp.sum(scaled * gated, axis=0, keepdims=True)
        smalls[0, 1:2, at] = jnp.sum(grad_y[0, :, at] * act[0, :, at], axis=0, keepdims=True)


def inside_back_kernel(
    dims,
    place,
    lengths,
    act,
    grad_y,
    late,
    run_rows,
    reach,
    states,
    direct,
    grad_signal,
    grad_maps,
    own,
    column_sums,
    read_parts,
):
    length, inner, heads, state, _, _ = dims
    head_size = inner // heads
    per_tile = LANES // head_size
    both = 2 * heads
    ends = bounds_of(lengths, pl.program_id(0))
    part, same, below, above = scores_of(act, ends, place[0] * length, inner, state, length)
    scores = jnp.where(above & same, dot(part(0), part(1), 1, 1), 0.0) + jnp.where(
        below & same, dot(part(2), part(3), 1, 1), 0.0
    )
    late_at = late[0]
    lane = lax.broadcasted_iota(jnp.int32, (length, LANES), 1)
    write_sums = jnp.zeros((length, LANES), F32)
    grad_scores = jnp.zeros((length, length), F32)
    zero = jnp.zeros((length, LANES), BF16)
    for t in range(inner // LANES):
        at = slice(t * LANES, (t + 1) * LANES)
        s_top, s_low = split(act[0, :, at])
        g_top, g_low = split(grad_y[0, :, at])
        pair = jnp.concatenate([g_top, g_low], axis=1)
        two = jnp.concatenate([g_top, g_top], axis=1)
        total = jnp.zeros((length, LANES), F32)
        for k in range(per_tile):
            h = t * per_tile + k
            weights = jnp.exp(
                jnp.where(
                    above,
                    run_rows[0, h : h + 1, :] - late_at[:, h : h + 1],
                    run_rows[0, heads + h : heads + h + 1, :]
                    - late_at[:, heads + h : heads + h + 1],
                )
            )
            mine = lane // head_size == k
            i_top = jnp.where(mine, s_top, zero)
            i_low = jnp.where(mine, s_low, zero)
            overlap = dot_bf16(jnp.concatenate([i_top, i_low], axis=1), two, 1, 1) + dot_bf16(
                i_top, g_low, 1, 1
            )
            product = weights * overlap
            grad_scores = grad_scores + product
            whole = product * scores
            ahead = jnp.where(above, whole, 0.0)
            ahead_writes = jnp.sum(ahead, axis=1, keepdims=True)
            all_writes = jnp.sum(whole, axis=1, keepdims=True)
            write_sums = jnp.where(lane == h, ahead_writes, write_sums)
            write_sums = jnp.where(lane == heads + h, all_writes - ahead_writes, write_sums)
            ahead_reads = jnp.sum(ahead, axis=0, keepdims=True)
            read_parts[h : h + 1, :] = ahead_reads
            read_parts[heads + h : heads + h + 1, :] = (
                jnp.sum(whole, axis=0, keepdims=True) - ahead_reads
            )
            m_top, m_low = split(scores * weights)
            wide = dot_bf16(m_top, pair)
            now = wide[:, :LANES] + wide[:, LANES:] + dot_bf16(m_low, g_top)
            total = jnp.where(mine, now, total)
        grad_signal[0, :, at] = total + direct[:, at] * grad_y[0, :, at]

    writes = write_sums[:, :both]
    column_sums[0] = writes
    total_own = flip_back(read_parts[...]) - writes
    reach_halves = halves(reach[0])
    per_wide = WIDE // head_size
    for d in range(2):
        side = (above, below)[d]
        grads = jnp.where(side & same, grad_scores, 0.0)
        reader = part(2 * d + 1)
        reader3 = left3(reader)
        grad_reader = dot(grads, part(2 * d), 0, 0)
        for t in range(inner // WIDE):
            at = slice(t * WIDE, (t + 1) * WIDE)
            first = d * heads + t * per_wide
            before = states[0, d, :, at]
            reached = grad_y[0, :, at] * dot_bf16(
                reach_halves, spread(first, head_size, both)
            )
            seen = dot_bf16(reader3, right3(before))
            total_own = total_own + dot_bf16(
                halves(reached * seen), gather_heads(first, head_size, both)
            )
            grad_reader = grad_reader + product_with(reached, stacked(before), state)
        grad_maps[0, :, 2 * d * state : (2 * d + 1) * state] = dot(grads, reader)
        grad_maps[0, :, (2 * d + 1) * state : (2 * d + 2) * state] = grad_reader
    own[0] = total_own


def product_with(x, stack, size):
    top, low = split(x)
    twice = dot_bf16(top, stack, 1, 1)
    return twice[:, :size] + twice[:, size:] + dot_bf16(low, stack[:size], 1, 1)


def flip_back(x):
    size = x.shape[0]
    one = triangle(size, lambda r, c: r == c).astype(BF16)
    a, b, c = split3(x)
    return dot_bf16(a, one, 0, 0) + dot_bf16(b, one, 0, 0) + dot_bf16(c, one, 0, 0)


def fold_rows(x):
    total = x[:EDGE]
    for r in range(EDGE, x.shape[0], EDGE):
        total = total + x[r : r + EDGE]
    return total


def end_kernel(
    dims,
    place,
    lengths,
    pay,
    act,
    z_in,
    tail,
    conv,
    states,
    keep,
    grad_inside,
    grad_maps,
    own,
    column_sums,
    mixed,
    taps,
    decays,
    grad_values,
    grad_states,
    grad_raw,
    smalls,
    later,
    grad_act,
    documents,
    masks,
):
    length, inner, heads, state, reach_cells, rows = dims
    head_size = inner // heads
    both = 2 * heads
    per_tile = WIDE // head_size
    width = inner + 4 * state
    offsets_count = 2 * reach_cells + 1
    long = length + 2 * EDGE
    first_row = EDGE - reach_cells
    unpack(pay, later, inner // LANES, rows, state)
    ends = bounds_of(lengths, pl.program_id(0))
    fill_masks(masks, documents, place[0] * length, ends, EDGE, length, reach_cells)

    tail_halves = halves(tail[0])
    leave = jnp.zeros((length, both), F32)
    through = jnp.zeros((1, both), F32)
    for d in range(2):
        writer3 = left3(act[0, :, inner + 2 * d * state : inner + (2 * d + 1) * state])
        grad_writer = grad_maps[0, :, 2 * d * state : (2 * d + 1) * state]
        for t in range(inner // WIDE):
            at = slice(t * WIDE, (t + 1) * WIDE)
            first = d * heads + t * per_tile
            fold = gather_heads(first, head_size, both)
            after = later[d, :, at]
            tails = dot_bf16(tail_halves, spread(first, head_size, both))
            weighted = act[0, :, at] * tails
            pulled = dot_bf16(writer3, right3(after))
            base = grad_inside[0, :, at] if d == 0 else grad_act[:, at]
            grad_act[:, at] = base + tails * pulled
            leave = leave + dot_bf16(halves(weighted * pulled), fold)
            grad_writer = grad_writer + product_with(weighted, stacked(after), state)
            crossed = jnp.sum(states[0, d, :, at] * after, axis=0, keepdims=True)
            through = (
                through + dot_bf16(halves(jnp.broadcast_to(crossed, (EDGE, WIDE))), fold)[:1]
            )
        at = inner + 2 * d * state
        grad_act[:, at : at + state] = grad_writer
        grad_act[:, at + state : at + 2 * state] = grad_maps[
            0, :, (2 * d + 1) * state : (2 * d + 2) * state
        ]

    grad_values[0] = jnp.zeros((long, inner), F32)
    grad_states[0] = jnp.zeros((long, width - inner), F32)
    def column(t, _, into, shift):
        at = pl.ds(pl.multiple_of(t * WIDE, WIDE), WIDE)
        put = pl.ds(pl.multiple_of((t - shift) * WIDE, WIDE), WIDE)
        bias_sum = jnp.zeros((EDGE, WIDE), F32)
        tap_sums = [jnp.zeros((EDGE, WIDE), F32) for _ in range(offsets_count)]
        for r in range(0, length, CHUNK):
            value = conv[0, r : r + CHUNK, at]
            chance = sigmoid(value)
            grad = grad_act[r : r + CHUNK, at] * (chance * (1.0 + value * (1.0 - chance)))
            bias_sum = bias_sum + fold_rows(grad)
            for o in range(offsets_count):
                begin = first_row + o + r
                mask = masks[o, r : r + CHUNK]
                now = grad * jnp.concatenate([mask] * (WIDE // LANES), axis=1)
                into[0, begin : begin + CHUNK, put] += now * taps[o : o + 1, at]
                tap_sums[o] = tap_sums[o] + fold_rows(now * mixed[0, begin : begin + CHUNK, at])
        smalls[0, offsets_count : offsets_count + 1, at] = jnp.sum(bias_sum, axis=0, keepdims=True)
        for o in range(offsets_count):
            smalls[0, o : o + 1, at] = jnp.sum(tap_sums[o], axis=0, keepdims=True)
        return 0

    split_at = inner // WIDE
    lax.fori_loop(0, split_at, partial(column, into=grad_values, shift=0), 0)
    lax.fori_loop(
        split_at, width // WIDE, partial(column, into=grad_states, shift=split_at), 0
    )

    ahead = lax.broadcasted_iota(jnp.int32, (length, both), 1) < heads
    from_here = triangle(length, lambda r, c: c >= r).astype(BF16)
    to_here = triangle(length, lambda r, c: c <= r).astype(BF16)
    before_here = triangle(length, lambda r, c: c < r).astype(BF16)
    after_here = triangle(length, lambda r, c: c > r).astype(BF16)
    entered = own[0]
    grad_decay = (
        jnp.where(
            ahead,
            exact_sum(from_here, entered) + exact_sum(before_here, leave),
            exact_sum(to_here, entered) + exact_sum(after_here, leave),
        )
        + through * keep[0]
    )
    z = z_in[0]
    step = softplus(z)
    chance = sigmoid(z)
    rates = jnp.exp(jnp.concatenate([decays[0:1, :], decays[1:2, :]], axis=1))
    ratio = jnp.where(step > 1e-30, chance / jnp.maximum(step, 1e-30), 1.0)
    grad_z = (leave + column_sums[0]) * ratio - rates * grad_decay * chance
    grad_raw[0, :EDGE] = jnp.zeros((EDGE, both), F32)
    grad_raw[0, EDGE + length :] = jnp.zeros((EDGE, both), F32)
    grad_raw[0, EDGE : EDGE + length] = grad_z
    smalls[0, EDGE:, :] = jnp.zeros((EDGE, width), F32)
    smalls[0, EDGE : EDGE + 1, :both] = jnp.sum(grad_z, axis=0, keepdims=True)
    smalls[0, EDGE + 1 : EDGE + 2, :both] = -rates * jnp.sum(
        step * grad_decay, axis=0, keepdims=True
    )


def pack_kernel(
    dims, rest, own_states, smalls, side_smalls, grad_stepper, grad_prenorm, packed
):
    _, inner, _, state, reach_cells, _ = dims
    both = grad_stepper.shape[0]
    small = smalls[0]
    side = side_smalls[0]
    for i in range(1, smalls.shape[0]):
        small = small + smalls[i]
        side = side + side_smalls[i]
    at = rest.shape[0]
    packed[:at] = rest[...]
    cut = own_states.shape[0]
    packed[at : at + cut] = own_states[...]
    at += cut
    packed[at:] = jnp.zeros((packed.shape[0] - at, inner), F32)
    packed[at : at + both] = grad_stepper[...]
    at += both
    packed[at : at + EDGE] = small[:EDGE, :inner]
    packed[at + EDGE : at + 2 * EDGE, : 4 * state] = small[:EDGE, inner:]
    packed[at + 2 * EDGE : at + 2 * EDGE + 2, :] = side[:2]
    packed[at + 2 * EDGE + 2 : at + 2 * EDGE + 4, :] = small[EDGE : EDGE + 2, :inner]
    packed[at + 2 * EDGE + 4 : at + 2 * EDGE + 5, :] = grad_prenorm[...]


def unpack_kernel(
    dims,
    mine,
    peer,
    filters,
    shifts,
    kernels,
    biases,
    postnorm,
    direct,
    offsets,
    decays,
    prenorm,
):
    _, inner, heads, state, reach_cells, _ = dims
    head_size = inner // heads
    count = 2 * reach_cells + 1
    at = 2 * state + 2 * heads
    filters[...] = mine[at : at + count]
    shifts[...] = mine[at + count]
    at += EDGE
    shared = mine[at : at + EDGE, : 4 * state] + peer[at : at + EDGE, : 4 * state]
    for k in range(4):
        kernels[:, k, :] = shared[:count, k * state : (k + 1) * state]
        biases[k : k + 1, :] = shared[count:, k * state : (k + 1) * state]
    at += EDGE
    postnorm[...] = mine[at]
    fold = jnp.zeros((EDGE, heads), F32)
    for t in range(inner // WIDE):
        row = jnp.broadcast_to(mine[at + 1 : at + 2, t * WIDE : (t + 1) * WIDE], (EDGE, WIDE))
        fold = fold + dot_bf16(
            jnp.concatenate(split3(row), axis=1),
            gather_heads(t * (WIDE // head_size), head_size, heads, 3),
        )
    direct[...] = fold[0]
    for d in range(2):
        offsets[d : d + 1, :] = mine[at + 2 : at + 3, d * heads : (d + 1) * heads]
        decays[d : d + 1, :] = mine[at + 3 : at + 4, d * heads : (d + 1) * heads]
    prenorm[...] = mine[at + 4] + peer[at + 4]


def finish_kernel(bits, own_first, came_first, own_second, came_second, values, last):
    half = own_first.shape[0]
    low = bits[0] == 0
    values[:half] = jnp.where(low, own_first[...], came_first[...])
    values[half : 2 * half] = jnp.where(low, came_first[...], own_first[...])
    low = bits[1] == 0
    values[2 * half :] = jnp.where(low, own_second[...], came_second[...])
    last[...] = jnp.where(low, came_second[...], own_second[...])


def exchange(x, axis, bit):
    peers = lax.axis_size(axis)
    return lax.ppermute(x, axis, [(i, i ^ (1 << bit)) for i in range(peers)])


def bit_of(place, bit):
    return (place >> bit) & 1


def join_halves(mine, own, other):
    return jnp.where(
        mine == 0, jnp.concatenate([own, other]), jnp.concatenate([other, own])
    )


def tie(*arrays):
    return lax.optimization_barrier(arrays)


class PairTotal:
    def __init__(self, axis):
        self.axis = axis
        self.place = lax.axis_index(axis)
        bits = lax.axis_size(axis).bit_length() - 1
        down = [(0, 1), (1, 0), (2,)] + [(bit,) for bit in range(3, bits)]
        self.steps = [("halve", order) for order in down]
        self.steps += [("join", order) for order in reversed(down)]
        self.at = 0
        self.now = [None, None]
        self.came = [None, None]

    def mine(self, bit):
        return bit_of(self.place, bit)

    def outgoing(self, k=None):
        kind, order = self.steps[self.at]
        which = range(len(order)) if k is None else (k,)
        out = []
        for i in which:
            x, mine = self.now[i], self.mine(order[i])
            if kind == "join":
                out.append(x)
            elif order == (2,):
                out.append(jnp.where(mine == 0, self.now[1], self.now[0]))
            else:
                half = x.shape[0] // 2
                out.append(lax.dynamic_slice_in_dim(x, (1 - mine) * half, half))
        return out

    def go(self, sent, k=None):
        _, order = self.steps[self.at]
        which = range(len(order)) if k is None else (k,)
        for i, x in zip(which, sent):
            self.came[i] = exchange(x, self.axis, order[i])

    def take(self, *others):
        kind, order = self.steps[self.at]
        came = [c for c in self.came[: len(order)]]
        if others:
            came = list(tie(*came, *others)[: len(order)])
        now = []
        for i, bit in enumerate(order):
            x, mine, c = self.now[i], self.mine(bit), came[i]
            if order == (2,):
                if kind == "halve":
                    now = [jnp.where(mine == 0, self.now[0], self.now[1]) + c]
                else:
                    now = [jnp.where(mine == 0, x, c), jnp.where(mine == 0, c, x)]
            elif kind == "halve":
                half = x.shape[0] // 2
                now.append(lax.dynamic_slice_in_dim(x, mine * half, half) + c)
            else:
                now.append(join_halves(mine, x, c))
        self.now = now
        self.at += 1

    def ahead_of(self, array, k=None):
        sent = self.outgoing(k)
        self.go(sent, k)
        return tie(array, *sent)[0]

    @property
    def done(self):
        return self.at == len(self.steps)

    def turn(self, *others):
        if self.done:
            return self.now[0]
        self.take(*others)
        if not self.done:
            sent = self.outgoing()
            self.go(sent)
            return sent[0]
        return self.now[0]


def local(
    hidden,
    lengths,
    prenorm,
    gating,
    values,
    states,
    stepper,
    offsets,
    decays,
    filters,
    shifts,
    kernels,
    biases,
    direct,
    postnorm,
    output,
    cotangent,
):
    micro, length, model = hidden.shape
    inner = gating.shape[1]
    heads = direct.shape[0]
    both = 2 * heads
    head_size = inner // heads
    state = states.shape[2]
    reach_cells = (filters.shape[0] - 1) // 2
    count = 2 * reach_cells + 1
    peers = lax.axis_size("seq")
    place = lax.axis_index("seq")
    head_place = lax.axis_index("head")
    inner_all = inner * lax.axis_size("head")
    rows = micro * 2 * state // peers
    tiles = inner // LANES
    dims = (length, inner, heads, state, reach_cells, rows)
    maps_width = 4 * state
    width = inner + maps_width
    long = length + 2 * EDGE
    half_peers = peers // micro
    where = place.reshape(1).astype(jnp.int32)

    up = [(i, i + 1) for i in range(peers - 1)]
    down = [(i + 1, i) for i in range(peers - 1)]
    swap = [(0, 1), (1, 0)]
    before = lax.ppermute(hidden[:, length - EDGE :], "seq", up)
    after = lax.ppermute(hidden[:, :EDGE], "seq", down)
    states_flat = states.reshape(model, maps_width)
    stepper_flat = stepper.reshape(model, both)
    direct_row = jnp.repeat(direct, head_size)[None]
    post_row = postnorm[None]

    def spec(*block):
        return pl.BlockSpec((1,) + block, lambda i: (i,) + (0,) * len(block))

    def fixed(*block):
        return pl.BlockSpec(block, lambda i: (0,) * len(block))

    def shape(*dims):
        return jax.ShapeDtypeStruct(dims, F32)

    smem = pl.BlockSpec(memory_space=pltpu.SMEM)
    vmem = pl.BlockSpec(memory_space=pltpu.VMEM)
    packed = tiles * rows + EDGE
    pay_spec = pl.BlockSpec((half_peers, packed, LANES), lambda i: (i, 0, 0))
    plain_spec = pl.BlockSpec((half_peers, tiles * rows, LANES), lambda i: (i, 0, 0))
    small = spec(length, both)
    wide = spec(length, inner)
    acts = spec(length, width)
    row = fixed(1, inner)
    flat = spec(both, length)

    (
        normed,
        mixed,
        conv,
        act,
        maps_t,
        z,
        run,
        late,
        run_rows,
        late_rows,
        reach,
        tail,
        keep,
        taps,
        pay,
    ) = pl.pallas_call(
        partial(front_kernel, dims),
        grid=(micro,),
        in_specs=[
            smem,
            smem,
            spec(EDGE, model),
            spec(length, model),
            spec(EDGE, model),
            fixed(model),
            fixed(model, inner),
            fixed(model, maps_width),
            fixed(model, both),
            fixed(count, inner),
            fixed(count, 4, state),
            fixed(inner),
            fixed(4, state),
            fixed(2, heads),
            fixed(2, heads),
        ],
        out_specs=[
            spec(long, model),
            spec(long, width),
            acts,
            acts,
            spec(maps_width, length),
            small,
            small,
            small,
            flat,
            flat,
            small,
            small,
            spec(1, both),
            fixed(EDGE, width),
            pay_spec,
        ],
        out_shape=[
            shape(micro, long, model),
            shape(micro, long, width),
            shape(micro, length, width),
            shape(micro, length, width),
            shape(micro, maps_width, length),
            shape(micro, length, both),
            shape(micro, length, both),
            shape(micro, length, both),
            shape(micro, both, length),
            shape(micro, both, length),
            shape(micro, length, both),
            shape(micro, length, both),
            shape(micro, 1, both),
            shape(EDGE, width),
            shape(peers, packed, LANES),
        ],
        scratch_shapes=[
            pltpu.VMEM((long + 2 * EDGE, LANES), jnp.int32),
            pltpu.VMEM((count, length, LANES), F32),
        ],
        compiler_params=PARAMS,
        name="front",
    )(
        where,
        lengths,
        before,
        hidden,
        after,
        prenorm,
        values,
        states_flat,
        stepper_flat,
        filters,
        kernels,
        shifts,
        biases,
        offsets,
        decays,
    )

    direction = lax.rem(place // (peers // (2 * micro)), 2)

    def prefix(terms, keeps, flipped):
        return pl.pallas_call(
            partial(prefix_kernel, tiles, rows),
            grid=(1,),
            in_specs=[smem, fixed(*terms.shape), fixed(*keeps.shape)],
            out_specs=fixed(peers, tiles * rows, LANES),
            out_shape=shape(peers, tiles * rows, LANES),
            compiler_params=PARAMS,
            name="prefix",
        )(flipped.reshape(1).astype(jnp.int32), terms, keeps)

    def swap_all(x):
        return lax.all_to_all(x, "seq", 0, 0, tiled=True)

    terms = swap_all(pay)
    arrived = swap_all(prefix(terms, terms, direction))

    normed_flat = normed.reshape(micro * long, model)
    cotangent_flat = cotangent.reshape(micro * length, model)
    back = dot(cotangent_flat, output, 1, 1).reshape(micro, length, inner)
    inside = pl.pallas_call(
        partial(inside_kernel, dims),
        grid=(micro,),
        in_specs=[smem, smem, acts, small, flat],
        out_specs=wide,
        out_shape=shape(micro, length, inner),
        compiler_params=PARAMS,
        name="inside",
    )(where, lengths, act, run, late_rows)
    gate = dot(normed_flat, gating).reshape(micro, long, inner)

    gates = spec(long, inner)
    sum_spec = spec(length, LANES)
    state_spec = spec(2, state, inner)
    mixed_y, sums, before_states = pl.pallas_call(
        partial(join_kernel, dims),
        grid=(micro,),
        in_specs=[wide, plain_spec, acts, small, gates, wide, row, row],
        out_specs=[wide, sum_spec, state_spec],
        out_shape=[
            shape(micro, length, inner),
            shape(micro, length, LANES),
            shape(micro, 2, state, inner),
        ],
        compiler_params=PARAMS,
        name="join",
    )(inside, arrived, act, reach, gate, back, direct_row, post_row)
    peer_sums = lax.ppermute(sums, "head", swap)

    grad_y, normal, pay_back = pl.pallas_call(
        partial(turn_kernel, dims, inner_all),
        grid=(micro,),
        in_specs=[
            sum_spec,
            sum_spec,
            wide,
            gates,
            wide,
            spec(maps_width, length),
            small,
            row,
        ],
        out_specs=[wide, wide, plain_spec],
        out_shape=[
            shape(micro, length, inner),
            shape(micro, length, inner),
            shape(peers, tiles * rows, LANES),
        ],
        compiler_params=PARAMS,
        name="turn",
    )(sums, peer_sums, mixed_y, gate, back, maps_t, reach, post_row)

    back_terms = swap_all(pay_back)

    normal_flat = normal.reshape(micro * length, inner)
    grad_output = dot(normal_flat, cotangent_flat, 0, 0)

    grad_gate, side_smalls = pl.pallas_call(
        partial(side_kernel, dims, inner_all),
        grid=(micro,),
        in_specs=[sum_spec, sum_spec, wide, gates, wide, acts, wide, row],
        out_specs=[gates, spec(EDGE, inner)],
        out_shape=[shape(micro, long, inner), shape(micro, EDGE, inner)],
        compiler_params=PARAMS,
        name="side",
    )(sums, peer_sums, mixed_y, gate, back, act, grad_y, post_row)
    grad_gate_flat = grad_gate.reshape(micro * long, inner)
    grad_gating = dot(normed_flat, grad_gate_flat, 0, 0)
    early = PairTotal("seq")
    early.now = [grad_output, grad_gating]
    back_terms = early.ahead_of(back_terms)
    prefixed = prefix(back_terms, terms, 1 - direction)
    back_arrived = swap_all(prefixed)
    grad_y = tie(grad_y, prefixed)[0]

    grad_inside, grad_maps, own, column_sums = pl.pallas_call(
        partial(inside_back_kernel, dims),
        grid=(micro,),
        in_specs=[smem, smem, acts, wide, small, flat, small, state_spec, row],
        out_specs=[wide, spec(length, maps_width), small, small],
        out_shape=[
            shape(micro, length, inner),
            shape(micro, length, maps_width),
            shape(micro, length, both),
            shape(micro, length, both),
        ],
        scratch_shapes=[pltpu.VMEM((both, length), F32)],
        compiler_params=PARAMS,
        name="inside_back",
    )(where, lengths, act, grad_y, late, run_rows, reach, before_states, direct_row)

    grad_normed_gate = dot(grad_gate_flat, gating, 1, 1)
    back_arrived = tie(back_arrived, own, grad_normed_gate)[0]

    grad_mixed, grad_mixed_maps, grad_raw, smalls = pl.pallas_call(
        partial(end_kernel, dims),
        grid=(micro,),
        in_specs=[
            smem,
            smem,
            plain_spec,
            acts,
            small,
            small,
            acts,
            state_spec,
            spec(1, both),
            wide,
            spec(length, maps_width),
            small,
            small,
            spec(long, width),
            fixed(EDGE, width),
            fixed(2, heads),
        ],
        out_specs=[gates, spec(long, maps_width), spec(long, both), spec(2 * EDGE, width)],
        out_shape=[
            shape(micro, long, inner),
            shape(micro, long, maps_width),
            shape(micro, long, both),
            shape(micro, 2 * EDGE, width),
        ],
        scratch_shapes=[
            pltpu.VMEM((2, state, inner), F32),
            pltpu.VMEM((length, width), F32),
            pltpu.VMEM((long + 2 * EDGE, LANES), jnp.int32),
            pltpu.VMEM((count, length, LANES), F32),
        ],
        compiler_params=PARAMS,
        name="end",
    )(
        where,
        lengths,
        back_arrived,
        act,
        z,
        tail,
        conv,
        before_states,
        keep,
        grad_inside,
        grad_maps,
        own,
        column_sums,
        mixed,
        taps,
        decays,
    )
    all_maps = grad_mixed_maps.reshape(micro * long, maps_width)
    all_maps = all_maps + lax.ppermute(all_maps, "head", swap)

    early.take(grad_raw)
    grad_mixed = early.ahead_of(grad_mixed)
    grad_mixed = grad_mixed.reshape(micro * long, inner)
    grad_mixed_maps = grad_mixed_maps.reshape(micro * long, maps_width)
    grad_raw = grad_raw.reshape(micro * long, both)
    cut = maps_width // 2
    most = (model + cut + cut) // 2
    assert 3 * (most // 2) == model
    late_total = PairTotal("seq")
    late_total.now = [dot(normed_flat[:, :most], grad_mixed, 0, 0), None]
    grad_normed = (
        dot(grad_mixed, values, 1, 1)
        + dot(grad_mixed_maps, states_flat, 1, 1)
        + grad_normed_gate
        + dot(grad_raw, stepper_flat, 1, 1)
    )
    grad_prenorm = jnp.sum(grad_normed * normed_flat, axis=0, keepdims=True) / prenorm[None]
    early.take(grad_prenorm, late_total.now[0])
    normed_flat = early.ahead_of(normed_flat)
    own_maps = lax.dynamic_slice_in_dim(all_maps, head_place * cut, cut, 1)
    second_late = pl.pallas_call(
        partial(pack_kernel, dims),
        in_specs=[vmem] * 6,
        out_specs=vmem,
        out_shape=shape(most, inner),
        compiler_params=PARAMS,
        name="pack",
    )(
        dot(normed_flat[:, most:], grad_mixed, 0, 0),
        dot(own_maps, normed_flat, 0, 0),
        smalls,
        side_smalls,
        dot(grad_raw, normed_flat, 0, 0),
        grad_prenorm,
    )
    late_total.now[1] = second_late
    grad_normed = late_total.ahead_of(grad_normed)

    grad_normed = grad_normed.reshape(micro, long, model)
    grad_normed = grad_normed + lax.ppermute(grad_normed, "head", swap)
    from_after = lax.ppermute(grad_normed[:, :EDGE], "seq", down)
    from_before = lax.ppermute(grad_normed[:, EDGE + length :], "seq", up)
    grad_here = grad_normed[:, EDGE : EDGE + length] + jnp.concatenate(
        [from_before, jnp.zeros((micro, length - 2 * EDGE, model), F32), from_after], axis=1
    )
    scale = lax.rsqrt(jnp.mean(hidden * hidden, axis=2, keepdims=True) + EPSILON)
    pulled = grad_here * prenorm
    grad_hidden = (
        cotangent
        + scale * pulled
        - hidden * (scale**3 * jnp.sum(pulled * hidden, axis=2, keepdims=True) / model)
    )

    normal_flat = tie(normal_flat, second_late)[0]
    projected = dot(normal_flat, output)
    result = hidden + (projected + lax.ppermute(projected, "head", swap)).reshape(hidden.shape)

    held = second_late
    for mine in "eelelelelllel":
        total = late_total if mine == "l" else early
        held = total.turn(held)
    while late_total.at < len(late_total.steps) - 1:
        held = late_total.turn(held)
        held = early.turn(held)
    while not early.done:
        held = early.turn(held)
    came = tie(*late_total.came, held, grad_hidden, result)[:2]
    _, order = late_total.steps[late_total.at]
    quarter = most // 2
    part = pl.BlockSpec((quarter, WIDE), lambda i: (0, i))
    late_done, last = pl.pallas_call(
        finish_kernel,
        grid=(inner // WIDE,),
        in_specs=[smem] + [part] * 4,
        out_specs=[pl.BlockSpec((3 * quarter, WIDE), lambda i: (0, i)), part],
        out_shape=[shape(3 * quarter, inner), shape(quarter, inner)],
        compiler_params=PARAMS,
        name="finish",
    )(
        jnp.stack([late_total.mine(bit) for bit in order]).astype(jnp.int32),
        late_total.now[0],
        came[0],
        late_total.now[1],
        came[1],
    )
    grad_output, grad_gating = early.now
    peer_last = lax.ppermute(last, "head", swap)
    own_states, other_states = last[:cut], peer_last[:cut]
    grad_states = jnp.where(
        head_place == 0,
        jnp.concatenate([own_states, other_states]),
        jnp.concatenate([other_states, own_states]),
    ).T.reshape(states.shape)
    grad_stepper = last[cut : cut + both].T.reshape(stepper.shape)
    (
        grad_filters,
        grad_shifts,
        grad_kernels,
        grad_biases,
        grad_postnorm,
        grad_direct,
        grad_offsets,
        grad_decays,
        grad_prenorm,
    ) = pl.pallas_call(
        partial(unpack_kernel, dims),
        in_specs=[vmem, vmem],
        out_specs=[vmem] * 9,
        out_shape=[
            shape(count, inner),
            shape(inner),
            shape(*kernels.shape),
            shape(*biases.shape),
            shape(inner),
            shape(heads),
            shape(*offsets.shape),
            shape(*decays.shape),
            shape(model),
        ],
        compiler_params=PARAMS,
        name="unpack",
    )(last, peer_last)
    return (
        result,
        grad_hidden,
        grad_prenorm,
        grad_gating,
        late_done,
        grad_states,
        grad_stepper,
        grad_offsets,
        grad_decays,
        grad_filters,
        grad_shifts,
        grad_kernels,
        grad_biases,
        grad_direct,
        grad_postnorm,
        grad_output,
    )


def solution(mesh):
    in_specs = (
        P(None, "seq", None),
        P(),
        P(),
        P(None, "head"),
        P(None, "head"),
        P(),
        P(None, None, "head"),
        P(None, "head"),
        P(None, "head"),
        P(None, "head"),
        P("head"),
        P(),
        P(),
        P("head"),
        P("head"),
        P("head", None),
        P(None, "seq", None),
    )
    out_specs = (
        P(None, "seq", None),
        P(None, "seq", None),
        P(),
        P(None, "head"),
        P(None, "head"),
        P(),
        P(None, None, "head"),
        P(None, "head"),
        P(None, "head"),
        P(None, "head"),
        P("head"),
        P(),
        P(),
        P("head"),
        P("head"),
        P("head", None),
    )
    return jax.shard_map(local, mesh=mesh, in_specs=in_specs, out_specs=out_specs, check_vma=False)
```

```python
from functools import partial

import jax
import jax.numpy as jnp
from jax import lax
from jax.experimental import pallas as pl
from jax.experimental.pallas import tpu as pltpu
from jax.sharding import PartitionSpec as P

EPSILON = 1e-05
HIGH = lax.Precision.HIGH
F32 = jnp.float32
BF16 = jnp.bfloat16
LANES = 128
WIDE = 256
CHUNK = 128
EDGE = 8
PARAMS = pltpu.CompilerParams(vmem_limit_bytes=53 * 1024 * 1024)


def dot(left, right, over_left=1, over_right=0, precision=HIGH):
    return lax.dot_general(
        left,
        right,
        (((over_left,), (over_right,)), ((), ())),
        precision=precision,
        preferred_element_type=F32,
    )


def split(x):
    top = x.astype(BF16)
    return top, (x - top.astype(F32)).astype(BF16)


def dot_bf16(left, right, over_left=1, over_right=0):
    return lax.dot_general(
        left,
        right,
        (((over_left,), (over_right,)), ((), ())),
        preferred_element_type=F32,
    )


def spread(first, head_size, both):
    rows = lax.broadcasted_iota(jnp.int32, (2 * both, WIDE), 0)
    columns = lax.broadcasted_iota(jnp.int32, (2 * both, WIDE), 1)
    return (lax.rem(rows, both) == first + columns // head_size).astype(BF16)


def gather_heads(first, head_size, both, parts=2):
    rows = lax.broadcasted_iota(jnp.int32, (parts * WIDE, both), 0)
    columns = lax.broadcasted_iota(jnp.int32, (parts * WIDE, both), 1)
    return (columns == first + lax.rem(rows, WIDE) // head_size).astype(BF16)


def split3(x):
    top = x.astype(BF16)
    rest = x - top.astype(F32)
    middle = rest.astype(BF16)
    return top, middle, (rest - middle.astype(F32)).astype(BF16)


def halves(x):
    return jnp.concatenate(split(x), axis=1)


def triangle(size, keep):
    rows = lax.broadcasted_iota(jnp.int32, (size, size), 0)
    columns = lax.broadcasted_iota(jnp.int32, (size, size), 1)
    return keep(rows, columns)


def exact_sum(zero_one, x):
    a, b, c = split3(x)
    return dot_bf16(zero_one, a) + dot_bf16(zero_one, b) + dot_bf16(zero_one, c)


def flip(x):
    size = x.shape[1]
    one = triangle(size, lambda r, c: r == c).astype(BF16)
    a, b, c = split3(x)
    return dot_bf16(one, a, 1, 1) + dot_bf16(one, b, 1, 1) + dot_bf16(one, c, 1, 1)


def sigmoid(x):
    return 1.0 / (1.0 + jnp.exp(-x))


def softplus(x):
    return jnp.maximum(x, 0.0) + jnp.log1p(jnp.exp(-jnp.abs(x)))


def bounds_of(lengths, i):
    ends = []
    total = jnp.int32(0)
    for k in range(lengths.shape[1]):
        total = total + lengths[i, k]
        ends.append(total)
    return ends


def document(places, ends):
    found = sum(jnp.where(places >= end, 1, 0) for end in ends)
    return jnp.where(places < 0, -1, jnp.where(places >= ends[-1], -2, found))


def same_document(first, ends, length):
    rows = document(first + lax.broadcasted_iota(jnp.int32, (length, LANES), 0), ends)
    columns = document(first + lax.broadcasted_iota(jnp.int32, (1, length), 1), ends)
    return jnp.concatenate([rows] * (length // LANES), axis=1) == columns


def fill_masks(masks, documents, first, ends, start, rows, reach_cells):
    total = documents.shape[0]
    documents[...] = document(
        first - 2 * EDGE + lax.broadcasted_iota(jnp.int32, (total, LANES), 0), ends
    )
    center = documents[EDGE + start : EDGE + start + rows]
    for o in range(2 * reach_cells + 1):
        at = EDGE + start + o - reach_cells
        masks[o] = (documents[at : at + rows] == center).astype(F32)


def left3(x):
    top = x.astype(BF16).astype(F32)
    return jnp.concatenate([top, top, x - top], axis=1).astype(BF16)


def right3(x):
    top, low = split(x)
    return jnp.concatenate([top, low, top], axis=0)


def stacked(x):
    return jnp.concatenate(split(x), axis=0)


def front_kernel(
    dims,
    place,
    lengths,
    before,
    hidden,
    after,
    prenorm,
    values,
    states,
    stepper,
    filters,
    kernels,
    shifts,
    biases,
    offsets,
    decays,
    normed,
    mixed,
    conv,
    act,
    maps_t,
    z_out,
    run,
    late,
    run_rows,
    late_rows,
    reach,
    tail,
    keep,
    taps,
    pay,
    documents,
    masks,
):
    length, inner, heads, state, reach_cells, rows = dims
    head_size = inner // heads
    both = 2 * heads
    maps_width = 4 * state
    width = inner + maps_width
    offsets_count = 2 * reach_cells + 1
    i = pl.program_id(0)
    ends = bounds_of(lengths, i)
    first = place[0] * length
    fill_masks(masks, documents, first, ends, EDGE, length, reach_cells)

    gain = prenorm[...][None]

    def norm(x):
        mean = jnp.sum(x * x, axis=1, keepdims=True) / x.shape[1]
        return x * lax.rsqrt(mean + EPSILON) * gain

    normed[0, :EDGE] = norm(before[0])
    for r in range(0, length, 64):
        normed[0, EDGE + r : EDGE + r + 64] = norm(hidden[0, r : r + 64])
    normed[0, EDGE + length :] = norm(after[0])

    whole = normed[0]
    for t in range(inner // WIDE):
        at = slice(t * WIDE, (t + 1) * WIDE)
        mixed[0, :, at] = dot(whole, values[:, at])
    mixed[0, :, inner:] = dot(whole, states[...])
    raw = dot(normed[0, EDGE : EDGE + length], stepper[...])

    taps[:offsets_count, :inner] = filters[...]
    taps[offsets_count:, :inner] = shifts[...][None]
    for k in range(4):
        at = slice(inner + k * state, inner + (k + 1) * state)
        taps[:offsets_count, at] = kernels[:, k, :]
        taps[offsets_count:, at] = biases[k : k + 1, :]

    for t in range(width // WIDE):
        at = slice(t * WIDE, (t + 1) * WIDE)
        for r in range(0, length, CHUNK):
            total = jnp.broadcast_to(taps[offsets_count:, at], (CHUNK, WIDE))
            for o in range(offsets_count):
                begin = EDGE - reach_cells + o + r
                mask = masks[o, r : r + CHUNK]
                total = total + (mixed[0, begin : begin + CHUNK, at] * taps[o : o + 1, at]) * (
                    jnp.concatenate([mask] * (WIDE // LANES), axis=1)
                )
            conv[0, r : r + CHUNK, at] = total
            act[0, r : r + CHUNK, at] = total * sigmoid(total)
    flipped = jnp.transpose(act[0, :, inner:])
    maps_t[0] = flipped

    ahead = lax.broadcasted_iota(jnp.int32, (length, both), 1) < heads
    ahead_row = ahead[:1]
    z = raw + jnp.concatenate([offsets[0:1, :], offsets[1:2, :]], axis=1)
    rates = jnp.exp(jnp.concatenate([decays[0:1, :], decays[1:2, :]], axis=1))
    step = softplus(z)
    decay = -step * rates
    lower = triangle(length, lambda r, c: r >= c).astype(BF16)
    upper = triangle(length, lambda r, c: r <= c).astype(BF16)
    running = jnp.where(ahead, exact_sum(lower, decay), exact_sum(upper, decay))
    edge = jnp.where(ahead_row, running[length - 1 :], running[:1])
    here = document(first + lax.broadcasted_iota(jnp.int32, (length, both), 0), ends)
    seg_before = document(first - 1, ends)
    seg_after = document(first + length, ends)
    seg_first = document(first, ends)
    seg_last = document(first + length - 1, ends)
    enter = (here == jnp.where(ahead, seg_before, seg_after)).astype(F32)
    leave = (here == jnp.where(ahead, seg_last, seg_first)).astype(F32)
    keep_mask = jnp.where(
        ahead_row,
        jnp.where(seg_last == seg_before, 1.0, 0.0),
        jnp.where(seg_first == seg_after, 1.0, 0.0),
    )
    reach_now = enter * jnp.exp(running)
    tail_now = leave * jnp.exp(edge - running) * step
    keep_now = keep_mask * jnp.exp(edge)
    late_now = running - jnp.log(jnp.maximum(step, 1e-37))
    z_out[0] = z
    run[0] = running
    late[0] = late_now
    reach[0] = reach_now
    tail[0] = tail_now
    run_rows[0] = flip(running)
    late_rows[0] = flip(late_now)
    keep[0] = keep_now

    tail_halves = halves(tail_now)
    keep_halves = halves(jnp.broadcast_to(keep_now, (EDGE, both)))
    pieces = state // rows
    per_tile = WIDE // head_size
    for d in range(2):
        maps_now = stacked(flipped[2 * d * state : (2 * d + 1) * state])
        keeps = []
        for t in range(inner // WIDE):
            grow = spread(d * heads + t * per_tile, head_size, both)
            weighted = act[0, :, t * WIDE : (t + 1) * WIDE] * dot_bf16(tail_halves, grow)
            put_states(pay, d, t, product_of_stack(maps_now, weighted, state), pieces, rows)
            keep_wide = dot_bf16(keep_halves, grow)[:1]
            keeps += [keep_wide[:, k * LANES : (k + 1) * LANES] for k in range(WIDE // LANES)]
        tiles = inner // LANES
        keeps.append(jnp.zeros((EDGE - tiles, LANES), F32))
        keep_block = jnp.concatenate(keeps, axis=0)
        for j in range(pieces):
            pay[d * pieces + j, tiles * rows :, :] = keep_block


def product_of_stack(stack, x, size):
    top, low = split(x)
    twice = dot_bf16(stack, top)
    return twice[:size] + twice[size:] + dot_bf16(stack[:size], low)


def put_states(pay, d, t, own, pieces, rows):
    for k in range(WIDE // LANES):
        at = (t * (WIDE // LANES) + k) * rows
        for j in range(pieces):
            pay[d * pieces + j, at : at + rows, :] = own[
                j * rows : (j + 1) * rows, k * LANES : (k + 1) * LANES
            ]


def prefix_kernel(tiles, rows, flipped, terms, keeps, into):
    peers = terms.shape[0]
    back = flipped[0] != 0

    def turn(i, carry):
        at = jnp.where(back, peers - 1 - i, i)
        factor = keeps[at, tiles * rows :, :]
        new = []
        for t in range(tiles):
            into[at, t * rows : (t + 1) * rows, :] = carry[t]
            new.append(
                carry[t] * factor[t : t + 1] + terms[at, t * rows : (t + 1) * rows, :]
            )
        return tuple(new)

    lax.fori_loop(0, peers, turn, tuple(jnp.zeros((rows, LANES), F32) for _ in range(tiles)))


def scores_of(act, ends, first, inner, state, length):
    def part(k):
        return act[0, :, inner + k * state : inner + (k + 1) * state]

    same = same_document(first, ends, length)
    below = triangle(length, lambda r, c: r > c)
    above = triangle(length, lambda r, c: r < c)
    return part, same, below, above


def inside_kernel(dims, place, lengths, act, run, late_rows, inside):
    length, inner, heads, state, _, _ = dims
    head_size = inner // heads
    per_tile = LANES // head_size
    ends = bounds_of(lengths, pl.program_id(0))
    part, same, below, above = scores_of(act, ends, place[0] * length, inner, state, length)
    scores = jnp.where(below & same, dot(part(1), part(0), 1, 1), 0.0) + jnp.where(
        above & same, dot(part(3), part(2), 1, 1), 0.0
    )
    run_at = run[0]
    lane = lax.broadcasted_iota(jnp.int32, (length, LANES), 1) // head_size
    for t in range(inner // LANES):
        top, low = split(act[0, :, t * LANES : (t + 1) * LANES])
        pair = jnp.concatenate([top, low], axis=1)
        total = jnp.zeros((length, LANES), F32)
        for k in range(per_tile):
            h = t * per_tile + k
            weights = jnp.exp(
                jnp.where(
                    below,
                    run_at[:, h : h + 1] - late_rows[0, h : h + 1, :],
                    run_at[:, heads + h : heads + h + 1]
                    - late_rows[0, heads + h : heads + h + 1, :],
                )
            )
            m_top, m_low = split(scores * weights)
            wide = dot_bf16(m_top, pair)
            now = wide[:, :LANES] + wide[:, LANES:] + dot_bf16(m_low, top)
            total = jnp.where(lane == k, now, total)
        inside[0, :, t * LANES : (t + 1) * LANES] = total


def unpack(pay, into, tiles, rows, state):
    pieces = state // rows
    for d in range(2):
        for j in range(pieces):
            for t in range(tiles):
                into[d, j * rows : (j + 1) * rows, t * LANES : (t + 1) * LANES] = pay[
                    d * pieces + j, t * rows : (t + 1) * rows, :
                ]


def join_kernel(
    dims, inside, pay, act, reach, gate, back, direct, postnorm, mixed_y, sums, states
):
    length, inner, heads, state, _, rows = dims
    head_size = inner // heads
    both = 2 * heads
    per_tile = WIDE // head_size
    unpack(pay, states.at[0], inner // LANES, rows, state)
    reach_halves = halves(reach[0])
    readers = [left3(act[0, :, inner + k * state : inner + (k + 1) * state]) for k in (1, 3)]
    squares = jnp.zeros((length, WIDE), F32)
    crossed = jnp.zeros((length, WIDE), F32)
    for t in range(inner // WIDE):
        at = slice(t * WIDE, (t + 1) * WIDE)
        total = inside[0, :, at] + direct[:, at] * act[0, :, at]
        for d in range(2):
            grow = spread(d * heads + t * per_tile, head_size, both)
            total = total + dot_bf16(readers[d], right3(states[0, d, :, at])) * dot_bf16(
                reach_halves, grow
            )
        mixed_y[0, :, at] = total
        gate_now = gate[0, EDGE : EDGE + length, at]
        gated = total * (gate_now * sigmoid(gate_now))
        squares = squares + gated * gated
        crossed = crossed + gated * postnorm[:, at] * back[0, :, at]
    lane = lax.broadcasted_iota(jnp.int32, (length, LANES), 1)
    sums[0] = jnp.where(
        lane == 0,
        jnp.sum(squares, axis=1, keepdims=True),
        jnp.sum(crossed, axis=1, keepdims=True),
    )


def norm_of(sums, peer_sums, inner_all, length):
    both_sums = sums[0] + peer_sums[0]
    q = lax.rsqrt(both_sums[:, 0:1] / inner_all + EPSILON)
    pull = both_sums[:, 1:2] * (q * q * q) / inner_all
    return (
        jnp.broadcast_to(q, (length, LANES)),
        jnp.broadcast_to(pull, (length, LANES)),
    )


def turn_kernel(
    dims,
    inner_all,
    sums,
    peer_sums,
    mixed_y,
    gate,
    back,
    maps_t,
    reach,
    postnorm,
    grad_y,
    normal,
    pay,
):
    length, inner, heads, state, _, rows = dims
    head_size = inner // heads
    both = 2 * heads
    per_tile = WIDE // head_size
    pieces = state // rows
    q, pull = norm_of(sums, peer_sums, inner_all, length)
    reach_halves = halves(reach[0])
    readers = [stacked(maps_t[0, k * state : (k + 1) * state]) for k in (1, 3)]
    for t in range(inner // WIDE):
        upstreams = []
        for k in range(WIDE // LANES):
            at = slice(t * WIDE + k * LANES, t * WIDE + (k + 1) * LANES)
            gate_now = gate[0, EDGE : EDGE + length, at]
            opened = gate_now * sigmoid(gate_now)
            gated = mixed_y[0, :, at] * opened
            post = postnorm[:, at]
            upstream = (q * back[0, :, at] * post - pull * gated) * opened
            grad_y[0, :, at] = upstream
            normal[0, :, at] = gated * post * q
            upstreams.append(upstream)
        upstream = jnp.concatenate(upstreams, axis=1)
        for d in range(2):
            grow = spread(d * heads + t * per_tile, head_size, both)
            seed = product_of_stack(readers[d], upstream * dot_bf16(reach_halves, grow), state)
            put_states(pay, d, t, seed, pieces, rows)


def side_kernel(
    dims,
    inner_all,
    sums,
    peer_sums,
    mixed_y,
    gate,
    back,
    act,
    grad_y,
    postnorm,
    grad_gate,
    smalls,
):
    length, inner, heads, _, _, _ = dims
    q, pull = norm_of(sums, peer_sums, inner_all, length)
    grad_gate[0, :EDGE] = jnp.zeros((EDGE, inner), F32)
    grad_gate[0, EDGE + length :] = jnp.zeros((EDGE, inner), F32)
    smalls[0] = jnp.zeros((EDGE, inner), F32)
    for t in range(inner // LANES):
        at = slice(t * LANES, (t + 1) * LANES)
        y = mixed_y[0, :, at]
        gate_now = gate[0, EDGE : EDGE + length, at]
        chance = sigmoid(gate_now)
        gated = y * (gate_now * chance)
        scaled = q * back[0, :, at]
        grad_gated = scaled * postnorm[:, at] - pull * gated
        grad_gate[0, EDGE : EDGE + length, at] = (
            grad_gated * y * (chance * (1.0 + gate_now * (1.0 - chance)))
        )
        smalls[0, 0:1, at] = jnp.sum(scaled * gated, axis=0, keepdims=True)
        smalls[0, 1:2, at] = jnp.sum(grad_y[0, :, at] * act[0, :, at], axis=0, keepdims=True)


def inside_back_kernel(
    dims,
    place,
    lengths,
    act,
    grad_y,
    late,
    run_rows,
    reach,
    states,
    direct,
    grad_signal,
    grad_maps,
    own,
    column_sums,
    read_parts,
):
    length, inner, heads, state, _, _ = dims
    head_size = inner // heads
    per_tile = LANES // head_size
    both = 2 * heads
    ends = bounds_of(lengths, pl.program_id(0))
    part, same, below, above = scores_of(act, ends, place[0] * length, inner, state, length)
    scores = jnp.where(above & same, dot(part(0), part(1), 1, 1), 0.0) + jnp.where(
        below & same, dot(part(2), part(3), 1, 1), 0.0
    )
    late_at = late[0]
    lane = lax.broadcasted_iota(jnp.int32, (length, LANES), 1)
    write_sums = jnp.zeros((length, LANES), F32)
    grad_scores = jnp.zeros((length, length), F32)
    zero = jnp.zeros((length, LANES), BF16)
    for t in range(inner // LANES):
        at = slice(t * LANES, (t + 1) * LANES)
        s_top, s_low = split(act[0, :, at])
        g_top, g_low = split(grad_y[0, :, at])
        pair = jnp.concatenate([g_top, g_low], axis=1)
        two = jnp.concatenate([g_top, g_top], axis=1)
        total = jnp.zeros((length, LANES), F32)
        for k in range(per_tile):
            h = t * per_tile + k
            weights = jnp.exp(
                jnp.where(
                    above,
                    run_rows[0, h : h + 1, :] - late_at[:, h : h + 1],
                    run_rows[0, heads + h : heads + h + 1, :]
                    - late_at[:, heads + h : heads + h + 1],
                )
            )
            mine = lane // head_size == k
            i_top = jnp.where(mine, s_top, zero)
            i_low = jnp.where(mine, s_low, zero)
            overlap = dot_bf16(jnp.concatenate([i_top, i_low], axis=1), two, 1, 1) + dot_bf16(
                i_top, g_low, 1, 1
            )
            product = weights * overlap
            grad_scores = grad_scores + product
            whole = product * scores
            ahead = jnp.where(above, whole, 0.0)
            ahead_writes = jnp.sum(ahead, axis=1, keepdims=True)
            all_writes = jnp.sum(whole, axis=1, keepdims=True)
            write_sums = jnp.where(lane == h, ahead_writes, write_sums)
            write_sums = jnp.where(lane == heads + h, all_writes - ahead_writes, write_sums)
            ahead_reads = jnp.sum(ahead, axis=0, keepdims=True)
            read_parts[h : h + 1, :] = ahead_reads
            read_parts[heads + h : heads + h + 1, :] = (
                jnp.sum(whole, axis=0, keepdims=True) - ahead_reads
            )
            m_top, m_low = split(scores * weights)
            wide = dot_bf16(m_top, pair)
            now = wide[:, :LANES] + wide[:, LANES:] + dot_bf16(m_low, g_top)
            total = jnp.where(mine, now, total)
        grad_signal[0, :, at] = total + direct[:, at] * grad_y[0, :, at]

    writes = write_sums[:, :both]
    column_sums[0] = writes
    total_own = flip_back(read_parts[...]) - writes
    reach_halves = halves(reach[0])
    per_wide = WIDE // head_size
    for d in range(2):
        side = (above, below)[d]
        grads = jnp.where(side & same, grad_scores, 0.0)
        reader = part(2 * d + 1)
        reader3 = left3(reader)
        grad_reader = dot(grads, part(2 * d), 0, 0)
        for t in range(inner // WIDE):
            at = slice(t * WIDE, (t + 1) * WIDE)
            first = d * heads + t * per_wide
            before = states[0, d, :, at]
            reached = grad_y[0, :, at] * dot_bf16(
                reach_halves, spread(first, head_size, both)
            )
            seen = dot_bf16(reader3, right3(before))
            total_own = total_own + dot_bf16(
                halves(reached * seen), gather_heads(first, head_size, both)
            )
            grad_reader = grad_reader + product_with(reached, stacked(before), state)
        grad_maps[0, :, 2 * d * state : (2 * d + 1) * state] = dot(grads, reader)
        grad_maps[0, :, (2 * d + 1) * state : (2 * d + 2) * state] = grad_reader
    own[0] = total_own


def product_with(x, stack, size):
    top, low = split(x)
    twice = dot_bf16(top, stack, 1, 1)
    return twice[:, :size] + twice[:, size:] + dot_bf16(low, stack[:size], 1, 1)


def flip_back(x):
    size = x.shape[0]
    one = triangle(size, lambda r, c: r == c).astype(BF16)
    a, b, c = split3(x)
    return dot_bf16(a, one, 0, 0) + dot_bf16(b, one, 0, 0) + dot_bf16(c, one, 0, 0)


def fold_rows(x):
    total = x[:EDGE]
    for r in range(EDGE, x.shape[0], EDGE):
        total = total + x[r : r + EDGE]
    return total


def end_kernel(
    dims,
    place,
    lengths,
    pay,
    act,
    z_in,
    tail,
    conv,
    states,
    keep,
    grad_inside,
    grad_maps,
    own,
    column_sums,
    mixed,
    taps,
    decays,
    grad_values,
    grad_states,
    grad_raw,
    smalls,
    later,
    grad_act,
    documents,
    masks,
):
    length, inner, heads, state, reach_cells, rows = dims
    head_size = inner // heads
    both = 2 * heads
    per_tile = WIDE // head_size
    width = inner + 4 * state
    offsets_count = 2 * reach_cells + 1
    long = length + 2 * EDGE
    first_row = EDGE - reach_cells
    unpack(pay, later, inner // LANES, rows, state)
    ends = bounds_of(lengths, pl.program_id(0))
    fill_masks(masks, documents, place[0] * length, ends, EDGE, length, reach_cells)

    tail_halves = halves(tail[0])
    leave = jnp.zeros((length, both), F32)
    through = jnp.zeros((1, both), F32)
    for d in range(2):
        writer3 = left3(act[0, :, inner + 2 * d * state : inner + (2 * d + 1) * state])
        grad_writer = grad_maps[0, :, 2 * d * state : (2 * d + 1) * state]
        for t in range(inner // WIDE):
            at = slice(t * WIDE, (t + 1) * WIDE)
            first = d * heads + t * per_tile
            fold = gather_heads(first, head_size, both)
            after = later[d, :, at]
            tails = dot_bf16(tail_halves, spread(first, head_size, both))
            weighted = act[0, :, at] * tails
            pulled = dot_bf16(writer3, right3(after))
            base = grad_inside[0, :, at] if d == 0 else grad_act[:, at]
            grad_act[:, at] = base + tails * pulled
            leave = leave + dot_bf16(halves(weighted * pulled), fold)
            grad_writer = grad_writer + product_with(weighted, stacked(after), state)
            crossed = jnp.sum(states[0, d, :, at] * after, axis=0, keepdims=True)
            through = (
                through + dot_bf16(halves(jnp.broadcast_to(crossed, (EDGE, WIDE))), fold)[:1]
            )
        at = inner + 2 * d * state
        grad_act[:, at : at + state] = grad_writer
        grad_act[:, at + state : at + 2 * state] = grad_maps[
            0, :, (2 * d + 1) * state : (2 * d + 2) * state
        ]

    grad_values[0] = jnp.zeros((long, inner), F32)
    grad_states[0] = jnp.zeros((long, width - inner), F32)
    def column(t, _, into, shift):
        at = pl.ds(pl.multiple_of(t * WIDE, WIDE), WIDE)
        put = pl.ds(pl.multiple_of((t - shift) * WIDE, WIDE), WIDE)
        bias_sum = jnp.zeros((EDGE, WIDE), F32)
        tap_sums = [jnp.zeros((EDGE, WIDE), F32) for _ in range(offsets_count)]
        for r in range(0, length, CHUNK):
            value = conv[0, r : r + CHUNK, at]
            chance = sigmoid(value)
            grad = grad_act[r : r + CHUNK, at] * (chance * (1.0 + value * (1.0 - chance)))
            bias_sum = bias_sum + fold_rows(grad)
            for o in range(offsets_count):
                begin = first_row + o + r
                mask = masks[o, r : r + CHUNK]
                now = grad * jnp.concatenate([mask] * (WIDE // LANES), axis=1)
                into[0, begin : begin + CHUNK, put] += now * taps[o : o + 1, at]
                tap_sums[o] = tap_sums[o] + fold_rows(now * mixed[0, begin : begin + CHUNK, at])
        smalls[0, offsets_count : offsets_count + 1, at] = jnp.sum(bias_sum, axis=0, keepdims=True)
        for o in range(offsets_count):
            smalls[0, o : o + 1, at] = jnp.sum(tap_sums[o], axis=0, keepdims=True)
        return 0

    split_at = inner // WIDE
    lax.fori_loop(0, split_at, partial(column, into=grad_values, shift=0), 0)
    lax.fori_loop(
        split_at, width // WIDE, partial(column, into=grad_states, shift=split_at), 0
    )

    ahead = lax.broadcasted_iota(jnp.int32, (length, both), 1) < heads
    from_here = triangle(length, lambda r, c: c >= r).astype(BF16)
    to_here = triangle(length, lambda r, c: c <= r).astype(BF16)
    before_here = triangle(length, lambda r, c: c < r).astype(BF16)
    after_here = triangle(length, lambda r, c: c > r).astype(BF16)
    entered = own[0]
    grad_decay = (
        jnp.where(
            ahead,
            exact_sum(from_here, entered) + exact_sum(before_here, leave),
            exact_sum(to_here, entered) + exact_sum(after_here, leave),
        )
        + through * keep[0]
    )
    z = z_in[0]
    step = softplus(z)
    chance = sigmoid(z)
    rates = jnp.exp(jnp.concatenate([decays[0:1, :], decays[1:2, :]], axis=1))
    ratio = jnp.where(step > 1e-30, chance / jnp.maximum(step, 1e-30), 1.0)
    grad_z = (leave + column_sums[0]) * ratio - rates * grad_decay * chance
    grad_raw[0, :EDGE] = jnp.zeros((EDGE, both), F32)
    grad_raw[0, EDGE + length :] = jnp.zeros((EDGE, both), F32)
    grad_raw[0, EDGE : EDGE + length] = grad_z
    smalls[0, EDGE:, :] = jnp.zeros((EDGE, width), F32)
    smalls[0, EDGE : EDGE + 1, :both] = jnp.sum(grad_z, axis=0, keepdims=True)
    smalls[0, EDGE + 1 : EDGE + 2, :both] = -rates * jnp.sum(
        step * grad_decay, axis=0, keepdims=True
    )


def pack_kernel(
    dims, rest, own_states, smalls, side_smalls, grad_stepper, grad_prenorm, packed
):
    _, inner, _, state, reach_cells, _ = dims
    both = grad_stepper.shape[0]
    small = smalls[0]
    side = side_smalls[0]
    for i in range(1, smalls.shape[0]):
        small = small + smalls[i]
        side = side + side_smalls[i]
    at = rest.shape[0]
    packed[:at] = rest[...]
    cut = own_states.shape[0]
    packed[at : at + cut] = own_states[...]
    at += cut
    packed[at:] = jnp.zeros((packed.shape[0] - at, inner), F32)
    packed[at : at + both] = grad_stepper[...]
    at += both
    packed[at : at + EDGE] = small[:EDGE, :inner]
    packed[at + EDGE : at + 2 * EDGE, : 4 * state] = small[:EDGE, inner:]
    packed[at + 2 * EDGE : at + 2 * EDGE + 2, :] = side[:2]
    packed[at + 2 * EDGE + 2 : at + 2 * EDGE + 4, :] = small[EDGE : EDGE + 2, :inner]
    packed[at + 2 * EDGE + 4 : at + 2 * EDGE + 5, :] = grad_prenorm[...]


def unpack_kernel(
    dims,
    mine,
    peer,
    filters,
    shifts,
    kernels,
    biases,
    postnorm,
    direct,
    offsets,
    decays,
    prenorm,
):
    _, inner, heads, state, reach_cells, _ = dims
    head_size = inner // heads
    count = 2 * reach_cells + 1
    at = 2 * state + 2 * heads
    filters[...] = mine[at : at + count]
    shifts[...] = mine[at + count]
    at += EDGE
    shared = mine[at : at + EDGE, : 4 * state] + peer[at : at + EDGE, : 4 * state]
    for k in range(4):
        kernels[:, k, :] = shared[:count, k * state : (k + 1) * state]
        biases[k : k + 1, :] = shared[count:, k * state : (k + 1) * state]
    at += EDGE
    postnorm[...] = mine[at]
    fold = jnp.zeros((EDGE, heads), F32)
    for t in range(inner // WIDE):
        row = jnp.broadcast_to(mine[at + 1 : at + 2, t * WIDE : (t + 1) * WIDE], (EDGE, WIDE))
        fold = fold + dot_bf16(
            jnp.concatenate(split3(row), axis=1),
            gather_heads(t * (WIDE // head_size), head_size, heads, 3),
        )
    direct[...] = fold[0]
    for d in range(2):
        offsets[d : d + 1, :] = mine[at + 2 : at + 3, d * heads : (d + 1) * heads]
        decays[d : d + 1, :] = mine[at + 3 : at + 4, d * heads : (d + 1) * heads]
    prenorm[...] = mine[at + 4] + peer[at + 4]


def finish_kernel(bits, own_first, came_first, own_second, came_second, values, last):
    half = own_first.shape[0]
    low = bits[0] == 0
    values[:half] = jnp.where(low, own_first[...], came_first[...])
    values[half : 2 * half] = jnp.where(low, came_first[...], own_first[...])
    low = bits[1] == 0
    values[2 * half :] = jnp.where(low, own_second[...], came_second[...])
    last[...] = jnp.where(low, came_second[...], own_second[...])


def exchange(x, axis, bit):
    peers = lax.axis_size(axis)
    return lax.ppermute(x, axis, [(i, i ^ (1 << bit)) for i in range(peers)])


def bit_of(place, bit):
    return (place >> bit) & 1


def join_halves(mine, own, other):
    return jnp.where(
        mine == 0, jnp.concatenate([own, other]), jnp.concatenate([other, own])
    )


def tie(*arrays):
    return lax.optimization_barrier(arrays)


class PairTotal:
    def __init__(self, axis):
        self.axis = axis
        self.place = lax.axis_index(axis)
        bits = lax.axis_size(axis).bit_length() - 1
        down = [(0, 1), (1, 0), (2,)] + [(bit,) for bit in range(3, bits)]
        self.steps = [("halve", order) for order in down]
        self.steps += [("join", order) for order in reversed(down)]
        self.at = 0
        self.now = [None, None]
        self.came = [None, None]

    def mine(self, bit):
        return bit_of(self.place, bit)

    def outgoing(self, k=None):
        kind, order = self.steps[self.at]
        which = range(len(order)) if k is None else (k,)
        out = []
        for i in which:
            x, mine = self.now[i], self.mine(order[i])
            if kind == "join":
                out.append(x)
            elif order == (2,):
                out.append(jnp.where(mine == 0, self.now[1], self.now[0]))
            else:
                half = x.shape[0] // 2
                out.append(lax.dynamic_slice_in_dim(x, (1 - mine) * half, half))
        return out

    def go(self, sent, k=None):
        _, order = self.steps[self.at]
        which = range(len(order)) if k is None else (k,)
        for i, x in zip(which, sent):
            self.came[i] = exchange(x, self.axis, order[i])

    def take(self, *others):
        kind, order = self.steps[self.at]
        came = [c for c in self.came[: len(order)]]
        if others:
            came = list(tie(*came, *others)[: len(order)])
        now = []
        for i, bit in enumerate(order):
            x, mine, c = self.now[i], self.mine(bit), came[i]
            if order == (2,):
                if kind == "halve":
                    now = [jnp.where(mine == 0, self.now[0], self.now[1]) + c]
                else:
                    now = [jnp.where(mine == 0, x, c), jnp.where(mine == 0, c, x)]
            elif kind == "halve":
                half = x.shape[0] // 2
                now.append(lax.dynamic_slice_in_dim(x, mine * half, half) + c)
            else:
                now.append(join_halves(mine, x, c))
        self.now = now
        self.at += 1

    def ahead_of(self, array, k=None):
        sent = self.outgoing(k)
        self.go(sent, k)
        return tie(array, *sent)[0]

    @property
    def done(self):
        return self.at == len(self.steps)

    def turn(self, *others):
        if self.done:
            return self.now[0]
        self.take(*others)
        if not self.done:
            sent = self.outgoing()
            self.go(sent)
            return sent[0]
        return self.now[0]


def local(
    hidden,
    lengths,
    prenorm,
    gating,
    values,
    states,
    stepper,
    offsets,
    decays,
    filters,
    shifts,
    kernels,
    biases,
    direct,
    postnorm,
    output,
    cotangent,
):
    micro, length, model = hidden.shape
    inner = gating.shape[1]
    heads = direct.shape[0]
    both = 2 * heads
    head_size = inner // heads
    state = states.shape[2]
    reach_cells = (filters.shape[0] - 1) // 2
    count = 2 * reach_cells + 1
    peers = lax.axis_size("seq")
    place = lax.axis_index("seq")
    head_place = lax.axis_index("head")
    inner_all = inner * lax.axis_size("head")
    rows = micro * 2 * state // peers
    tiles = inner // LANES
    dims = (length, inner, heads, state, reach_cells, rows)
    maps_width = 4 * state
    width = inner + maps_width
    long = length + 2 * EDGE
    half_peers = peers // micro
    where = place.reshape(1).astype(jnp.int32)

    up = [(i, i + 1) for i in range(peers - 1)]
    down = [(i + 1, i) for i in range(peers - 1)]
    swap = [(0, 1), (1, 0)]
    before = lax.ppermute(hidden[:, length - EDGE :], "seq", up)
    after = lax.ppermute(hidden[:, :EDGE], "seq", down)
    states_flat = states.reshape(model, maps_width)
    stepper_flat = stepper.reshape(model, both)
    direct_row = jnp.repeat(direct, head_size)[None]
    post_row = postnorm[None]

    def spec(*block):
        return pl.BlockSpec((1,) + block, lambda i: (i,) + (0,) * len(block))

    def fixed(*block):
        return pl.BlockSpec(block, lambda i: (0,) * len(block))

    def shape(*dims):
        return jax.ShapeDtypeStruct(dims, F32)

    smem = pl.BlockSpec(memory_space=pltpu.SMEM)
    vmem = pl.BlockSpec(memory_space=pltpu.VMEM)
    packed = tiles * rows + EDGE
    pay_spec = pl.BlockSpec((half_peers, packed, LANES), lambda i: (i, 0, 0))
    plain_spec = pl.BlockSpec((half_peers, tiles * rows, LANES), lambda i: (i, 0, 0))
    small = spec(length, both)
    wide = spec(length, inner)
    acts = spec(length, width)
    row = fixed(1, inner)
    flat = spec(both, length)

    (
        normed,
        mixed,
        conv,
        act,
        maps_t,
        z,
        run,
        late,
        run_rows,
        late_rows,
        reach,
        tail,
        keep,
        taps,
        pay,
    ) = pl.pallas_call(
        partial(front_kernel, dims),
        grid=(micro,),
        in_specs=[
            smem,
            smem,
            spec(EDGE, model),
            spec(length, model),
            spec(EDGE, model),
            fixed(model),
            fixed(model, inner),
            fixed(model, maps_width),
            fixed(model, both),
            fixed(count, inner),
            fixed(count, 4, state),
            fixed(inner),
            fixed(4, state),
            fixed(2, heads),
            fixed(2, heads),
        ],
        out_specs=[
            spec(long, model),
            spec(long, width),
            acts,
            acts,
            spec(maps_width, length),
            small,
            small,
            small,
            flat,
            flat,
            small,
            small,
            spec(1, both),
            fixed(EDGE, width),
            pay_spec,
        ],
        out_shape=[
            shape(micro, long, model),
            shape(micro, long, width),
            shape(micro, length, width),
            shape(micro, length, width),
            shape(micro, maps_width, length),
            shape(micro, length, both),
            shape(micro, length, both),
            shape(micro, length, both),
            shape(micro, both, length),
            shape(micro, both, length),
            shape(micro, length, both),
            shape(micro, length, both),
            shape(micro, 1, both),
            shape(EDGE, width),
            shape(peers, packed, LANES),
        ],
        scratch_shapes=[
            pltpu.VMEM((long + 2 * EDGE, LANES), jnp.int32),
            pltpu.VMEM((count, length, LANES), F32),
        ],
        compiler_params=PARAMS,
        name="front",
    )(
        where,
        lengths,
        before,
        hidden,
        after,
        prenorm,
        values,
        states_flat,
        stepper_flat,
        filters,
        kernels,
        shifts,
        biases,
        offsets,
        decays,
    )

    direction = lax.rem(place // (peers // (2 * micro)), 2)

    def prefix(terms, keeps, flipped):
        return pl.pallas_call(
            partial(prefix_kernel, tiles, rows),
            grid=(1,),
            in_specs=[smem, vmem, vmem],
            out_specs=fixed(peers, tiles * rows, LANES),
            out_shape=shape(peers, tiles * rows, LANES),
            compiler_params=PARAMS,
            name="prefix",
        )(flipped.reshape(1).astype(jnp.int32), terms, keeps)

    def swap_all(x):
        return lax.all_to_all(x, "seq", 0, 0, tiled=True)

    terms = swap_all(pay)
    arrived = swap_all(prefix(terms, terms, direction))

    normed_flat = normed.reshape(micro * long, model)
    cotangent_flat = cotangent.reshape(micro * length, model)
    back = dot(cotangent_flat, output, 1, 1).reshape(micro, length, inner)
    inside = pl.pallas_call(
        partial(inside_kernel, dims),
        grid=(micro,),
        in_specs=[smem, smem, acts, small, flat],
        out_specs=wide,
        out_shape=shape(micro, length, inner),
        compiler_params=PARAMS,
        name="inside",
    )(where, lengths, act, run, late_rows)
    gate = dot(normed_flat, gating).reshape(micro, long, inner)

    gates = spec(long, inner)
    sum_spec = spec(length, LANES)
    state_spec = spec(2, state, inner)
    mixed_y, sums, before_states = pl.pallas_call(
        partial(join_kernel, dims),
        grid=(micro,),
        in_specs=[wide, plain_spec, acts, small, gates, wide, row, row],
        out_specs=[wide, sum_spec, state_spec],
        out_shape=[
            shape(micro, length, inner),
            shape(micro, length, LANES),
            shape(micro, 2, state, inner),
        ],
        compiler_params=PARAMS,
        name="join",
    )(inside, arrived, act, reach, gate, back, direct_row, post_row)
    peer_sums = lax.ppermute(sums, "head", swap)

    grad_y, normal, pay_back = pl.pallas_call(
        partial(turn_kernel, dims, inner_all),
        grid=(micro,),
        in_specs=[
            sum_spec,
            sum_spec,
            wide,
            gates,
            wide,
            spec(maps_width, length),
            small,
            row,
        ],
        out_specs=[wide, wide, plain_spec],
        out_shape=[
            shape(micro, length, inner),
            shape(micro, length, inner),
            shape(peers, tiles * rows, LANES),
        ],
        compiler_params=PARAMS,
        name="turn",
    )(sums, peer_sums, mixed_y, gate, back, maps_t, reach, post_row)

    back_terms = swap_all(pay_back)

    normal_flat = normal.reshape(micro * length, inner)
    grad_output = dot(normal_flat, cotangent_flat, 0, 0)

    grad_gate, side_smalls = pl.pallas_call(
        partial(side_kernel, dims, inner_all),
        grid=(micro,),
        in_specs=[sum_spec, sum_spec, wide, gates, wide, acts, wide, row],
        out_specs=[gates, spec(EDGE, inner)],
        out_shape=[shape(micro, long, inner), shape(micro, EDGE, inner)],
        compiler_params=PARAMS,
        name="side",
    )(sums, peer_sums, mixed_y, gate, back, act, grad_y, post_row)
    grad_gate_flat = grad_gate.reshape(micro * long, inner)
    grad_gating = dot(normed_flat, grad_gate_flat, 0, 0)
    early = PairTotal("seq")
    early.now = [grad_output, grad_gating]
    back_terms = early.ahead_of(back_terms)
    prefixed = prefix(back_terms, terms, 1 - direction)
    back_arrived = swap_all(prefixed)
    grad_y = tie(grad_y, prefixed)[0]

    grad_inside, grad_maps, own, column_sums = pl.pallas_call(
        partial(inside_back_kernel, dims),
        grid=(micro,),
        in_specs=[smem, smem, acts, wide, small, flat, small, state_spec, row],
        out_specs=[wide, spec(length, maps_width), small, small],
        out_shape=[
            shape(micro, length, inner),
            shape(micro, length, maps_width),
            shape(micro, length, both),
            shape(micro, length, both),
        ],
        scratch_shapes=[pltpu.VMEM((both, length), F32)],
        compiler_params=PARAMS,
        name="inside_back",
    )(where, lengths, act, grad_y, late, run_rows, reach, before_states, direct_row)

    grad_normed_gate = dot(grad_gate_flat, gating, 1, 1)
    back_arrived = tie(back_arrived, own, grad_normed_gate)[0]

    grad_mixed, grad_mixed_maps, grad_raw, smalls = pl.pallas_call(
        partial(end_kernel, dims),
        grid=(micro,),
        in_specs=[
            smem,
            smem,
            plain_spec,
            acts,
            small,
            small,
            acts,
            state_spec,
            spec(1, both),
            wide,
            spec(length, maps_width),
            small,
            small,
            spec(long, width),
            fixed(EDGE, width),
            fixed(2, heads),
        ],
        out_specs=[gates, spec(long, maps_width), spec(long, both), spec(2 * EDGE, width)],
        out_shape=[
            shape(micro, long, inner),
            shape(micro, long, maps_width),
            shape(micro, long, both),
            shape(micro, 2 * EDGE, width),
        ],
        scratch_shapes=[
            pltpu.VMEM((2, state, inner), F32),
            pltpu.VMEM((length, width), F32),
            pltpu.VMEM((long + 2 * EDGE, LANES), jnp.int32),
            pltpu.VMEM((count, length, LANES), F32),
        ],
        compiler_params=PARAMS,
        name="end",
    )(
        where,
        lengths,
        back_arrived,
        act,
        z,
        tail,
        conv,
        before_states,
        keep,
        grad_inside,
        grad_maps,
        own,
        column_sums,
        mixed,
        taps,
        decays,
    )
    all_maps = grad_mixed_maps.reshape(micro * long, maps_width)
    all_maps = all_maps + lax.ppermute(all_maps, "head", swap)

    early.take(grad_raw)
    grad_mixed = early.ahead_of(grad_mixed)
    grad_mixed = grad_mixed.reshape(micro * long, inner)
    grad_mixed_maps = grad_mixed_maps.reshape(micro * long, maps_width)
    grad_raw = grad_raw.reshape(micro * long, both)
    cut = maps_width // 2
    most = (model + cut + cut) // 2
    assert 3 * (most // 2) == model
    late_total = PairTotal("seq")
    late_total.now = [dot(normed_flat[:, :most], grad_mixed, 0, 0), None]
    grad_normed = (
        dot(grad_mixed, values, 1, 1)
        + dot(grad_mixed_maps, states_flat, 1, 1)
        + grad_normed_gate
        + dot(grad_raw, stepper_flat, 1, 1)
    )
    grad_prenorm = jnp.sum(grad_normed * normed_flat, axis=0, keepdims=True) / prenorm[None]
    early.take(grad_prenorm, late_total.now[0])
    normed_flat = early.ahead_of(normed_flat)
    own_maps = lax.dynamic_slice_in_dim(all_maps, head_place * cut, cut, 1)
    second_late = pl.pallas_call(
        partial(pack_kernel, dims),
        in_specs=[vmem] * 6,
        out_specs=vmem,
        out_shape=shape(most, inner),
        compiler_params=PARAMS,
        name="pack",
    )(
        dot(normed_flat[:, most:], grad_mixed, 0, 0),
        dot(own_maps, normed_flat, 0, 0),
        smalls,
        side_smalls,
        dot(grad_raw, normed_flat, 0, 0),
        grad_prenorm,
    )
    late_total.now[1] = second_late
    grad_normed = late_total.ahead_of(grad_normed)

    grad_normed = grad_normed.reshape(micro, long, model)
    grad_normed = grad_normed + lax.ppermute(grad_normed, "head", swap)
    from_after = lax.ppermute(grad_normed[:, :EDGE], "seq", down)
    from_before = lax.ppermute(grad_normed[:, EDGE + length :], "seq", up)
    grad_here = grad_normed[:, EDGE : EDGE + length] + jnp.concatenate(
        [from_before, jnp.zeros((micro, length - 2 * EDGE, model), F32), from_after], axis=1
    )
    scale = lax.rsqrt(jnp.mean(hidden * hidden, axis=2, keepdims=True) + EPSILON)
    pulled = grad_here * prenorm
    grad_hidden = (
        cotangent
        + scale * pulled
        - hidden * (scale**3 * jnp.sum(pulled * hidden, axis=2, keepdims=True) / model)
    )

    normal_flat = tie(normal_flat, second_late)[0]
    projected = dot(normal_flat, output)
    result = hidden + (projected + lax.ppermute(projected, "head", swap)).reshape(hidden.shape)

    held = second_late
    for mine in "eelelelelllel":
        total = late_total if mine == "l" else early
        held = total.turn(held)
    while late_total.at < len(late_total.steps) - 1:
        held = late_total.turn(held)
        held = early.turn(held)
    while not early.done:
        held = early.turn(held)
    came = tie(*late_total.came, held, grad_hidden, result)[:2]
    _, order = late_total.steps[late_total.at]
    quarter = most // 2
    part = pl.BlockSpec((quarter, WIDE), lambda i: (0, i))
    late_done, last = pl.pallas_call(
        finish_kernel,
        grid=(inner // WIDE,),
        in_specs=[smem] + [part] * 4,
        out_specs=[pl.BlockSpec((3 * quarter, WIDE), lambda i: (0, i)), part],
        out_shape=[shape(3 * quarter, inner), shape(quarter, inner)],
        compiler_params=PARAMS,
        name="finish",
    )(
        jnp.stack([late_total.mine(bit) for bit in order]).astype(jnp.int32),
        late_total.now[0],
        came[0],
        late_total.now[1],
        came[1],
    )
    grad_output, grad_gating = early.now
    peer_last = lax.ppermute(last, "head", swap)
    own_states, other_states = last[:cut], peer_last[:cut]
    grad_states = jnp.where(
        head_place == 0,
        jnp.concatenate([own_states, other_states]),
        jnp.concatenate([other_states, own_states]),
    ).T.reshape(states.shape)
    grad_stepper = last[cut : cut + both].T.reshape(stepper.shape)
    (
        grad_filters,
        grad_shifts,
        grad_kernels,
        grad_biases,
        grad_postnorm,
        grad_direct,
        grad_offsets,
        grad_decays,
        grad_prenorm,
    ) = pl.pallas_call(
        partial(unpack_kernel, dims),
        in_specs=[vmem, vmem],
        out_specs=[vmem] * 9,
        out_shape=[
            shape(count, inner),
            shape(inner),
            shape(*kernels.shape),
            shape(*biases.shape),
            shape(inner),
            shape(heads),
            shape(*offsets.shape),
            shape(*decays.shape),
            shape(model),
        ],
        compiler_params=PARAMS,
        name="unpack",
    )(last, peer_last)
    return (
        result,
        grad_hidden,
        grad_prenorm,
        grad_gating,
        late_done,
        grad_states,
        grad_stepper,
        grad_offsets,
        grad_decays,
        grad_filters,
        grad_shifts,
        grad_kernels,
        grad_biases,
        grad_direct,
        grad_postnorm,
        grad_output,
    )


def solution(mesh):
    in_specs = (
        P(None, "seq", None),
        P(),
        P(),
        P(None, "head"),
        P(None, "head"),
        P(),
        P(None, None, "head"),
        P(None, "head"),
        P(None, "head"),
        P(None, "head"),
        P("head"),
        P(),
        P(),
        P("head"),
        P("head"),
        P("head", None),
        P(None, "seq", None),
    )
    out_specs = (
        P(None, "seq", None),
        P(None, "seq", None),
        P(),
        P(None, "head"),
        P(None, "head"),
        P(),
        P(None, None, "head"),
        P(None, "head"),
        P(None, "head"),
        P(None, "head"),
        P("head"),
        P(),
        P(),
        P("head"),
        P("head"),
        P("head", None),
    )
    return jax.shard_map(local, mesh=mesh, in_specs=in_specs, out_specs=out_specs, check_vma=False)
```
